32 devices in a mesh: dp: 16 (over z, y, core), mp: 2 (over x).
Axes of the slice: x: 2, y: 2, z: 4, core: 2. Of those that a mesh axis runs over, the one named last changes fastest.
Arguments:
- tokens: bfloat16 [35840, 1024], P(('dp', 'mp')), may hold values from -6 to 6
- cond_flags: int32 [32, 3], P('dp'), may hold values 0 or 1
- seg_lengths: int32 [32, 3], P('dp'), may hold values from 1 to 560, 1120 in all within a row
- norm_gains: float32 [4, 1024], replicated, may hold values from 0.5 to 1.5
- norm_biases: float32 [4, 1024], replicated, may hold values from -3 to 3
- w_qkv: bfloat16 [3, 1024, 1024], P(None, None, 'mp'), may hold values from -0.25 to 0.25
- qv_bias: float32 [2, 1024], P(None, 'mp'), may hold values from -3 to 3
- w_out: bfloat16 [1024, 1024], P('mp'), may hold values from -0.1875 to 0.1875
- out_biases: float32 [2, 1024], replicated, may hold values from -3 to 3
- w_up: bfloat16 [1024, 4096], P(None, 'mp'), may hold values from -0.1875 to 0.1875
- up_bias: float32 [4096], P('mp'), may hold values from -3 to 3
- w_down: bfloat16 [4096, 1024], P('mp'), may hold values from -0.09375 to 0.09375
- cotangent: bfloat16 [35840, 1024], P(('dp', 'mp')), may hold values from -6 to 6
Outputs:
- output: bfloat16 [35840, 1024], P(('dp', 'mp'))
- grad_input: float32 [35840, 1024], P(('dp', 'mp'))
- grad_norm_gains: float32 [4, 1024], replicated
- grad_norm_biases: float32 [4, 1024], replicated
- grad_w_qkv: float32 [3, 1024, 1024], P(None, None, 'mp')
- grad_qv_bias: float32 [2, 1024], P(None, 'mp')
- grad_w_out: float32 [1024, 1024], P('mp')
- grad_out_biases: float32 [2, 1024], replicated
- grad_w_up: float32 [1024, 4096], P(None, 'mp')
- grad_up_bias: float32 [4096], P('mp')
- grad_w_down: float32 [4096, 1024], P('mp')
The draws below stay inside these ranges and needn't reach their ends.
Inputs may be any that keep to these rules, and one draw needn't show every extreme that they name: `cond_flags`: 1 marks a segment whose tokens are conditioning. `seg_lengths`: a sequence's segment lengths in order (text, low-resolution codes, high-resolution patch codes); they sum to 1120, and the longest is exactly half of 1120.
All inputs are finite; a program needn't handle non-finite values. No bound on the sum of `cond_flags` on one device may be relied on, other than what follows from the above.
Results may differ from the reference program's by a relative error of at most 0.02.
Values may be sent and summed in bfloat16 or wider, within the bound.
A program may use at most 320 MiB of HBM per device.

```python
import math
from functools import partial
import jax
import jax.numpy as jnp
import numpy as np
from jax import lax

D = 1024
HEADS = 16
HD = 64
FF = 4096
SEQ_LEN = 1120
SEQS = 32
TOKENS = 35840


def place_ends(values, rng, smallest, largest):
    shape = values.shape
    place = [jax.random.randint(jax.random.fold_in(rng, axis), (), 0, shape[axis]) for axis in range(len(shape))]
    values = values.at[tuple(place)].set(smallest)
    longest = shape.index(max(shape))
    place[longest] = (place[longest] + 1) % shape[longest]
    return values.at[tuple(place)].set(largest)


def block_levels(own_key, dims, cuts, smallest, top_value):
    factor_of, own = 1.0, jax.random.fold_in(own_key, 6)
    for dim, shards_of in cuts:
        steps = jnp.exp(jax.random.uniform(jax.random.fold_in(own, dim), (shards_of,), jnp.float32, smallest / len(cuts), top_value / len(cuts)))
        factor_of = factor_of * jnp.repeat(steps, dims[dim] // shards_of).reshape([-1 if axis == dim else 1 for axis in range(len(dims))])
    return factor_of


def length_profile(count, total, reach, slope):
    loads = [(1 << 20) // math.isqrt(standing ** slope) + 1 for standing in range(2, count + 1)]
    rest, holding = total - reach - (count - 1), [1] * (count - 1)
    while rest > 0:
        free = [i for i in range(count - 1) if holding[i] < reach]
        mass, left = sum([loads[i] for i in free]), rest
        for i in free:
            addition = min(reach - holding[i], max(1, left * loads[i] // mass), rest)
            holding[i] = holding[i] + addition
            rest = rest - addition
    return np.array([reach] + holding)


def ragged(own_key, count, total, bound, skew):
    if count == 2:
        one = jax.random.randint(own_key, (), max(1, total - bound), min(bound, total - 1) + 1)
        return jnp.stack([one, total - one])
    sizes = jnp.asarray(length_profile(count, total, bound, skew), jnp.int32)
    twos = (count - 1) // 2
    source_of, taker = sizes[1:1 + 2 * twos:2], sizes[2:2 + 2 * twos:2]
    margin = jnp.minimum(source_of - 1, bound - taker)
    shifted = jax.random.randint(jax.random.fold_in(own_key, 1), (twos,), 0, 1 << 20) % (margin + 1)
    sizes = sizes.at[1:1 + 2 * twos:2].set(source_of - shifted).at[2:2 + 2 * twos:2].set(taker + shifted)
    return sizes[jax.random.permutation(jax.random.fold_in(own_key, 2), count)]


def gaussian(key, shape, scale, bound, split=(), held_as=jnp.bfloat16):
    drawn = jax.random.normal(key, shape, jnp.float32) * scale
    if len(split) > 0:
        drawn = block_levels(key, shape, split, -0.22, 0.18) * drawn
    return jnp.clip(drawn, min=-bound, max=bound).astype(held_as)


def setup_inputs(seed: int = 0) -> dict:
    key_list = jax.random.split(jax.random.key(seed), 14)
    tokens = gaussian(key_list[0], (TOKENS, D), 1.0, 6.0, ((0, 32),))
    cond_flags = place_ends((jax.random.randint(key_list[1], (SEQS, 3), 0, 2) < 1).astype(jnp.int32), jax.random.fold_in(key_list[1], 1), 0, 1)
    seg_lengths = jax.vmap(lambda own: ragged(own, 3, SEQ_LEN, SEQ_LEN // 2, 1))(jax.random.split(key_list[2], SEQS)).reshape((SEQS, 3)).astype(jnp.int32)
    norm_gains = jnp.clip(1.0 + 0.1 * jax.random.normal(key_list[3], (4, D), jnp.float32), 0.5, 1.5)
    norm_biases = gaussian(key_list[4], (4, D), 0.3, 3.0, (), jnp.float32)
    w_qkv = gaussian(key_list[5], (3, D, D), (D // 2) ** -0.5, 0.25, ((2, 2),))
    qv_bias = gaussian(key_list[6], (2, D), 0.3, 3.0, ((1, 2),), jnp.float32)
    w_out = gaussian(key_list[7], (D, D), D ** -0.5, 0.1875, ((0, 2),))
    out_biases = gaussian(key_list[8], (2, D), 0.3, 3.0, (), jnp.float32)
    w_up = gaussian(key_list[9], (D, FF), D ** -0.5, 0.1875, ((1, 2),))
    up_bias = gaussian(key_list[10], (FF,), 0.5, 3.0, ((0, 2),), jnp.float32)
    w_down = gaussian(key_list[11], (FF, D), FF ** -0.5, 0.09375, ((0, 2),))
    cotangent = gaussian(key_list[12], (TOKENS, D), 1.0, 6.0, ((0, 32),))
    return dict(tokens=tokens, cond_flags=cond_flags, seg_lengths=seg_lengths, norm_gains=norm_gains, norm_biases=norm_biases, w_qkv=w_qkv, qv_bias=qv_bias, w_out=w_out, out_biases=out_biases, w_up=w_up, up_bias=up_bias, w_down=w_down, cotangent=cotangent)


@jax.custom_vjp
def low(v):
    return lax.optimization_barrier(v.astype(jnp.bfloat16)).astype(jnp.float32)

@jax.custom_vjp
def low_back(v):
    return v

def low_keep(v):
    return (low(v), None)

def low_pass(kept, grad):
    return (grad,)

def back_keep(v):
    return (v, None)

def back_low(kept, grad):
    return (low(grad),)
low.defvjp(low_keep, low_pass)
low_back.defvjp(back_keep, back_low)
epsilon = 1e-05
relax_factor = 32.0
highest = lax.Precision.HIGHEST

def standardize(entries, gain_row, shift_row):
    average = lax.optimization_barrier(jnp.mean(entries, axis=-1, keepdims=True))
    centred = entries - average
    spread = lax.optimization_barrier(jnp.mean(centred * centred, axis=-1, keepdims=True))
    return centred * lax.rsqrt(spread + epsilon) * gain_row + shift_row

def token_marks(seg_flags, lengths):
    position = jnp.arange(SEQ_LEN, dtype=jnp.int32)
    segment = (position >= lengths[0]).astype(jnp.int32) + (position >= lengths[0] + lengths[1]).astype(jnp.int32)
    segment_hits = (segment[:, None] == jnp.arange(3, dtype=jnp.int32)[None, :]).astype(jnp.int32)
    return lax.optimization_barrier(jnp.sum(segment_hits * seg_flags[None, :], axis=1))

def attend_block(key_all, value_all, marks_seq, block_item):
    queries, first_row = block_item
    query_places = first_row + jnp.arange(queries.shape[1], dtype=jnp.int32)
    key_places = jnp.arange(SEQ_LEN, dtype=jnp.int32)
    allowed = (key_places[None, :] <= query_places[:, None]) | (marks_seq[None, :] == 1)
    scores = low_back(jnp.einsum('hqd,hkd->hqk', queries, key_all, precision=highest))
    row_top = lax.optimization_barrier(jnp.max(jnp.where(allowed[None], scores, -1e+30), axis=-1, keepdims=True))
    logits = jnp.where(allowed[None], (scores - row_top) * relax_factor, -30000.0)
    weights = jnp.exp(logits)
    probs = weights / lax.optimization_barrier(jnp.sum(weights, axis=-1, keepdims=True))
    return jnp.einsum('hqk,hkd->hqd', low(probs), value_all, precision=highest)

def split_heads(matrix):
    return matrix.reshape(SEQ_LEN, HEADS, HD).transpose(1, 0, 2)

def forward(seq_x, marks_seq, norm_gains, norm_biases, w_qkv, qv_bias, w_out, out_biases, w_up, up_bias, w_down):
    first_in = low(standardize(seq_x, norm_gains[0], norm_biases[0]))
    bias_rows = jnp.stack([qv_bias[0], jnp.zeros_like(qv_bias[0]), qv_bias[1]])
    projected = low_back(jnp.einsum('td,cde->cte', first_in, w_qkv, precision=highest) + bias_rows[:, None, :])
    queries = low(projected[0] * (1.0 / (relax_factor * math.sqrt(HD))))
    key_all = split_heads(low(projected[1]))
    value_all = split_heads(low(projected[2]))
    half_len = SEQ_LEN // 2
    query_blocks = split_heads(queries).reshape(HEADS, 2, half_len, HD).transpose(1, 0, 2, 3)
    starts = jnp.arange(2, dtype=jnp.int32) * half_len
    blocks_out = lax.map(jax.checkpoint(partial(attend_block, key_all, value_all, marks_seq)), (query_blocks, starts))
    mixed_heads = blocks_out.transpose(0, 2, 1, 3).reshape(SEQ_LEN, D)
    mixed_heads = low(low_back(mixed_heads))
    attended = low_back(jnp.dot(mixed_heads, w_out, precision=highest)) + out_biases[0]
    residual = seq_x + standardize(attended, norm_gains[1], norm_biases[1])
    third_in = low(standardize(residual, norm_gains[2], norm_biases[2]))
    up_value = low_back(jnp.dot(third_in, w_up, precision=highest) + up_bias)
    activated = low(jax.nn.gelu(up_value, approximate=True))
    down = low_back(jnp.dot(activated, w_down, precision=highest)) + out_biases[1]
    return residual + standardize(down, norm_gains[3], norm_biases[3])

def reference(tokens, cond_flags, seg_lengths, norm_gains, norm_biases, w_qkv, qv_bias, w_out, out_biases, w_up, up_bias, w_down, cotangent):
    params = (norm_gains, norm_biases, w_qkv.astype(jnp.float32), qv_bias, w_out.astype(jnp.float32), out_biases, w_up.astype(jnp.float32), up_bias, w_down.astype(jnp.float32))
    seq_count = cond_flags.shape[0]
    seq_tokens = tokens.astype(jnp.float32).reshape(seq_count, SEQ_LEN, D)
    seq_cot = cotangent.astype(jnp.float32).reshape(seq_count, SEQ_LEN, D)
    all_marks = jax.vmap(token_marks)(cond_flags, seg_lengths)

    def step(totals, item):
        seq_x, seq_grad, marks_seq = item
        result, pull = jax.vjp(lambda entries, *weights: forward(entries, marks_seq, *weights), seq_x, *params)
        grads = pull(seq_grad)
        return (tuple((running + update for running, update in zip(totals, grads[1:]))), (result, grads[0]))
    zeros = tuple((jnp.zeros_like(param) for param in params))
    totals, (results, grad_in) = lax.scan(step, zeros, (seq_tokens, seq_cot, all_marks))
    return (results.reshape(seq_count * SEQ_LEN, D).astype(jnp.bfloat16), grad_in.reshape(seq_count * SEQ_LEN, D), totals[0], totals[1], totals[2], totals[3], totals[4], totals[5], totals[6], totals[7], totals[8])
```

```python
from functools import partial
import math

import jax
import jax.numpy as jnp
from jax import lax
from jax.experimental import pallas as pl
from jax.experimental.pallas import tpu as pltpu
from jax.sharding import PartitionSpec as P

HD = 64


epsilon = 1e-05
relax_factor = 32.0


def standardize(entries):
    average = jnp.mean(entries, axis=-1, keepdims=True)
    centred = entries - average
    spread = jnp.mean(centred * centred, axis=-1, keepdims=True)
    inv_std = lax.rsqrt(spread + epsilon)
    return (centred * inv_std, inv_std)


def norm_back(grad_in, normed, inv_std, gain_row):
    weighted = grad_in * gain_row
    return inv_std * (
        weighted
        - jnp.mean(weighted, axis=-1, keepdims=True)
        - normed * jnp.mean(weighted * normed, axis=-1, keepdims=True)
    )


def token_marks(seg_flags, lengths, length):
    position = jnp.arange(length, dtype=jnp.int32)
    segment = (position >= lengths[0]).astype(jnp.int32) + (
        position >= lengths[0] + lengths[1]
    ).astype(jnp.int32)
    segment_hits = (segment[:, None] == jnp.arange(3, dtype=jnp.int32)[None, :]).astype(jnp.int32)
    return jnp.sum(segment_hits * seg_flags[None, :], axis=1)


def block_mask(marks_seq, first_row, block_rows, length):
    query_places = first_row + jnp.arange(block_rows, dtype=jnp.int32)
    key_places = jnp.arange(length, dtype=jnp.int32)
    return (key_places[None, :] <= query_places[:, None]) | (marks_seq[None, :] == 1)


def shards(
    tokens,
    cond_flags,
    seg_lengths,
    norm_gains,
    norm_biases,
    w_qkv,
    qv_bias,
    w_out,
    out_biases,
    w_up,
    up_bias,
    w_down,
    cotangent,
):
    shard_rows = tokens.shape[0]
    group_rows = shard_rows * lax.axis_size("mp")
    seq_count = cond_flags.shape[0]
    length = group_rows // seq_count
    block_rows = length // 2
    head_count = w_qkv.shape[2] // HD
    local_width = head_count * HD
    query_scale = 1.0 / (relax_factor * math.sqrt(HD))
    all_marks = jax.vmap(lambda seg_flags, lengths: token_marks(seg_flags, lengths, length))(
        cond_flags, seg_lengths
    )
    numbers = jnp.arange(seq_count * 2, dtype=jnp.int32)
    source = tokens.astype(jnp.float32)
    normed_one, scale_one = standardize(source)
    first_in = (normed_one * norm_gains[0] + norm_biases[0]).astype(jnp.bfloat16)
    first_all = lax.all_gather(first_in, "mp", axis=0, tiled=True)
    bias_rows = jnp.stack([qv_bias[0], jnp.zeros_like(qv_bias[0]), qv_bias[1]])
    projected = (
        jnp.einsum("td,cde->cte", first_all, w_qkv, preferred_element_type=jnp.float32)
        + bias_rows[:, None, :]
    )
    queries = (
        (projected[0] * query_scale)
        .astype(jnp.bfloat16)
        .reshape(seq_count * 2, block_rows, head_count, HD)
    )
    key_all = projected[1].astype(jnp.bfloat16).reshape(seq_count, length, head_count, HD)
    value_all = projected[2].astype(jnp.bfloat16).reshape(seq_count, length, head_count, HD)

    def block_probs(query_block, number, row_top, row_total):
        sequence = number // 2
        first_row = number % 2 * block_rows
        key_seq = lax.dynamic_index_in_dim(key_all, sequence, 0, keepdims=False)
        allowed = block_mask(
            lax.dynamic_index_in_dim(all_marks, sequence, 0, keepdims=False),
            first_row,
            block_rows,
            length,
        )
        scores = jnp.einsum(
            "qhd,khd->hqk", query_block, key_seq, preferred_element_type=jnp.float32
        )
        if row_top is None:
            row_top = jnp.max(jnp.where(allowed[None], scores, -1e30), axis=-1, keepdims=True)
        weights = jnp.exp(jnp.where(allowed[None], (scores - row_top) * relax_factor, -30000.0))
        if row_total is None:
            row_total = jnp.sum(weights, axis=-1, keepdims=True)
        return (weights / row_total, row_top, row_total, key_seq)

    def forward_block(block_item):
        query_block, number = block_item
        probs, row_top, row_total, key_seq = block_probs(query_block, number, None, None)
        value_seq = lax.dynamic_index_in_dim(value_all, number // 2, 0, keepdims=False)
        mixed_block = jnp.einsum(
            "hqk,khd->qhd",
            probs.astype(jnp.bfloat16),
            value_seq,
            preferred_element_type=jnp.float32,
        )
        return (mixed_block.astype(jnp.bfloat16), row_top, row_total)

    mixed_heads, row_tops, row_totals = lax.map(forward_block, (queries, numbers))
    mixed_heads = mixed_heads.reshape(group_rows, local_width)
    attended = (
        lax.psum_scatter(
            jnp.dot(mixed_heads, w_out, preferred_element_type=jnp.float32),
            "mp",
            scatter_dimension=0,
            tiled=True,
        )
        + out_biases[0]
    )
    normed_two, scale_two = standardize(attended)
    residual = source + normed_two * norm_gains[1] + norm_biases[1]
    normed_three, scale_three = standardize(residual)
    third_in = (normed_three * norm_gains[2] + norm_biases[2]).astype(jnp.bfloat16)
    third_all = lax.all_gather(third_in, "mp", axis=0, tiled=True)
    up_value = jnp.dot(third_all, w_up, preferred_element_type=jnp.float32) + up_bias
    activated = jax.nn.gelu(up_value, approximate=True).astype(jnp.bfloat16)
    down = (
        lax.psum_scatter(
            jnp.dot(activated, w_down, preferred_element_type=jnp.float32),
            "mp",
            scatter_dimension=0,
            tiled=True,
        )
        + out_biases[1]
    )
    normed_four, scale_four = standardize(down)
    result = (residual + normed_four * norm_gains[3] + norm_biases[3]).astype(jnp.bfloat16)
    grad_out = cotangent.astype(jnp.float32)
    d_down = norm_back(grad_out, normed_four, scale_four, norm_gains[3])
    d_down_low = d_down.astype(jnp.bfloat16)
    d_down_all = lax.all_gather(d_down_low, "mp", axis=0, tiled=True)
    d_act = jnp.einsum("td,fd->tf", d_down_all, w_down, preferred_element_type=jnp.float32)
    grad_w_down = jnp.einsum("tf,td->fd", activated, d_down_all, preferred_element_type=jnp.float32)
    gelu_value, gelu_pull = jax.vjp(partial(jax.nn.gelu, approximate=True), up_value)
    d_up = gelu_pull(d_act)[0].astype(jnp.bfloat16)
    grad_w_up = jnp.einsum("td,tf->df", third_all, d_up, preferred_element_type=jnp.float32)
    grad_up_bias = jnp.sum(d_up, axis=0, dtype=jnp.float32)
    d_third = lax.psum_scatter(
        jnp.einsum("tf,df->td", d_up, w_up, preferred_element_type=jnp.float32),
        "mp",
        scatter_dimension=0,
        tiled=True,
    )
    d_residual = grad_out + norm_back(d_third, normed_three, scale_three, norm_gains[2])
    d_attended = norm_back(d_residual, normed_two, scale_two, norm_gains[1])
    d_att_low = d_attended.astype(jnp.bfloat16)
    d_att_all = lax.all_gather(d_att_low, "mp", axis=0, tiled=True)
    d_mixed = jnp.einsum("td,hd->th", d_att_all, w_out, preferred_element_type=jnp.float32).astype(
        jnp.bfloat16
    )
    grad_w_out = jnp.einsum("th,td->hd", mixed_heads, d_att_all, preferred_element_type=jnp.float32)
    d_mixed_blocks = d_mixed.reshape(seq_count * 2, block_rows, head_count, HD)

    def backward_block(block_item):
        query_block, d_block, row_top, row_total, number = block_item
        probs, kept_top, kept_total, key_seq = block_probs(query_block, number, row_top, row_total)
        value_seq = lax.dynamic_index_in_dim(value_all, number // 2, 0, keepdims=False)
        d_probs = jnp.einsum("qhd,khd->hqk", d_block, value_seq, preferred_element_type=jnp.float32)
        inner = jnp.sum(probs * d_probs, axis=-1, keepdims=True)
        d_scores = (relax_factor * probs * (d_probs - inner)).astype(jnp.bfloat16)
        d_query = (
            jnp.einsum("hqk,khd->qhd", d_scores, key_seq, preferred_element_type=jnp.float32)
            * query_scale
        )
        d_key = jnp.einsum(
            "hqk,qhd->khd", d_scores, query_block, preferred_element_type=jnp.float32
        )
        d_value = jnp.einsum(
            "hqk,qhd->khd", probs.astype(jnp.bfloat16), d_block, preferred_element_type=jnp.float32
        )
        return (d_query.astype(jnp.bfloat16), d_key, d_value)

    d_queries, d_keys, d_values = lax.map(
        backward_block, (queries, d_mixed_blocks, row_tops, row_totals, numbers)
    )
    d_keys = jnp.sum(d_keys.reshape(seq_count, 2, length, local_width), axis=1).reshape(
        group_rows, local_width
    )
    d_values = jnp.sum(d_values.reshape(seq_count, 2, length, local_width), axis=1).reshape(
        group_rows, local_width
    )
    d_qkv = jnp.stack(
        [
            d_queries.reshape(group_rows, local_width),
            d_keys.astype(jnp.bfloat16),
            d_values.astype(jnp.bfloat16),
        ]
    )
    grad_w_qkv = jnp.einsum("td,cte->cde", first_all, d_qkv, preferred_element_type=jnp.float32)
    grad_qv_bias = jnp.stack(
        [jnp.sum(d_qkv[0], axis=0, dtype=jnp.float32), jnp.sum(d_qkv[2], axis=0, dtype=jnp.float32)]
    )
    d_first = lax.psum_scatter(
        jnp.einsum("cte,cde->td", d_qkv, w_qkv, preferred_element_type=jnp.float32).astype(
            jnp.bfloat16
        ),
        "mp",
        scatter_dimension=0,
        tiled=True,
    ).astype(jnp.float32)
    grad_input = d_residual + norm_back(d_first, normed_one, scale_one, norm_gains[0])
    error_terms = (d_first, d_residual, d_third, grad_out)
    normed_terms = (normed_one, normed_two, normed_three, normed_four)
    gain_sums = jnp.stack(
        [
            jnp.sum(error_term * normed_term, axis=0)
            for error_term, normed_term in zip(error_terms, normed_terms)
        ]
    )
    bias_sums = jnp.stack([jnp.sum(error_term, axis=0) for error_term in error_terms])
    outer_sums = jnp.stack([jnp.sum(d_attended, axis=0), jnp.sum(d_down, axis=0)])
    gain_sums, bias_sums, outer_sums = lax.psum((gain_sums, bias_sums, outer_sums), ("dp", "mp"))
    grad_w_qkv, grad_qv_bias, grad_w_out, grad_w_up, grad_up_bias, grad_w_down = (
        lax.psum(grad_w_qkv.astype(jnp.bfloat16), "dp").astype(jnp.float32),
        lax.psum(grad_qv_bias.astype(jnp.bfloat16), "dp").astype(jnp.float32),
        lax.psum(grad_w_out.astype(jnp.bfloat16), "dp").astype(jnp.float32),
        lax.psum(grad_w_up.astype(jnp.bfloat16), "dp").astype(jnp.float32),
        lax.psum(grad_up_bias.astype(jnp.bfloat16), "dp").astype(jnp.float32),
        lax.psum(grad_w_down.astype(jnp.bfloat16), "dp").astype(jnp.float32),
    )
    return (
        result,
        grad_input,
        gain_sums,
        bias_sums,
        grad_w_qkv,
        grad_qv_bias,
        grad_w_out,
        outer_sums,
        grad_w_up,
        grad_up_bias,
        grad_w_down,
    )


LOG2E = 1.4426950408889634
HIDDEN = -1e30


def dot_nt(a, b):
    return lax.dot_general(a, b, (((1,), (1,)), ((), ())), preferred_element_type=jnp.float32)


def dot_nn(a, b):
    return lax.dot_general(a, b, (((1,), (0,)), ((), ())), preferred_element_type=jnp.float32)


def dot_tn(a, b):
    return lax.dot_general(a, b, (((0,), (0,)), ((), ())), preferred_element_type=jnp.float32)


def attend_kernel(rows, bias_ref, q_ref, k_ref, v_ref, out_ref, weight_ref, inv_ref):
    length = q_ref.shape[0]
    bias = bias_ref[...]
    lane = lax.broadcasted_iota(jnp.int32, (1, 2 * HD), 1)
    keys = k_ref[...]
    values = v_ref[...]
    for first in range(0, length, rows):
        part = pl.ds(first, rows)
        queries = q_ref[part, :]
        query_places = lax.broadcasted_iota(jnp.int32, (rows, length), 0) + first
        key_places = lax.broadcasted_iota(jnp.int32, (rows, length), 1)
        hide = jnp.where(key_places <= query_places, 0.0, bias)
        outs, invs = [], []
        for head in range(2):
            mine = jnp.where((lane // HD) == head, queries, jnp.zeros_like(queries))
            scores = dot_nt(mine, keys) + hide
            top = jnp.max(scores, axis=1, keepdims=True)
            weights = jnp.exp2((scores - top) * (relax_factor * LOG2E))
            inv = 1.0 / jnp.sum(weights, axis=1, keepdims=True)
            low = weights.astype(jnp.bfloat16)
            weight_ref[head, part, :] = low
            outs.append(dot_nn(low, values) * inv)
            invs.append(inv)
        out_ref[part, :] = jnp.where(lane < HD, outs[0], outs[1]).astype(jnp.bfloat16)
        inv_ref[part, :] = jnp.where(lane < HD, invs[0], invs[1])


def attend(queries, keys, values, bias):
    length, width = queries.shape
    pairs = width // (2 * HD)
    column = pl.BlockSpec((length, 2 * HD), lambda i: (0, i))
    return pl.pallas_call(
        partial(attend_kernel, length // 2),
        grid=(pairs,),
        in_specs=[pl.BlockSpec((1, length), lambda i: (0, 0)), column, column, column],
        out_specs=[column, pl.BlockSpec((2, length, length), lambda i: (i, 0, 0)), column],
        out_shape=[
            jax.ShapeDtypeStruct((length, width), jnp.bfloat16),
            jax.ShapeDtypeStruct((2 * pairs, length, length), jnp.bfloat16),
            jax.ShapeDtypeStruct((length, width), jnp.float32),
        ],
        compiler_params=pltpu.CompilerParams(vmem_limit_bytes=56 * 2**20),
        cost_estimate=pl.CostEstimate(
            flops=pairs * 6 * 10**9, bytes_accessed=pairs * 7 * 10**6, transcendentals=0
        ),
    )(bias, queries, keys, values)


def attend_back_kernel(
    query_scale,
    q_ref,
    k_ref,
    v_ref,
    out_ref,
    grad_ref,
    inv_ref,
    weight_ref,
    dq_ref,
    dk_ref,
    dv_ref,
    ds_ref,
):
    lane = lax.broadcasted_iota(jnp.int32, (1, 2 * HD), 1)
    keys = k_ref[...]
    values = v_ref[...]
    queries = q_ref[...]
    scaled = grad_ref[...].astype(jnp.float32) * inv_ref[...]
    mixed = out_ref[...].astype(jnp.float32)
    low = scaled.astype(jnp.bfloat16)
    dqs, dks, dvs = [], [], []
    for head in range(2):
        mine = (lane // HD) == head
        grad = jnp.where(mine, scaled * relax_factor, 0.0).astype(jnp.bfloat16)
        inner = jnp.sum(grad.astype(jnp.float32) * mixed, axis=1, keepdims=True)
        d_probs = dot_nt(grad, values)
        ds_ref[...] = (
            weight_ref[head].astype(jnp.float32) * (d_probs - inner)
        ).astype(jnp.bfloat16)
        dqs.append((dot_nn(ds_ref[...], keys) * query_scale).astype(jnp.bfloat16))
        dks.append(dot_tn(ds_ref[...], queries).astype(jnp.bfloat16))
        dvs.append(dot_tn(weight_ref[head], low).astype(jnp.bfloat16))
    dq_ref[...] = jnp.where(lane < HD, dqs[0], dqs[1])
    dk_ref[...] = jnp.where(lane < HD, dks[0], dks[1])
    dv_ref[...] = jnp.where(lane < HD, dvs[0], dvs[1])


def attend_back(queries, keys, values, mixed, grad, inv, weights, query_scale):
    length, width = queries.shape
    pairs = width // (2 * HD)
    column = pl.BlockSpec((length, 2 * HD), lambda i: (0, i))
    return pl.pallas_call(
        partial(attend_back_kernel, query_scale),
        grid=(pairs,),
        in_specs=[column] * 6 + [pl.BlockSpec((2, length, length), lambda i: (i, 0, 0))],
        out_specs=[column] * 3,
        out_shape=[jax.ShapeDtypeStruct((length, width), jnp.bfloat16)] * 3,
        scratch_shapes=[pltpu.VMEM((length, length), jnp.bfloat16)],
        compiler_params=pltpu.CompilerParams(vmem_limit_bytes=56 * 2**20),
        cost_estimate=pl.CostEstimate(
            flops=pairs * 7 * 10**9, bytes_accessed=pairs * 7 * 10**6, transcendentals=0
        ),
    )(queries, keys, values, mixed, grad, inv, weights)


def flip(value, bit):
    count = lax.axis_size("dp")
    return lax.ppermute(value, "dp", [(i, i ^ bit) for i in range(count)])


def cross(value):
    return lax.ppermute(value, "mp", [(0, 1), (1, 0)])


def block(value, index, count, axis):
    size = value.shape[axis] // count
    return lax.dynamic_slice_in_dim(value, index * size, size, axis)


def low(value):
    return value.astype(jnp.bfloat16)


MESH = pl.DeviceIdType.MESH
CHUNK = 128


def reduce_kernel(quarters, *refs):
    count = len(quarters)
    owns, others = refs[:count], refs[count : 2 * count]
    (out, mine, core_in, held, x_out, x_in, y_out, y_in, z_out, z_in, last) = refs[2 * count : 2 * count + 11]
    (load_sem, core_sem, x_sem, y_sem, z_sem, zz_sem, yy_sem, cc_sem, keep_sem) = refs[2 * count + 11 :]
    place = lax.axis_index("dp")
    turn = lax.axis_index("mp")
    core, side, level = place % 2, (place // 2) % 2, place // 4
    levels = lax.axis_size("dp") // 4
    sibling = {"dp": place + 1 - 2 * core}
    across = {"mp": 1 - turn}
    beside = {"dp": place + 2 - 4 * side}
    floors = [{"dp": (level + step) % levels * 4 + place % 4} for step in range(1, levels)]
    half, piece = CHUNK // 2, CHUNK // 2 // levels
    chunks = sum(quarters) // CHUNK

    barrier = pltpu.get_barrier_semaphore()
    partners = [sibling, across, beside, *floors]
    for partner in partners:
        pl.semaphore_signal(barrier, inc=1, device_id=partner, device_id_type=MESH)
    pl.semaphore_wait(barrier, len(partners))

    def rows(start, size):
        return pl.ds(pl.multiple_of(start, 16), size)

    def remote(source, target, sems, index, device):
        return pltpu.make_async_remote_copy(
            src_ref=source,
            dst_ref=target,
            send_sem=sems.at[(0, *index)],
            recv_sem=sems.at[(1, *index)],
            device_id=device,
            device_id_type=MESH,
        )

    def loads(weight, offset, slot):
        copies = []
        for index, refs_of in enumerate((others, owns)):
            ref, quarter = refs_of[weight], quarters[weight]
            copies.append(
                pltpu.make_async_copy(
                    ref.at[rows(core * quarter + offset, CHUNK)], mine.at[index], load_sem.at[index]
                )
            )
            copies.append(
                remote(
                    ref.at[rows((1 - core) * quarter + offset, CHUNK)],
                    core_in.at[slot, index],
                    core_sem,
                    (slot, index),
                    sibling,
                )
            )
        return copies

    def x_copy(slot):
        return remote(x_out, x_in.at[slot], x_sem, (slot,), across)

    def y_copy(slot):
        return remote(y_out.at[rows((1 - side) * half, half)], y_in.at[slot], y_sem, (slot,), beside)

    def z_copies(slot):
        return [
            remote(
                z_out.at[rows((level + step) % levels * piece, piece)],
                z_in.at[slot, step - 1],
                z_sem,
                (slot, step - 1),
                floors[step - 1],
            )
            for step in range(1, levels)
        ]

    def keep_copies(chunk, slot):
        target = out.at[core, rows(chunk * CHUNK + side * half + level * piece, piece)]
        copies = [pltpu.make_async_copy(last, target, keep_sem)]
        for step in range(1, levels):
            copies.append(remote(last, target, zz_sem, (slot, step - 1), floors[step - 1]))
        return copies

    def yy_copy(chunk, slot):
        part = out.at[core, rows(chunk * CHUNK + side * half, half)]
        return remote(part, part, yy_sem, (slot,), beside)

    def cc_copy(chunk, slot):
        part = out.at[core, rows(chunk * CHUNK, CHUNK)]
        return remote(part, part, cc_sem, (slot,), sibling)

    def wide(value):
        return value.astype(jnp.float32)

    def at_stage(turn_now, stage, action):
        chunk = turn_now - stage

        @pl.when((chunk >= 0) & (chunk < chunks))
        def _():
            action(chunk, chunk % 2)

    def stage_7(chunk, slot):
        cc_copy(chunk, slot).wait()

    def stage_6(chunk, slot):
        yy_copy(chunk, slot).wait()
        cc_copy(chunk, slot).start()

    def stage_5(chunk, slot):
        for copy in keep_copies(chunk, slot):
            copy.wait()
        yy_copy(chunk, slot).start()

    def stage_4(chunk, slot):
        for copy in z_copies(slot):
            copy.wait()
        total = wide(z_out[rows(level * piece, piece), :])
        for step in range(1, levels):
            total = total + wide(z_in[slot, step - 1])
        last[...] = low(total)
        for copy in keep_copies(chunk, slot):
            copy.start()

    def stage_3(chunk, slot):
        y_copy(slot).wait()
        z_out[...] = low(wide(y_out[rows(side * half, half), :]) + wide(y_in[slot]))
        for copy in z_copies(slot):
            copy.start()

    def stage_2(chunk, slot):
        x_copy(slot).wait()
        y_out[...] = low(held[...] + wide(x_in[slot]))
        y_copy(slot).start()

    def stage_1(chunk, slot):
        for copy in loads(0, 0, slot):
            copy.wait()
        x_out[...] = low(wide(mine[0]) + wide(core_in[slot, 0]))
        x_copy(slot).start()
        held[...] = wide(mine[1]) + wide(core_in[slot, 1])

    def stage_0(chunk, slot):
        first = 0
        for weight, quarter in enumerate(quarters):
            span = quarter // CHUNK

            @pl.when((chunk >= first) & (chunk < first + span))
            def _(weight=weight, first=first):
                for copy in loads(weight, (chunk - first) * CHUNK, slot):
                    copy.start()

            first += span

    stages = [stage_0, stage_1, stage_2, stage_3, stage_4, stage_5, stage_6, stage_7]

    @pl.loop(0, chunks + len(stages) - 1)
    def _(now):
        for stage in reversed(range(len(stages))):
            at_stage(now, stage, stages[stage])


def reduce_all(owns, others):
    width = owns[0].shape[1]
    quarters = tuple(own.shape[0] // 2 for own in owns)
    levels = lax.axis_size("dp") // 4
    half, piece = CHUNK // 2, CHUNK // 2 // levels
    kind = jnp.bfloat16
    sem = pltpu.SemaphoreType.DMA
    return pl.pallas_call(
        partial(reduce_kernel, quarters),
        in_specs=[pl.BlockSpec(memory_space=pl.ANY)] * (2 * len(owns)),
        out_specs=pl.BlockSpec(memory_space=pl.ANY),
        out_shape=jax.ShapeDtypeStruct((2, sum(quarters), width), kind),
        scratch_shapes=[
            pltpu.VMEM((2, CHUNK, width), kind),
            pltpu.VMEM((2, 2, CHUNK, width), kind),
            pltpu.VMEM((CHUNK, width), jnp.float32),
            pltpu.VMEM((CHUNK, width), kind),
            pltpu.VMEM((2, CHUNK, width), kind),
            pltpu.VMEM((CHUNK, width), kind),
            pltpu.VMEM((2, half, width), kind),
            pltpu.VMEM((half, width), kind),
            pltpu.VMEM((2, levels - 1, piece, width), kind),
            pltpu.VMEM((piece, width), kind),
            sem((2,)),
            sem((2, 2, 2)),
            sem((2, 2)),
            sem((2, 2)),
            sem((2, 2, levels - 1)),
            sem((2, 2, levels - 1)),
            sem((2, 2)),
            sem((2, 2)),
            sem,
        ],
        compiler_params=pltpu.CompilerParams(collective_id=0, has_side_effects=True, vmem_limit_bytes=56 * 2**20),
    )(*owns, *others)


def sequence_shards(
    tokens,
    cond_flags,
    seg_lengths,
    norm_gains,
    norm_biases,
    w_qkv,
    qv_bias,
    w_out,
    out_biases,
    w_up,
    up_bias,
    w_down,
    cotangent,
):
    length = tokens.shape[0]
    place = lax.axis_index("dp")
    turn = lax.axis_index("mp")
    core = place % 2
    side = (place // 2) % 2
    query_scale = 1.0 / (relax_factor * math.sqrt(HD))

    def in_order(which, mine, other, axis):
        return jnp.where(
            which == 0,
            jnp.concatenate([mine, other], axis=axis),
            jnp.concatenate([other, mine], axis=axis),
        )

    def fetch(weight, axis):
        first = cross(block(weight, 2 * core + side, 4, axis))
        near = in_order(side, first, flip(first, 2), axis)
        return in_order(core, near, flip(near, 1), axis)

    qkv_sets = (w_qkv, fetch(w_qkv, 2))
    bias_sets = (qv_bias, cross(qv_bias))
    out_sets = (w_out, fetch(w_out, 0))
    up_sets = (w_up, fetch(w_up, 1))
    up_bias_sets = (up_bias, cross(up_bias))
    down_sets = (w_down, fetch(w_down, 0))

    marks = token_marks(
        lax.dynamic_index_in_dim(cond_flags, turn, 0, keepdims=False),
        lax.dynamic_index_in_dim(seg_lengths, turn, 0, keepdims=False),
        length,
    )
    hide = jnp.where(marks[None, :] == 1, 0.0, HIDDEN).astype(jnp.float32)

    source = tokens.astype(jnp.float32)
    normed_one, scale_one = standardize(source)
    first_in = low(normed_one * norm_gains[0] + norm_biases[0])
    heads = []
    attended = out_biases[0]
    for weight, bias, out in zip(qkv_sets, bias_sets, out_sets):
        queries = low((dot_nn(first_in, weight[0]) + bias[0]) * query_scale)
        keys = low(dot_nn(first_in, weight[1]))
        values = low(dot_nn(first_in, weight[2]) + bias[1])
        mixed, kept, inv = attend(queries, keys, values, hide)
        heads.append((queries, keys, values, mixed, kept, inv))
    for (_, _, _, mixed, _, _), out in zip(heads, out_sets):
        attended = attended + dot_nn(mixed, out)
    normed_two, scale_two = standardize(attended)
    residual = source + normed_two * norm_gains[1] + norm_biases[1]
    normed_three, scale_three = standardize(residual)
    third_in = low(normed_three * norm_gains[2] + norm_biases[2])
    ups = [dot_nn(third_in, weight) + bias for weight, bias in zip(up_sets, up_bias_sets)]
    acts = [low(jax.nn.gelu(up, approximate=True)) for up in ups]
    down = out_biases[1]
    for act, weight in zip(acts, down_sets):
        down = down + dot_nn(act, weight)
    normed_four, scale_four = standardize(down)
    result = low(residual + normed_four * norm_gains[3] + norm_biases[3])
    grad_out = cotangent.astype(jnp.float32)
    d_down = norm_back(grad_out, normed_four, scale_four, norm_gains[3])
    d_down_low = low(d_down)

    d_ups = []
    for up, weight in zip(ups, down_sets):
        pull = jax.vjp(partial(jax.nn.gelu, approximate=True), up)[1]
        d_ups.append(low(pull(dot_nt(d_down_low, weight))[0]))

    down_parts = [low(dot_tn(act, d_down_low)) for act in acts]
    up_parts = [low(dot_tn(grad, third_in)) for grad in d_ups]
    d_third = sum(dot_nt(grad, weight) for grad, weight in zip(d_ups, up_sets))
    d_residual = grad_out + norm_back(d_third, normed_three, scale_three, norm_gains[2])
    d_attended = norm_back(d_residual, normed_two, scale_two, norm_gains[1])
    d_att_low = low(d_attended)
    out_parts = [low(dot_tn(item[3], d_att_low)) for item in heads]
    d_qkvs = []
    d_first = 0.0
    for item, weight, out in zip(heads, qkv_sets, out_sets):
        queries, keys, values, mixed, kept, inv = item
        d_mixed = low(dot_nt(d_att_low, out))
        grads = attend_back(queries, keys, values, mixed, d_mixed, inv, kept, query_scale)
        d_qkvs.append(grads)
        for index in range(3):
            d_first = d_first + dot_nt(grads[index], weight[index])

    qkv_parts = [[low(dot_tn(grads[index], first_in)) for grads in d_qkvs] for index in range(3)]
    parts = [down_parts, up_parts, out_parts, *qkv_parts]
    total = reduce_all([part[0] for part in parts], [part[1] for part in parts])
    spans = [0]
    for part in parts:
        spans.append(spans[-1] + part[0].shape[0] // 2)
    wholes = [
        total[:, first:last].reshape(-1, total.shape[2]).astype(jnp.float32)
        for first, last in zip(spans[:-1], spans[1:])
    ]
    grad_w_down, grad_w_up, grad_w_out = wholes[0], wholes[1].T, wholes[2]
    grad_w_qkv = jnp.stack([whole.T for whole in wholes[3:]])
    grad_input = d_residual + norm_back(d_first, normed_one, scale_one, norm_gains[0])

    error_terms = (d_first, d_residual, d_third, grad_out)
    normed_terms = (normed_one, normed_two, normed_three, normed_four)
    sums = jnp.stack(
        [jnp.sum(error * normed, axis=0) for error, normed in zip(error_terms, normed_terms)]
        + [jnp.sum(error, axis=0) for error in error_terms]
        + [jnp.sum(d_attended, axis=0), jnp.sum(d_down, axis=0)]
    )

    def columns(value):
        return jnp.sum(value, axis=0, dtype=jnp.float32)

    qv_sums = [jnp.stack([columns(grads[0]), columns(grads[2])]) for grads in d_qkvs]
    up_sums = [columns(grad) for grad in d_ups]
    own_small = jnp.concatenate([qv_sums[0].reshape(-1), up_sums[0]])
    other_small = jnp.concatenate([qv_sums[1].reshape(-1), up_sums[1]])
    small = jnp.concatenate([sums.reshape(-1), own_small])
    small = small + cross(jnp.concatenate([sums.reshape(-1), other_small]))
    bit = 1
    while bit < lax.axis_size("dp"):
        small = small + flip(small, bit)
        bit *= 2
    sums = small[: sums.size].reshape(sums.shape)
    grad_qv_bias = small[sums.size : sums.size + qv_bias.size].reshape(qv_bias.shape)
    grad_up_bias = small[sums.size + qv_bias.size :]
    return (
        result,
        grad_input,
        sums[:4],
        sums[4:8],
        grad_w_qkv,
        grad_qv_bias,
        grad_w_out,
        sums[8:],
        grad_w_up,
        grad_up_bias,
        grad_w_down,
    )


def solution(mesh):
    in_specs = (
        P(("dp", "mp"), None),
        P("dp", None),
        P("dp", None),
        P(),
        P(),
        P(None, None, "mp"),
        P(None, "mp"),
        P("mp", None),
        P(),
        P(None, "mp"),
        P("mp"),
        P("mp", None),
        P(("dp", "mp"), None),
    )
    out_specs = (
        P(("dp", "mp"), None),
        P(("dp", "mp"), None),
        P(),
        P(),
        P(None, None, "mp"),
        P(None, "mp"),
        P("mp", None),
        P(),
        P(None, "mp"),
        P("mp"),
        P("mp", None),
    )
    per_device = mesh.shape["dp"] * mesh.shape["mp"]

    def step(*args):
        whole_sequences = args[1].shape[0] == per_device
        local = sequence_shards if whole_sequences and mesh.shape["mp"] == 2 and mesh.shape["dp"] == 16 else shards
        return jax.shard_map(
            local, mesh=mesh, in_specs=in_specs, out_specs=out_specs, check_vma=False
        )(*args)

    return step
```

```python
from functools import partial
import math

import jax
import jax.numpy as jnp
from jax import lax
from jax.experimental import pallas as pl
from jax.experimental.pallas import tpu as pltpu
from jax.sharding import PartitionSpec as P

HD = 64


epsilon = 1e-05
relax_factor = 32.0


def standardize(entries):
    average = jnp.mean(entries, axis=-1, keepdims=True)
    centred = entries - average
    spread = jnp.mean(centred * centred, axis=-1, keepdims=True)
    inv_std = lax.rsqrt(spread + epsilon)
    return (centred * inv_std, inv_std)


def norm_back(grad_in, normed, inv_std, gain_row):
    weighted = grad_in * gain_row
    return inv_std * (
        weighted
        - jnp.mean(weighted, axis=-1, keepdims=True)
        - normed * jnp.mean(weighted * normed, axis=-1, keepdims=True)
    )


def token_marks(seg_flags, lengths, length):
    position = jnp.arange(length, dtype=jnp.int32)
    segment = (position >= lengths[0]).astype(jnp.int32) + (
        position >= lengths[0] + lengths[1]
    ).astype(jnp.int32)
    segment_hits = (segment[:, None] == jnp.arange(3, dtype=jnp.int32)[None, :]).astype(jnp.int32)
    return jnp.sum(segment_hits * seg_flags[None, :], axis=1)


def block_mask(marks_seq, first_row, block_rows, length):
    query_places = first_row + jnp.arange(block_rows, dtype=jnp.int32)
    key_places = jnp.arange(length, dtype=jnp.int32)
    return (key_places[None, :] <= query_places[:, None]) | (marks_seq[None, :] == 1)


def shards(
    tokens,
    cond_flags,
    seg_lengths,
    norm_gains,
    norm_biases,
    w_qkv,
    qv_bias,
    w_out,
    out_biases,
    w_up,
    up_bias,
    w_down,
    cotangent,
):
    shard_rows = tokens.shape[0]
    group_rows = shard_rows * lax.axis_size("mp")
    seq_count = cond_flags.shape[0]
    length = group_rows // seq_count
    block_rows = length // 2
    head_count = w_qkv.shape[2] // HD
    local_width = head_count * HD
    query_scale = 1.0 / (relax_factor * math.sqrt(HD))
    all_marks = jax.vmap(lambda seg_flags, lengths: token_marks(seg_flags, lengths, length))(
        cond_flags, seg_lengths
    )
    numbers = jnp.arange(seq_count * 2, dtype=jnp.int32)
    source = tokens.astype(jnp.float32)
    normed_one, scale_one = standardize(source)
    first_in = (normed_one * norm_gains[0] + norm_biases[0]).astype(jnp.bfloat16)
    first_all = lax.all_gather(first_in, "mp", axis=0, tiled=True)
    bias_rows = jnp.stack([qv_bias[0], jnp.zeros_like(qv_bias[0]), qv_bias[1]])
    projected = (
        jnp.einsum("td,cde->cte", first_all, w_qkv, preferred_element_type=jnp.float32)
        + bias_rows[:, None, :]
    )
    queries = (
        (projected[0] * query_scale)
        .astype(jnp.bfloat16)
        .reshape(seq_count * 2, block_rows, head_count, HD)
    )
    key_all = projected[1].astype(jnp.bfloat16).reshape(seq_count, length, head_count, HD)
    value_all = projected[2].astype(jnp.bfloat16).reshape(seq_count, length, head_count, HD)

    def block_probs(query_block, number, row_top, row_total):
        sequence = number // 2
        first_row = number % 2 * block_rows
        key_seq = lax.dynamic_index_in_dim(key_all, sequence, 0, keepdims=False)
        allowed = block_mask(
            lax.dynamic_index_in_dim(all_marks, sequence, 0, keepdims=False),
            first_row,
            block_rows,
            length,
        )
        scores = jnp.einsum(
            "qhd,khd->hqk", query_block, key_seq, preferred_element_type=jnp.float32
        )
        if row_top is None:
            row_top = jnp.max(jnp.where(allowed[None], scores, -1e30), axis=-1, keepdims=True)
        weights = jnp.exp(jnp.where(allowed[None], (scores - row_top) * relax_factor, -30000.0))
        if row_total is None:
            row_total = jnp.sum(weights, axis=-1, keepdims=True)
        return (weights / row_total, row_top, row_total, key_seq)

    def forward_block(block_item):
        query_block, number = block_item
        probs, row_top, row_total, key_seq = block_probs(query_block, number, None, None)
        value_seq = lax.dynamic_index_in_dim(value_all, number // 2, 0, keepdims=False)
        mixed_block = jnp.einsum(
            "hqk,khd->qhd",
            probs.astype(jnp.bfloat16),
            value_seq,
            preferred_element_type=jnp.float32,
        )
        return (mixed_block.astype(jnp.bfloat16), row_top, row_total)

    mixed_heads, row_tops, row_totals = lax.map(forward_block, (queries, numbers))
    mixed_heads = mixed_heads.reshape(group_rows, local_width)
    attended = (
        lax.psum_scatter(
            jnp.dot(mixed_heads, w_out, preferred_element_type=jnp.float32),
            "mp",
            scatter_dimension=0,
            tiled=True,
        )
        + out_biases[0]
    )
    normed_two, scale_two = standardize(attended)
    residual = source + normed_two * norm_gains[1] + norm_biases[1]
    normed_three, scale_three = standardize(residual)
    third_in = (normed_three * norm_gains[2] + norm_biases[2]).astype(jnp.bfloat16)
    third_all = lax.all_gather(third_in, "mp", axis=0, tiled=True)
    up_value = jnp.dot(third_all, w_up, preferred_element_type=jnp.float32) + up_bias
    activated = jax.nn.gelu(up_value, approximate=True).astype(jnp.bfloat16)
    down = (
        lax.psum_scatter(
            jnp.dot(activated, w_down, preferred_element_type=jnp.float32),
            "mp",
            scatter_dimension=0,
            tiled=True,
        )
        + out_biases[1]
    )
    normed_four, scale_four = standardize(down)
    result = (residual + normed_four * norm_gains[3] + norm_biases[3]).astype(jnp.bfloat16)
    grad_out = cotangent.astype(jnp.float32)
    d_down = norm_back(grad_out, normed_four, scale_four, norm_gains[3])
    d_down_low = d_down.astype(jnp.bfloat16)
    d_down_all = lax.all_gather(d_down_low, "mp", axis=0, tiled=True)
    d_act = jnp.einsum("td,fd->tf", d_down_all, w_down, preferred_element_type=jnp.float32)
    grad_w_down = jnp.einsum("tf,td->fd", activated, d_down_all, preferred_element_type=jnp.float32)
    gelu_value, gelu_pull = jax.vjp(partial(jax.nn.gelu, approximate=True), up_value)
    d_up = gelu_pull(d_act)[0].astype(jnp.bfloat16)
    grad_w_up = jnp.einsum("td,tf->df", third_all, d_up, preferred_element_type=jnp.float32)
    grad_up_bias = jnp.sum(d_up, axis=0, dtype=jnp.float32)
    d_third = lax.psum_scatter(
        jnp.einsum("tf,df->td", d_up, w_up, preferred_element_type=jnp.float32),
        "mp",
        scatter_dimension=0,
        tiled=True,
    )
    d_residual = grad_out + norm_back(d_third, normed_three, scale_three, norm_gains[2])
    d_attended = norm_back(d_residual, normed_two, scale_two, norm_gains[1])
    d_att_low = d_attended.astype(jnp.bfloat16)
    d_att_all = lax.all_gather(d_att_low, "mp", axis=0, tiled=True)
    d_mixed = jnp.einsum("td,hd->th", d_att_all, w_out, preferred_element_type=jnp.float32).astype(
        jnp.bfloat16
    )
    grad_w_out = jnp.einsum("th,td->hd", mixed_heads, d_att_all, preferred_element_type=jnp.float32)
    d_mixed_blocks = d_mixed.reshape(seq_count * 2, block_rows, head_count, HD)

    def backward_block(block_item):
        query_block, d_block, row_top, row_total, number = block_item
        probs, kept_top, kept_total, key_seq = block_probs(query_block, number, row_top, row_total)
        value_seq = lax.dynamic_index_in_dim(value_all, number // 2, 0, keepdims=False)
        d_probs = jnp.einsum("qhd,khd->hqk", d_block, value_seq, preferred_element_type=jnp.float32)
        inner = jnp.sum(probs * d_probs, axis=-1, keepdims=True)
        d_scores = (relax_factor * probs * (d_probs - inner)).astype(jnp.bfloat16)
        d_query = (
            jnp.einsum("hqk,khd->qhd", d_scores, key_seq, preferred_element_type=jnp.float32)
            * query_scale
        )
        d_key = jnp.einsum(
            "hqk,qhd->khd", d_scores, query_block, preferred_element_type=jnp.float32
        )
        d_value = jnp.einsum(
            "hqk,qhd->khd", probs.astype(jnp.bfloat16), d_block, preferred_element_type=jnp.float32
        )
        return (d_query.astype(jnp.bfloat16), d_key, d_value)

    d_queries, d_keys, d_values = lax.map(
        backward_block, (queries, d_mixed_blocks, row_tops, row_totals, numbers)
    )
    d_keys = jnp.sum(d_keys.reshape(seq_count, 2, length, local_width), axis=1).reshape(
        group_rows, local_width
    )
    d_values = jnp.sum(d_values.reshape(seq_count, 2, length, local_width), axis=1).reshape(
        group_rows, local_width
    )
    d_qkv = jnp.stack(
        [
            d_queries.reshape(group_rows, local_width),
            d_keys.astype(jnp.bfloat16),
            d_values.astype(jnp.bfloat16),
        ]
    )
    grad_w_qkv = jnp.einsum("td,cte->cde", first_all, d_qkv, preferred_element_type=jnp.float32)
    grad_qv_bias = jnp.stack(
        [jnp.sum(d_qkv[0], axis=0, dtype=jnp.float32), jnp.sum(d_qkv[2], axis=0, dtype=jnp.float32)]
    )
    d_first = lax.psum_scatter(
        jnp.einsum("cte,cde->td", d_qkv, w_qkv, preferred_element_type=jnp.float32).astype(
            jnp.bfloat16
        ),
        "mp",
        scatter_dimension=0,
        tiled=True,
    ).astype(jnp.float32)
    grad_input = d_residual + norm_back(d_first, normed_one, scale_one, norm_gains[0])
    error_terms = (d_first, d_residual, d_third, grad_out)
    normed_terms = (normed_one, normed_two, normed_three, normed_four)
    gain_sums = jnp.stack(
        [
            jnp.sum(error_term * normed_term, axis=0)
            for error_term, normed_term in zip(error_terms, normed_terms)
        ]
    )
    bias_sums = jnp.stack([jnp.sum(error_term, axis=0) for error_term in error_terms])
    outer_sums = jnp.stack([jnp.sum(d_attended, axis=0), jnp.sum(d_down, axis=0)])
    gain_sums, bias_sums, outer_sums = lax.psum((gain_sums, bias_sums, outer_sums), ("dp", "mp"))
    grad_w_qkv, grad_qv_bias, grad_w_out, grad_w_up, grad_up_bias, grad_w_down = (
        lax.psum(grad_w_qkv.astype(jnp.bfloat16), "dp").astype(jnp.float32),
        lax.psum(grad_qv_bias.astype(jnp.bfloat16), "dp").astype(jnp.float32),
        lax.psum(grad_w_out.astype(jnp.bfloat16), "dp").astype(jnp.float32),
        lax.psum(grad_w_up.astype(jnp.bfloat16), "dp").astype(jnp.float32),
        lax.psum(grad_up_bias.astype(jnp.bfloat16), "dp").astype(jnp.float32),
        lax.psum(grad_w_down.astype(jnp.bfloat16), "dp").astype(jnp.float32),
    )
    return (
        result,
        grad_input,
        gain_sums,
        bias_sums,
        grad_w_qkv,
        grad_qv_bias,
        grad_w_out,
        outer_sums,
        grad_w_up,
        grad_up_bias,
        grad_w_down,
    )


LOG2E = 1.4426950408889634
HIDDEN = -1e30


def dot_nt(a, b):
    return lax.dot_general(a, b, (((1,), (1,)), ((), ())), preferred_element_type=jnp.float32)


def dot_nn(a, b):
    return lax.dot_general(a, b, (((1,), (0,)), ((), ())), preferred_element_type=jnp.float32)


def dot_tn(a, b):
    return lax.dot_general(a, b, (((0,), (0,)), ((), ())), preferred_element_type=jnp.float32)


def attend_kernel(rows, bias_ref, q_ref, k_ref, v_ref, out_ref, weight_ref, inv_ref):
    length = q_ref.shape[0]
    bias = bias_ref[...]
    lane = lax.broadcasted_iota(jnp.int32, (1, 2 * HD), 1)
    keys = k_ref[...]
    values = v_ref[...]
    for first in range(0, length, rows):
        part = pl.ds(first, rows)
        queries = q_ref[part, :]
        query_places = lax.broadcasted_iota(jnp.int32, (rows, length), 0) + first
        key_places = lax.broadcasted_iota(jnp.int32, (rows, length), 1)
        hide = jnp.where(key_places <= query_places, 0.0, bias)
        outs, invs = [], []
        for head in range(2):
            mine = jnp.where((lane // HD) == head, queries, jnp.zeros_like(queries))
            scores = dot_nt(mine, keys) + hide
            top = jnp.max(scores, axis=1, keepdims=True)
            weights = jnp.exp2((scores - top) * (relax_factor * LOG2E))
            inv = 1.0 / jnp.sum(weights, axis=1, keepdims=True)
            low = weights.astype(jnp.bfloat16)
            weight_ref[head, part, :] = low
            outs.append(dot_nn(low, values) * inv)
            invs.append(inv)
        out_ref[part, :] = jnp.where(lane < HD, outs[0], outs[1]).astype(jnp.bfloat16)
        inv_ref[part, :] = jnp.where(lane < HD, invs[0], invs[1])


def attend(queries, keys, values, bias):
    length, width = queries.shape
    pairs = width // (2 * HD)
    column = pl.BlockSpec((length, 2 * HD), lambda i: (0, i))
    return pl.pallas_call(
        partial(attend_kernel, length // 2),
        grid=(pairs,),
        in_specs=[pl.BlockSpec((1, length), lambda i: (0, 0)), column, column, column],
        out_specs=[column, pl.BlockSpec((2, length, length), lambda i: (i, 0, 0)), column],
        out_shape=[
            jax.ShapeDtypeStruct((length, width), jnp.bfloat16),
            jax.ShapeDtypeStruct((2 * pairs, length, length), jnp.bfloat16),
            jax.ShapeDtypeStruct((length, width), jnp.float32),
        ],
        compiler_params=pltpu.CompilerParams(vmem_limit_bytes=56 * 2**20),
        cost_estimate=pl.CostEstimate(
            flops=pairs * 6 * 10**9, bytes_accessed=pairs * 7 * 10**6, transcendentals=0
        ),
    )(bias, queries, keys, values)


def flip(value, bit):
    count = lax.axis_size("dp")
    return lax.ppermute(value, "dp", [(i, i ^ bit) for i in range(count)])


def cross(value):
    return lax.ppermute(value, "mp", [(0, 1), (1, 0)])


def block(value, index, count, axis):
    size = value.shape[axis] // count
    return lax.dynamic_slice_in_dim(value, index * size, size, axis)


def low(value):
    return value.astype(jnp.bfloat16)


MESH = pl.DeviceIdType.MESH
CHUNK = 128


def remote(source, target, sems, index, device):
    return pltpu.make_async_remote_copy(
        src_ref=source,
        dst_ref=target,
        send_sem=sems.at[(0, *index)],
        recv_sem=sems.at[(1, *index)],
        device_id=device,
        device_id_type=MESH,
    )


def aligned(start, size, unit=16):
    return pl.ds(pl.multiple_of(start, unit), size)


def wide(value):
    return value.astype(jnp.float32)


def back_kernel(
    query_scale,
    q_ref,
    k_ref,
    v_ref,
    mixed_ref,
    grad_ref,
    inv_ref,
    weight_ref,
    w_ref,
    first_ref,
    tokens_ref,
    residual_ref,
    gain_ref,
    small_ref,
    g_down,
    g_up,
    g_out,
    input_ref,
    sums_ref,
    t_down,
    t_up,
    t_out,
    t_qkv,
    ds_ref,
    dqkv_ref,
    d_first,
    g_qkv,
    columns_of,
    small_out,
    small_in,
    mine,
    core_in,
    held,
    x_out,
    x_in,
    y_out,
    y_in,
    z_out,
    z_in,
    last,
    load_sem,
    core_sem,
    x_sem,
    y_sem,
    z_sem,
    zz_sem,
    yy_sem,
    cc_sem,
    keep_sem,
    small_sem,
):
    now = pl.program_id(0)
    place = lax.axis_index("dp")
    turn = lax.axis_index("mp")
    core, side, level = place % 2, (place // 2) % 2, place // 4
    levels = lax.axis_size("dp") // 4
    sibling = {"dp": place + 1 - 2 * core}
    across = {"mp": 1 - turn}
    beside = {"dp": place + 2 - 4 * side}
    floors = [{"dp": (level + step) % levels * 4 + place % 4} for step in range(1, levels)]
    half, piece = CHUNK // 2, CHUNK // 2 // levels
    width = d_first.shape[1]
    pairs = width // (2 * HD)
    q_down, q_up, q_out = t_down.shape[0] // 2, t_up.shape[0] // 2, t_out.shape[0] // 2
    wides = t_up.shape[1] // width
    n_down, n_up, n_out = q_down // CHUNK, q_up // CHUNK * wides, q_out // CHUNK
    n_head = t_qkv.shape[1] // 2 // CHUNK
    s_up = n_down
    s_out = s_up + n_up
    s_qkv = s_out + n_out
    chunks = s_qkv + 3 * n_head

    @pl.when(now == 0)
    def _():
        barrier = pltpu.get_barrier_semaphore()
        partners = [sibling, across, beside, *floors]
        for partner in partners:
            pl.semaphore_signal(barrier, inc=1, device_id=partner, device_id_type=MESH)
        pl.semaphore_wait(barrier, len(partners))


    def pick(chunk, action):
        @pl.when(chunk < s_up)
        def _():
            action(
                lambda group, which: g_down.at[
                    aligned((2 * group + which) * q_down + chunk * CHUNK, CHUNK), :
                ],
                lambda which, first, size: t_down.at[aligned(which * q_down + chunk * CHUNK + first, size), :],
            )

        @pl.when((chunk >= s_up) & (chunk < s_out))
        def _():
            row = (chunk - s_up) // wides * CHUNK
            column = (chunk - s_up) % wides * width
            action(
                lambda group, which: g_up.at[
                    aligned(which * q_up + row, CHUNK), aligned(group * wides * width + column, width, 128)
                ],
                lambda which, first, size: t_up.at[
                    aligned(which * q_up + row + first, size), aligned(column, width, 128)
                ],
            )

        @pl.when((chunk >= s_out) & (chunk < s_qkv))
        def _():
            action(
                lambda group, which: g_out.at[
                    aligned((2 * group + which) * q_out + (chunk - s_out) * CHUNK, CHUNK), :
                ],
                lambda which, first, size: t_out.at[
                    aligned(which * q_out + (chunk - s_out) * CHUNK + first, size), :
                ],
            )

        @pl.when(chunk >= s_qkv)
        def _():
            kind = (chunk - s_qkv) // n_head
            row = (chunk - s_qkv) % n_head * CHUNK
            action(
                lambda group, which: g_qkv.at[group, kind, aligned(which * n_head * CHUNK + row, CHUNK), :],
                lambda which, first, size: t_qkv.at[kind, aligned(which * n_head * CHUNK + row + first, size), :],
            )

    def any_source(group, which):
        return g_down.at[pl.ds(0, CHUNK), :]

    def any_target(which, first, size):
        return t_down.at[pl.ds(0, size), :]

    def loads(source, slot):
        copies = []
        for index, group in enumerate((1, 0)):
            copies.append(pltpu.make_async_copy(source(group, core), mine.at[index], load_sem.at[index]))
            copies.append(
                remote(source(group, 1 - core), core_in.at[slot, index], core_sem, (slot, index), sibling)
            )
        return copies

    def x_copy(slot):
        return remote(x_out, x_in.at[slot], x_sem, (slot,), across)

    def y_copy(slot):
        return remote(y_out.at[aligned((1 - side) * half, half)], y_in.at[slot], y_sem, (slot,), beside)

    def z_copies(slot):
        return [
            remote(
                z_out.at[aligned((level + step) % levels * piece, piece)],
                z_in.at[slot, step - 1],
                z_sem,
                (slot, step - 1),
                floors[step - 1],
            )
            for step in range(1, levels)
        ]

    def keep_copies(target, slot):
        part = target(core, side * half + level * piece, piece)
        copies = [pltpu.make_async_copy(last, part, keep_sem)]
        for step in range(1, levels):
            copies.append(remote(last, part, zz_sem, (slot, step - 1), floors[step - 1]))
        return copies

    def yy_copy(target, slot):
        part = target(core, side * half, half)
        return remote(part, part, yy_sem, (slot,), beside)

    def cc_copy(target, slot):
        part = target(core, 0, CHUNK)
        return remote(part, part, cc_sem, (slot,), sibling)

    def stage_7(chunk, slot):
        cc_copy(any_target, slot).wait()

    def stage_6(chunk, slot):
        yy_copy(any_target, slot).wait()
        pick(chunk, lambda source, target: cc_copy(target, slot).start())

    def stage_5(chunk, slot):
        for copy in keep_copies(any_target, slot):
            copy.wait()
        pick(chunk, lambda source, target: yy_copy(target, slot).start())

    def stage_4(chunk, slot):
        for copy in z_copies(slot):
            copy.wait()
        total = wide(z_out[aligned(level * piece, piece), :])
        for step in range(1, levels):
            total = total + wide(z_in[slot, step - 1])
        last[...] = low(total)

        def send(source, target):
            for copy in keep_copies(target, slot):
                copy.start()

        pick(chunk, send)

    def stage_3(chunk, slot):
        y_copy(slot).wait()
        z_out[...] = low(wide(y_out[aligned(side * half, half), :]) + wide(y_in[slot]))
        for copy in z_copies(slot):
            copy.start()

    def stage_2(chunk, slot):
        x_copy(slot).wait()
        y_out[...] = low(held[...] + wide(x_in[slot]))
        y_copy(slot).start()

    def stage_1(chunk, slot):
        for copy in loads(any_source, slot):
            copy.wait()
        x_out[...] = low(wide(mine[0]) + wide(core_in[slot, 0]))
        x_copy(slot).start()
        held[...] = wide(mine[1]) + wide(core_in[slot, 1])

    def stage_0(chunk, slot):
        def send(source, target):
            for copy in loads(source, slot):
                copy.start()

        pick(chunk, send)

    stages = [stage_0, stage_1, stage_2, stage_3, stage_4, stage_5, stage_6, stage_7]
    for stage in reversed(range(len(stages))):
        chunk = now - stage

        @pl.when((chunk >= 0) & (chunk < chunks))
        def _(stage=stage, chunk=chunk):
            stages[stage](chunk, chunk % 2)


    @pl.when(now < 2 * pairs)
    def _():
        head = now % 2
        pair = now // 2
        lane = lax.broadcasted_iota(jnp.int32, (1, 2 * HD), 1)
        own = (lane // HD) == head
        scaled = wide(grad_ref[...]) * inv_ref[...]
        grad = jnp.where(own, scaled * relax_factor, 0.0).astype(jnp.bfloat16)
        inner = jnp.sum(wide(grad) * wide(mixed_ref[...]), axis=1, keepdims=True)
        d_probs = dot_nt(grad, v_ref[...])
        ds_ref[...] = low(wide(weight_ref[0]) * (d_probs - inner))
        dq = low(dot_nn(ds_ref[...], k_ref[...]) * query_scale)
        dk = low(dot_tn(ds_ref[...], q_ref[...]))
        dv = low(dot_tn(weight_ref[0], low(scaled)))
        for index, value in enumerate((dq, dk, dv)):
            part = pl.ds(index * 2 * HD, 2 * HD)
            dqkv_ref[:, part] = jnp.where(own | (head == 0), value, dqkv_ref[:, part])

        @pl.when(head == 1)
        def _():
            d_qkv = dqkv_ref[...]
            grads = low(dot_tn(d_qkv, first_ref[...]))
            group, start = pair // (pairs // 2), pair % (pairs // 2) * 2 * HD
            for index in range(3):
                g_qkv[group, index, aligned(start, 2 * HD), :] = grads[index * 2 * HD : (index + 1) * 2 * HD]
            columns = jnp.sum(wide(d_qkv), axis=0, keepdims=True)
            columns_of[group, 0:1, aligned(start, 2 * HD, 128)] = columns[:, : 2 * HD]
            columns_of[group, 0:1, aligned(width // 2 + start, 2 * HD, 128)] = columns[:, 4 * HD :]
            weights = jnp.concatenate([w_ref[0], w_ref[1], w_ref[2]], axis=1)
            update = dot_nt(d_qkv, weights)

            @pl.when(pair == 0)
            def _():
                d_first[...] = update

            @pl.when(pair > 0)
            def _():
                d_first[...] += update

    small_at = 2 * pairs

    @pl.when(now == small_at)
    def _():
        normed, scale = standardize(wide(tokens_ref[...]))
        errors = d_first[...]
        input_ref[...] = residual_ref[...] + norm_back(errors, normed, scale, gain_ref[...])
        small_out[0:1, :] = jnp.sum(errors * normed, axis=0, keepdims=True)
        small_out[1:4, :] = small_ref[1:4, :]
        small_out[4:5, :] = jnp.sum(errors, axis=0, keepdims=True)
        small_out[5:10, :] = small_ref[5:10, :]
        small_out[10:11, :] = columns_of[0, 0:1, :]
        small_out[11:13, :] = small_ref[11:13, :]
        small_out[13:14, :] = columns_of[1, 0:1, :]
        small_out[14:16, :] = small_ref[14:16, :]


    def small_copies(stage):
        if stage < 3:
            return [remote(small_out, small_in.at[stage], small_sem, (stage,), (sibling, across, beside)[stage])]
        return [
            remote(small_out, small_in.at[3 + level], small_sem, (2 + step,), floors[step - 1])
            for step in range(1, levels)
        ]

    @pl.when(now == small_at)
    def _():
        small_copies(0)[0].start()

    @pl.when(now == small_at + 1)
    def _():
        small_copies(0)[0].wait()
        small_out[...] += small_in[0]
        small_copies(1)[0].start()

    @pl.when(now == small_at + 2)
    def _():
        small_copies(1)[0].wait()
        small_out[0:10, :] += small_in[1, 0:10, :]
        small_out[10:13, :] += small_in[1, 13:16, :]
        small_copies(2)[0].start()

    @pl.when(now == small_at + 3)
    def _():
        small_copies(2)[0].wait()
        small_out[...] += small_in[2]
        small_in[3 + level] = small_out[...]
        for copy in small_copies(3):
            copy.start()

    @pl.when(now == small_at + 4)
    def _():
        for copy in small_copies(3):
            copy.wait()
        total = small_in[3]
        for index in range(1, levels):
            total = total + small_in[3 + index]
        sums_ref[...] = total


def back_all(queries, keys, values, mixed, grad, inv, weights, w_qkv, first, tokens, residual, gain, small, g_down, g_up, g_out, query_scale):
    length, width = queries.shape
    pairs = width // (2 * HD)
    ff = g_down.shape[0]
    levels = lax.axis_size("dp") // 4
    half, piece = CHUNK // 2, CHUNK // 2 // levels
    chunks = (ff // 4 + width // 2 * ff // 2 // width + width // 4 + 3 * width // 4) // CHUNK
    kind, sem = jnp.bfloat16, pltpu.SemaphoreType.DMA
    column = pl.BlockSpec((length, 2 * HD), lambda i: (0, jnp.minimum(i // 2, pairs - 1)))

    def whole(shape):
        return pl.BlockSpec(shape, lambda i: (0,) * len(shape), pipeline_mode=pl.Buffered(1))

    hbm = pl.BlockSpec(memory_space=pl.ANY)
    return pl.pallas_call(
        partial(back_kernel, query_scale),
        grid=(chunks + 7,),
        in_specs=[
            *[column] * 6,
            pl.BlockSpec((1, length, length), lambda i: (jnp.minimum(i, 2 * pairs - 1), 0, 0)),
            pl.BlockSpec((3, width, 2 * HD), lambda i: (0, 0, jnp.minimum(i // 2, pairs - 1))),
            whole((length, width)),
            whole((length, width)),
            whole((length, width)),
            whole((1, width)),
            whole((16, width)),
            hbm,
            hbm,
            hbm,
        ],
        out_specs=[
            whole((length, width)),
            whole((16, width)),
            hbm,
            hbm,
            hbm,
            hbm,
        ],
        out_shape=[
            jax.ShapeDtypeStruct((length, width), jnp.float32),
            jax.ShapeDtypeStruct((16, width), jnp.float32),
            jax.ShapeDtypeStruct((ff // 2, width), kind),
            jax.ShapeDtypeStruct((width, ff // 2), kind),
            jax.ShapeDtypeStruct((width // 2, width), kind),
            jax.ShapeDtypeStruct((3, width // 2, width), kind),
        ],
        scratch_shapes=[
            pltpu.VMEM((length, length), kind),
            pltpu.VMEM((length, 6 * HD), kind),
            pltpu.VMEM((length, width), jnp.float32),
            pltpu.VMEM((2, 3, width // 2, width), kind),
            pltpu.VMEM((2, 8, width), jnp.float32),
            pltpu.VMEM((16, width), jnp.float32),
            pltpu.VMEM((3 + levels, 16, width), jnp.float32),
            pltpu.VMEM((2, CHUNK, width), kind),
            pltpu.VMEM((2, 2, CHUNK, width), kind),
            pltpu.VMEM((CHUNK, width), jnp.float32),
            pltpu.VMEM((CHUNK, width), kind),
            pltpu.VMEM((2, CHUNK, width), kind),
            pltpu.VMEM((CHUNK, width), kind),
            pltpu.VMEM((2, half, width), kind),
            pltpu.VMEM((half, width), kind),
            pltpu.VMEM((2, levels - 1, piece, width), kind),
            pltpu.VMEM((piece, width), kind),
            sem((2,)),
            sem((2, 2, 2)),
            sem((2, 2)),
            sem((2, 2)),
            sem((2, 2, levels - 1)),
            sem((2, 2, levels - 1)),
            sem((2, 2)),
            sem((2, 2)),
            sem,
            sem((2, 2 + levels)),
        ],
        compiler_params=pltpu.CompilerParams(
            collective_id=0, has_side_effects=True, vmem_limit_bytes=60 * 2**20
        ),
    )(queries, keys, values, mixed, grad, inv, weights, w_qkv, first, tokens, residual, gain, small, g_down, g_up, g_out)


def sequence_shards(
    tokens,
    cond_flags,
    seg_lengths,
    norm_gains,
    norm_biases,
    w_qkv,
    qv_bias,
    w_out,
    out_biases,
    w_up,
    up_bias,
    w_down,
    cotangent,
):
    length, width = tokens.shape
    place = lax.axis_index("dp")
    turn = lax.axis_index("mp")
    core = place % 2
    side = (place // 2) % 2
    query_scale = 1.0 / (relax_factor * math.sqrt(HD))

    def in_order(which, mine, other, axis):
        return jnp.where(
            which == 0,
            jnp.concatenate([mine, other], axis=axis),
            jnp.concatenate([other, mine], axis=axis),
        )

    def fetch(weight, axis):
        first = cross(block(weight, 2 * core + side, 4, axis))
        near = in_order(side, first, flip(first, 2), axis)
        return jnp.concatenate([weight, in_order(core, near, flip(near, 1), axis)], axis=axis)

    w_qkv = fetch(w_qkv, 2)
    w_out = fetch(w_out, 0)
    w_up = fetch(w_up, 1)
    w_down = fetch(w_down, 0)
    qv_bias = jnp.concatenate([qv_bias, cross(qv_bias)], axis=1)
    up_bias = jnp.concatenate([up_bias, cross(up_bias)])

    marks = token_marks(
        lax.dynamic_index_in_dim(cond_flags, turn, 0, keepdims=False),
        lax.dynamic_index_in_dim(seg_lengths, turn, 0, keepdims=False),
        length,
    )
    hide = jnp.where(marks[None, :] == 1, 0.0, HIDDEN).astype(jnp.float32)

    source = tokens.astype(jnp.float32)
    normed_one, scale_one = standardize(source)
    first_in = low(normed_one * norm_gains[0] + norm_biases[0])
    queries = low((dot_nn(first_in, w_qkv[0]) + qv_bias[0]) * query_scale)
    keys = low(dot_nn(first_in, w_qkv[1]))
    values = low(dot_nn(first_in, w_qkv[2]) + qv_bias[1])
    mixed, kept, inv = attend(queries, keys, values, hide)
    attended = out_biases[0] + dot_nn(mixed, w_out)
    normed_two, scale_two = standardize(attended)
    residual = source + normed_two * norm_gains[1] + norm_biases[1]
    normed_three, scale_three = standardize(residual)
    third_in = low(normed_three * norm_gains[2] + norm_biases[2])
    up = dot_nn(third_in, w_up) + up_bias
    act = low(jax.nn.gelu(up, approximate=True))
    down = out_biases[1] + dot_nn(act, w_down)
    normed_four, scale_four = standardize(down)
    result = low(residual + normed_four * norm_gains[3] + norm_biases[3])
    grad_out = cotangent.astype(jnp.float32)
    d_down = norm_back(grad_out, normed_four, scale_four, norm_gains[3])
    d_down_low = low(d_down)
    pull = jax.vjp(partial(jax.nn.gelu, approximate=True), up)[1]
    d_up = low(pull(dot_nt(d_down_low, w_down))[0])
    g_down = low(dot_tn(act, d_down_low))
    g_up = low(dot_tn(third_in, d_up))
    d_third = dot_nt(d_up, w_up)
    d_residual = grad_out + norm_back(d_third, normed_three, scale_three, norm_gains[2])
    d_attended = norm_back(d_residual, normed_two, scale_two, norm_gains[1])
    d_att_low = low(d_attended)
    g_out = low(dot_tn(mixed, d_att_low))
    d_mixed = low(dot_nt(d_att_low, w_out))

    def rows(value):
        return jnp.sum(value, axis=0, dtype=jnp.float32).reshape(-1, width)

    blank = jnp.zeros((1, width), jnp.float32)
    up_rows = rows(d_up)
    small = jnp.concatenate(
        [
            blank,
            rows(d_residual * normed_two),
            rows(d_third * normed_three),
            rows(grad_out * normed_four),
            blank,
            rows(d_residual),
            rows(d_third),
            rows(grad_out),
            rows(d_attended),
            rows(d_down),
            blank,
            up_rows[:2],
            blank,
            up_rows[2:],
        ]
    )
    grad_input, sums, t_down, t_up, t_out, t_qkv = back_all(
        queries, keys, values, mixed, d_mixed, inv, kept, w_qkv, first_in, tokens, d_residual,
        norm_gains[:1], small, g_down, g_up, g_out, query_scale,
    )
    return (
        result,
        grad_input,
        sums[:4],
        sums[4:8],
        t_qkv.astype(jnp.float32).transpose(0, 2, 1),
        sums[10].reshape(2, -1),
        t_out.astype(jnp.float32),
        sums[8:10],
        t_up.astype(jnp.float32),
        sums[11:13].reshape(-1),
        t_down.astype(jnp.float32),
    )


def solution(mesh):
    in_specs = (
        P(("dp", "mp"), None),
        P("dp", None),
        P("dp", None),
        P(),
        P(),
        P(None, None, "mp"),
        P(None, "mp"),
        P("mp", None),
        P(),
        P(None, "mp"),
        P("mp"),
        P("mp", None),
        P(("dp", "mp"), None),
    )
    out_specs = (
        P(("dp", "mp"), None),
        P(("dp", "mp"), None),
        P(),
        P(),
        P(None, None, "mp"),
        P(None, "mp"),
        P("mp", None),
        P(),
        P(None, "mp"),
        P("mp"),
        P("mp", None),
    )
    per_device = mesh.shape["dp"] * mesh.shape["mp"]

    def step(*args):
        whole_sequences = args[1].shape[0] == per_device
        local = sequence_shards if whole_sequences and mesh.shape["mp"] == 2 and mesh.shape["dp"] == 16 else shards
        return jax.shard_map(
            local, mesh=mesh, in_specs=in_specs, out_specs=out_specs, check_vma=False
        )(*args)

    return step
```

```python
from functools import partial
import math

import jax
import jax.numpy as jnp
from jax import lax
from jax.experimental import pallas as pl
from jax.experimental.pallas import tpu as pltpu
from jax.sharding import PartitionSpec as P

HD = 64


epsilon = 1e-05
relax_factor = 32.0


def standardize(entries):
    average = jnp.mean(entries, axis=-1, keepdims=True)
    centred = entries - average
    spread = jnp.mean(centred * centred, axis=-1, keepdims=True)
    inv_std = lax.rsqrt(spread + epsilon)
    return (centred * inv_std, inv_std)


def norm_back(grad_in, normed, inv_std, gain_row):
    weighted = grad_in * gain_row
    return inv_std * (
        weighted
        - jnp.mean(weighted, axis=-1, keepdims=True)
        - normed * jnp.mean(weighted * normed, axis=-1, keepdims=True)
    )


def token_marks(seg_flags, lengths, length):
    position = jnp.arange(length, dtype=jnp.int32)
    segment = (position >= lengths[0]).astype(jnp.int32) + (
        position >= lengths[0] + lengths[1]
    ).astype(jnp.int32)
    segment_hits = (segment[:, None] == jnp.arange(3, dtype=jnp.int32)[None, :]).astype(jnp.int32)
    return jnp.sum(segment_hits * seg_flags[None, :], axis=1)


def block_mask(marks_seq, first_row, block_rows, length):
    query_places = first_row + jnp.arange(block_rows, dtype=jnp.int32)
    key_places = jnp.arange(length, dtype=jnp.int32)
    return (key_places[None, :] <= query_places[:, None]) | (marks_seq[None, :] == 1)


def shards(
    tokens,
    cond_flags,
    seg_lengths,
    norm_gains,
    norm_biases,
    w_qkv,
    qv_bias,
    w_out,
    out_biases,
    w_up,
    up_bias,
    w_down,
    cotangent,
):
    shard_rows = tokens.shape[0]
    group_rows = shard_rows * lax.axis_size("mp")
    seq_count = cond_flags.shape[0]
    length = group_rows // seq_count
    block_rows = length // 2
    head_count = w_qkv.shape[2] // HD
    local_width = head_count * HD
    query_scale = 1.0 / (relax_factor * math.sqrt(HD))
    all_marks = jax.vmap(lambda seg_flags, lengths: token_marks(seg_flags, lengths, length))(
        cond_flags, seg_lengths
    )
    numbers = jnp.arange(seq_count * 2, dtype=jnp.int32)
    source = tokens.astype(jnp.float32)
    normed_one, scale_one = standardize(source)
    first_in = (normed_one * norm_gains[0] + norm_biases[0]).astype(jnp.bfloat16)
    first_all = lax.all_gather(first_in, "mp", axis=0, tiled=True)
    bias_rows = jnp.stack([qv_bias[0], jnp.zeros_like(qv_bias[0]), qv_bias[1]])
    projected = (
        jnp.einsum("td,cde->cte", first_all, w_qkv, preferred_element_type=jnp.float32)
        + bias_rows[:, None, :]
    )
    queries = (
        (projected[0] * query_scale)
        .astype(jnp.bfloat16)
        .reshape(seq_count * 2, block_rows, head_count, HD)
    )
    key_all = projected[1].astype(jnp.bfloat16).reshape(seq_count, length, head_count, HD)
    value_all = projected[2].astype(jnp.bfloat16).reshape(seq_count, length, head_count, HD)

    def block_probs(query_block, number, row_top, row_total):
        sequence = number // 2
        first_row = number % 2 * block_rows
        key_seq = lax.dynamic_index_in_dim(key_all, sequence, 0, keepdims=False)
        allowed = block_mask(
            lax.dynamic_index_in_dim(all_marks, sequence, 0, keepdims=False),
            first_row,
            block_rows,
            length,
        )
        scores = jnp.einsum(
            "qhd,khd->hqk", query_block, key_seq, preferred_element_type=jnp.float32
        )
        if row_top is None:
            row_top = jnp.max(jnp.where(allowed[None], scores, -1e30), axis=-1, keepdims=True)
        weights = jnp.exp(jnp.where(allowed[None], (scores - row_top) * relax_factor, -30000.0))
        if row_total is None:
            row_total = jnp.sum(weights, axis=-1, keepdims=True)
        return (weights / row_total, row_top, row_total, key_seq)

    def forward_block(block_item):
        query_block, number = block_item
        probs, row_top, row_total, key_seq = block_probs(query_block, number, None, None)
        value_seq = lax.dynamic_index_in_dim(value_all, number // 2, 0, keepdims=False)
        mixed_block = jnp.einsum(
            "hqk,khd->qhd",
            probs.astype(jnp.bfloat16),
            value_seq,
            preferred_element_type=jnp.float32,
        )
        return (mixed_block.astype(jnp.bfloat16), row_top, row_total)

    mixed_heads, row_tops, row_totals = lax.map(forward_block, (queries, numbers))
    mixed_heads = mixed_heads.reshape(group_rows, local_width)
    attended = (
        lax.psum_scatter(
            jnp.dot(mixed_heads, w_out, preferred_element_type=jnp.float32),
            "mp",
            scatter_dimension=0,
            tiled=True,
        )
        + out_biases[0]
    )
    normed_two, scale_two = standardize(attended)
    residual = source + normed_two * norm_gains[1] + norm_biases[1]
    normed_three, scale_three = standardize(residual)
    third_in = (normed_three * norm_gains[2] + norm_biases[2]).astype(jnp.bfloat16)
    third_all = lax.all_gather(third_in, "mp", axis=0, tiled=True)
    up_value = jnp.dot(third_all, w_up, preferred_element_type=jnp.float32) + up_bias
    activated = jax.nn.gelu(up_value, approximate=True).astype(jnp.bfloat16)
    down = (
        lax.psum_scatter(
            jnp.dot(activated, w_down, preferred_element_type=jnp.float32),
            "mp",
            scatter_dimension=0,
            tiled=True,
        )
        + out_biases[1]
    )
    normed_four, scale_four = standardize(down)
    result = (residual + normed_four * norm_gains[3] + norm_biases[3]).astype(jnp.bfloat16)
    grad_out = cotangent.astype(jnp.float32)
    d_down = norm_back(grad_out, normed_four, scale_four, norm_gains[3])
    d_down_low = d_down.astype(jnp.bfloat16)
    d_down_all = lax.all_gather(d_down_low, "mp", axis=0, tiled=True)
    d_act = jnp.einsum("td,fd->tf", d_down_all, w_down, preferred_element_type=jnp.float32)
    grad_w_down = jnp.einsum("tf,td->fd", activated, d_down_all, preferred_element_type=jnp.float32)
    gelu_value, gelu_pull = jax.vjp(partial(jax.nn.gelu, approximate=True), up_value)
    d_up = gelu_pull(d_act)[0].astype(jnp.bfloat16)
    grad_w_up = jnp.einsum("td,tf->df", third_all, d_up, preferred_element_type=jnp.float32)
    grad_up_bias = jnp.sum(d_up, axis=0, dtype=jnp.float32)
    d_third = lax.psum_scatter(
        jnp.einsum("tf,df->td", d_up, w_up, preferred_element_type=jnp.float32),
        "mp",
        scatter_dimension=0,
        tiled=True,
    )
    d_residual = grad_out + norm_back(d_third, normed_three, scale_three, norm_gains[2])
    d_attended = norm_back(d_residual, normed_two, scale_two, norm_gains[1])
    d_att_low = d_attended.astype(jnp.bfloat16)
    d_att_all = lax.all_gather(d_att_low, "mp", axis=0, tiled=True)
    d_mixed = jnp.einsum("td,hd->th", d_att_all, w_out, preferred_element_type=jnp.float32).astype(
        jnp.bfloat16
    )
    grad_w_out = jnp.einsum("th,td->hd", mixed_heads, d_att_all, preferred_element_type=jnp.float32)
    d_mixed_blocks = d_mixed.reshape(seq_count * 2, block_rows, head_count, HD)

    def backward_block(block_item):
        query_block, d_block, row_top, row_total, number = block_item
        probs, kept_top, kept_total, key_seq = block_probs(query_block, number, row_top, row_total)
        value_seq = lax.dynamic_index_in_dim(value_all, number // 2, 0, keepdims=False)
        d_probs = jnp.einsum("qhd,khd->hqk", d_block, value_seq, preferred_element_type=jnp.float32)
        inner = jnp.sum(probs * d_probs, axis=-1, keepdims=True)
        d_scores = (relax_factor * probs * (d_probs - inner)).astype(jnp.bfloat16)
        d_query = (
            jnp.einsum("hqk,khd->qhd", d_scores, key_seq, preferred_element_type=jnp.float32)
            * query_scale
        )
        d_key = jnp.einsum(
            "hqk,qhd->khd", d_scores, query_block, preferred_element_type=jnp.float32
        )
        d_value = jnp.einsum(
            "hqk,qhd->khd", probs.astype(jnp.bfloat16), d_block, preferred_element_type=jnp.float32
        )
        return (d_query.astype(jnp.bfloat16), d_key, d_value)

    d_queries, d_keys, d_values = lax.map(
        backward_block, (queries, d_mixed_blocks, row_tops, row_totals, numbers)
    )
    d_keys = jnp.sum(d_keys.reshape(seq_count, 2, length, local_width), axis=1).reshape(
        group_rows, local_width
    )
    d_values = jnp.sum(d_values.reshape(seq_count, 2, length, local_width), axis=1).reshape(
        group_rows, local_width
    )
    d_qkv = jnp.stack(
        [
            d_queries.reshape(group_rows, local_width),
            d_keys.astype(jnp.bfloat16),
            d_values.astype(jnp.bfloat16),
        ]
    )
    grad_w_qkv = jnp.einsum("td,cte->cde", first_all, d_qkv, preferred_element_type=jnp.float32)
    grad_qv_bias = jnp.stack(
        [jnp.sum(d_qkv[0], axis=0, dtype=jnp.float32), jnp.sum(d_qkv[2], axis=0, dtype=jnp.float32)]
    )
    d_first = lax.psum_scatter(
        jnp.einsum("cte,cde->td", d_qkv, w_qkv, preferred_element_type=jnp.float32).astype(
            jnp.bfloat16
        ),
        "mp",
        scatter_dimension=0,
        tiled=True,
    ).astype(jnp.float32)
    grad_input = d_residual + norm_back(d_first, normed_one, scale_one, norm_gains[0])
    error_terms = (d_first, d_residual, d_third, grad_out)
    normed_terms = (normed_one, normed_two, normed_three, normed_four)
    gain_sums = jnp.stack(
        [
            jnp.sum(error_term * normed_term, axis=0)
            for error_term, normed_term in zip(error_terms, normed_terms)
        ]
    )
    bias_sums = jnp.stack([jnp.sum(error_term, axis=0) for error_term in error_terms])
    outer_sums = jnp.stack([jnp.sum(d_attended, axis=0), jnp.sum(d_down, axis=0)])
    gain_sums, bias_sums, outer_sums = lax.psum((gain_sums, bias_sums, outer_sums), ("dp", "mp"))
    grad_w_qkv, grad_qv_bias, grad_w_out, grad_w_up, grad_up_bias, grad_w_down = (
        lax.psum(grad_w_qkv.astype(jnp.bfloat16), "dp").astype(jnp.float32),
        lax.psum(grad_qv_bias.astype(jnp.bfloat16), "dp").astype(jnp.float32),
        lax.psum(grad_w_out.astype(jnp.bfloat16), "dp").astype(jnp.float32),
        lax.psum(grad_w_up.astype(jnp.bfloat16), "dp").astype(jnp.float32),
        lax.psum(grad_up_bias.astype(jnp.bfloat16), "dp").astype(jnp.float32),
        lax.psum(grad_w_down.astype(jnp.bfloat16), "dp").astype(jnp.float32),
    )
    return (
        result,
        grad_input,
        gain_sums,
        bias_sums,
        grad_w_qkv,
        grad_qv_bias,
        grad_w_out,
        outer_sums,
        grad_w_up,
        grad_up_bias,
        grad_w_down,
    )


LOG2E = 1.4426950408889634
HIDDEN = -1e30


def dot_nt(a, b):
    return lax.dot_general(a, b, (((1,), (1,)), ((), ())), preferred_element_type=jnp.float32)


def dot_nn(a, b):
    return lax.dot_general(a, b, (((1,), (0,)), ((), ())), preferred_element_type=jnp.float32)


def dot_tn(a, b):
    return lax.dot_general(a, b, (((0,), (0,)), ((), ())), preferred_element_type=jnp.float32)


def low(value):
    return value.astype(jnp.bfloat16)


MESH = pl.DeviceIdType.MESH
CHUNK = 128


def remote(source, target, sems, index, device):
    return pltpu.make_async_remote_copy(
        src_ref=source,
        dst_ref=target,
        send_sem=sems.at[(0, *index)],
        recv_sem=sems.at[(1, *index)],
        device_id=device,
        device_id_type=MESH,
    )


def aligned(start, size, unit=16):
    return pl.ds(pl.multiple_of(start, unit), size)


def wide(value):
    return value.astype(jnp.float32)


GELU_SCALE = math.sqrt(2.0 / math.pi)
GELU_CUBE = 0.044715


def gelu_both(up):
    square = up * up
    half = 0.5 * jnp.tanh(up * (GELU_SCALE + GELU_SCALE * GELU_CUBE * square)) + 0.5
    value = up * half
    slope = half + value * (1.0 - half) * (2.0 * GELU_SCALE + 6.0 * GELU_SCALE * GELU_CUBE * square)
    return value, slope


def column_sum(value):
    return jnp.sum(value, axis=0, keepdims=True)


def layer_kernel(
    parts,
    att_ref,
    res_ref,
    cot_ref,
    gain_ref,
    d_down_ref,
    third_ref,
    act_ref,
    slope_ref,
    w_up_ref,
    w_down_ref,
    sums_ref,
    d_res_ref,
    d_att_ref,
    g_down_ref,
    g_up_ref,
    up_sum_ref,
    small_ref,
    total,
    d_up_ref,
):
    now = pl.program_id(0)
    length = att_ref.shape[0]
    chunks = pl.num_programs(0) - 1
    step = length // parts
    blocks = [pl.ds(first, step) for first in range(0, length, step)]

    def gain(index):
        return gain_ref[index : index + 1, :]

    @pl.when(now < chunks)
    def _():
        for part in blocks:
            d_act = dot_nt(d_down_ref[part, :], w_down_ref[...])
            d_up = low(d_act * wide(slope_ref[part, :]))
            d_up_ref[part, :] = d_up
            update = dot_nt(d_up, w_up_ref[...])
            total[part, :] = jnp.where(now == 0, update, update + total[part, :])
        up_sum_ref[0] = column_sum(wide(d_up_ref[...]))
        g_down_ref[...] = low(dot_tn(act_ref[...], d_down_ref[...]))
        g_up_ref[...] = low(dot_tn(third_ref[...], d_up_ref[...]))

    @pl.when(now == chunks)
    def _():
        sums = [0.0] * 5
        for part in blocks:
            normed_three, scale_three = standardize(res_ref[part, :])
            normed_two, scale_two = standardize(att_ref[part, :])
            d_third = total[part, :]
            d_residual = wide(cot_ref[part, :]) + norm_back(d_third, normed_three, scale_three, gain(2))
            d_res_ref[part, :] = d_residual
            d_attended = norm_back(d_residual, normed_two, scale_two, gain(1))
            d_att_ref[part, :] = low(d_attended)
            terms = [d_residual * normed_two, d_third * normed_three, d_residual, d_third, d_attended]
            sums = [old + column_sum(term) for old, term in zip(sums, terms)]
        small_ref[...] = sums_ref[...]
        for index, row in enumerate((1, 2, 5, 6, 8)):
            small_ref[row : row + 1, :] = sums[index]


def layer_back(attended, residual, cotangent, gains, d_down, third, acts, slopes, w_up, w_down, small):
    length, width = attended.shape
    ff = w_up.shape[1]
    size = 512
    chunks = ff // size
    kind = jnp.bfloat16

    def whole(shape):
        return pl.BlockSpec(shape, lambda i: (0,) * len(shape), pipeline_mode=pl.Buffered(1))

    def back_of(i):
        return jnp.minimum(i, chunks - 1)

    return pl.pallas_call(
        partial(layer_kernel, 5),
        grid=(chunks + 1,),
        in_specs=[
            whole((length, width)),
            whole((length, width)),
            whole((length, width)),
            whole((4, width)),
            whole((length, width)),
            whole((length, width)),
            pl.BlockSpec((length, size), lambda i: (0, back_of(i))),
            pl.BlockSpec((length, size), lambda i: (0, back_of(i))),
            pl.BlockSpec((width, size), lambda i: (0, back_of(i))),
            pl.BlockSpec((size, width), lambda i: (back_of(i), 0)),
            whole((16, width)),
        ],
        out_specs=[
            whole((length, width)),
            whole((length, width)),
            pl.BlockSpec((size, width), lambda i: (back_of(i), 0)),
            pl.BlockSpec((width, size), lambda i: (0, back_of(i))),
            pl.BlockSpec((1, 1, size), lambda i: (back_of(i), 0, 0)),
            whole((16, width)),
        ],
        out_shape=[
            jax.ShapeDtypeStruct((length, width), jnp.float32),
            jax.ShapeDtypeStruct((length, width), kind),
            jax.ShapeDtypeStruct((ff, width), kind),
            jax.ShapeDtypeStruct((width, ff), kind),
            jax.ShapeDtypeStruct((chunks, 1, size), jnp.float32),
            jax.ShapeDtypeStruct((16, width), jnp.float32),
        ],
        scratch_shapes=[
            pltpu.VMEM((length, width), jnp.float32),
            pltpu.VMEM((length, size), kind),
        ],
        compiler_params=pltpu.CompilerParams(vmem_limit_bytes=62 * 2**20),
    )(attended, residual, cotangent, gains, d_down, third, acts, slopes, w_up, w_down, small)


def front_kernel(
    query_scale,
    events,
    flags_ref,
    lengths_ref,
    gain_ref,
    shift_ref,
    out_bias_ref,
    qv_bias_ref,
    up_bias_ref,
    tokens_in,
    cot_in,
    own_qkv,
    own_out,
    own_up,
    own_down,
    q_ref,
    k_ref,
    v_ref,
    inv_ref,
    weight_ref,
    act_ref,
    slope_ref,
    small_ref,
    first_out,
    mixed_out,
    att_out,
    residual_out,
    third_out,
    result_out,
    d_down_out,
    all_qkv,
    all_out,
    all_up,
    all_down,
    first_ref,
    mixed_ref,
    tokens_ref,
    third_ref,
    att_ref,
    residual_ref,
    total,
    qkv_buf,
    out_buf,
    up_buf,
    down_buf,
    hide_ref,
    qv_all,
    up_bias_all,
    qkv_load,
    out_load,
    up_load,
    down_load,
    qkv_keep,
    out_keep,
    up_keep,
    down_keep,
    bias_sem,
    x_sem,
    y_sem,
    c_sem,
    in_sem,
    save_sem,
    end_sem,
):
    now = pl.program_id(0)
    place = lax.axis_index("dp")
    turn = lax.axis_index("mp")
    core, side = place % 2, (place // 2) % 2
    sibling = {"dp": place + 1 - 2 * core}
    across = {"mp": 1 - turn}
    beside = {"dp": place + 2 - 4 * side}
    length, width = tokens_ref.shape
    pairs = width // (2 * HD)
    size = act_ref.shape[1]
    ff = all_up.shape[1]
    chunks = ff // size
    mid = pairs
    end = mid + chunks + 1
    parts = 5
    step = length // parts
    blocks = [pl.ds(start, step) for start in range(0, length, step)]

    def gain(index):
        return gain_ref[index : index + 1, :]

    def shift(index):
        return shift_ref[index : index + 1, :]


    q_qkv, q_out, q_up, q_down = width // 8, width // 8, ff // 8, ff // 8
    row_up = width // 4

    def places(index, quarter, count):
        if index < 3:
            cols = aligned(quarter * q_qkv, count * q_qkv, 128)
            far = aligned(width // 2 + quarter * q_qkv, count * q_qkv, 128)
            return own_qkv.at[index, :, cols], all_qkv.at[index, :, far]
        if index < 4:
            rows = aligned(quarter * q_out, count * q_out)
            return own_out.at[rows, :], all_out.at[aligned(width // 2 + quarter * q_out, count * q_out), :]
        if index < 8:
            rows = pl.ds((index - 4) * row_up, row_up)
            cols = aligned(quarter * q_up, count * q_up, 128)
            return own_up.at[rows, cols], all_up.at[rows, aligned(ff // 2 + quarter * q_up, count * q_up, 128)]
        cols = pl.ds((index - 8) * (width // 4), width // 4)
        rows = aligned(quarter * q_down, count * q_down)
        return own_down.at[rows, cols], all_down.at[aligned(ff // 2 + quarter * q_down, count * q_down), cols]

    def hop(index, stage):
        if stage == 0:
            source, target = places(index, 2 * core + side, 1)
            return remote(source, target, x_sem, (index,), across)
        if stage == 1:
            part = places(index, 2 * core + side, 1)[1]
            return remote(part, part, y_sem, (index,), beside)
        part = places(index, 2 * core, 2)[1]
        return remote(part, part, c_sem, (index,), sibling)

    bias_copies = [
        remote(qv_bias_ref, qv_all.at[1], bias_sem, (0,), across),
        remote(up_bias_ref, up_bias_all.at[1], bias_sem, (1,), across),
    ]
    def load_pair(pair, ref):
        start = pair % (pairs // 2) * 2 * HD if ref is own_qkv else pair * 2 * HD
        return pltpu.make_async_copy(
            ref.at[:, :, aligned(start, 2 * HD, 128)], qkv_buf.at[pair % 2], qkv_load.at[pair % 2]
        )

    def load_chunk(chunk, up, down):
        slot = chunk % 2
        return [
            pltpu.make_async_copy(up.at[:, aligned(chunk * size, size, 128)], up_buf.at[slot], up_load.at[slot]),
            pltpu.make_async_copy(down.at[aligned(chunk * size, size), :], down_buf.at[slot], down_load.at[slot]),
        ]

    out_loads = [
        pltpu.make_async_copy(
            own_out, out_buf.at[pl.ds(0, width // 2), :], out_load.at[0]
        ),
        pltpu.make_async_copy(
            all_out.at[pl.ds(width // 2, width // 2), :], out_buf.at[pl.ds(width // 2, width // 2), :], out_load.at[1]
        ),
    ]

    def keep_pair(pair):
        return pltpu.make_async_copy(
            qkv_buf.at[pair % 2], all_qkv.at[:, :, aligned(pair * 2 * HD, 2 * HD, 128)], qkv_keep.at[pair % 2]
        )

    def keep_chunk(chunk):
        slot = chunk % 2
        return [
            pltpu.make_async_copy(up_buf.at[slot], all_up.at[:, aligned(chunk * size, size, 128)], up_keep.at[slot]),
            pltpu.make_async_copy(down_buf.at[slot], all_down.at[aligned(chunk * size, size), :], down_keep.at[slot]),
        ]

    keep_out = pltpu.make_async_copy(
        out_buf.at[pl.ds(0, width // 2), :], all_out.at[pl.ds(0, width // 2), :], out_keep
    )
    take_tokens = pltpu.make_async_copy(tokens_in, tokens_ref, in_sem.at[0])
    take_cot = pltpu.make_async_copy(cot_in, first_ref, in_sem.at[1])
    save_first = pltpu.make_async_copy(first_ref, first_out, save_sem.at[0])
    saves = [
        pltpu.make_async_copy(mixed_ref, mixed_out, save_sem.at[1]),
        pltpu.make_async_copy(att_ref, att_out, save_sem.at[2]),
        pltpu.make_async_copy(residual_ref, residual_out, save_sem.at[3]),
        pltpu.make_async_copy(third_ref, third_out, save_sem.at[4]),
    ]

    def end_copies(index):
        part = blocks[index]
        return [
            pltpu.make_async_copy(tokens_ref.at[part, :], result_out.at[part, :], end_sem.at[0, index]),
            pltpu.make_async_copy(mixed_ref.at[part, :], d_down_out.at[part, :], end_sem.at[1, index]),
        ]

    def run_events(slot):
        for index, stage in events.get(slot, []):
            if stage > 0:
                hop(index, stage - 1).wait()
            if stage < 3:
                hop(index, stage).start()

    @pl.when(now == 0)
    def _():
        take_tokens.start()
        load_pair(0, own_qkv).start()
        barrier = pltpu.get_barrier_semaphore()
        partners = [sibling, across, beside]
        for partner in partners:
            pl.semaphore_signal(barrier, inc=1, device_id=partner, device_id_type=MESH)
        pl.semaphore_wait(barrier, len(partners))
        for copy in bias_copies:
            copy.start()

    for moment in range(end):

        @pl.when(now == moment)
        def _(moment=moment):
            run_events(2 * moment if moment < mid else moment + mid)

    @pl.when(now == 0)
    def _():
        qv_all[0] = qv_bias_ref[...]
        up_bias_all[0] = up_bias_ref[...]
        spots = lax.broadcasted_iota(jnp.int32, (1, length), 1)
        one = lengths_ref[turn, 0]
        two = one + lengths_ref[turn, 1]
        marks = jnp.where(
            spots < one, flags_ref[turn, 0], jnp.where(spots < two, flags_ref[turn, 1], flags_ref[turn, 2])
        )
        hide_ref[...] = jnp.where(marks == 1, 0.0, HIDDEN)
        take_tokens.wait()
        for part in blocks:
            normed, _ = standardize(wide(tokens_ref[part, :]))
            first_ref[part, :] = low(normed * gain(0) + shift(0))
        save_first.start()

    @pl.when(now == pairs // 2)
    def _():
        bias_copies[0].wait()

    @pl.when(now == mid)
    def _():
        bias_copies[1].wait()


    def attend_head(head):
        lane = lax.broadcasted_iota(jnp.int32, (1, 2 * HD), 1)
        own = (lane // HD) == head
        keys = k_ref[...]
        values = jnp.where(own, v_ref[...], jnp.ones((1, 2 * HD), jnp.bfloat16))
        rows = length // 2
        spot = aligned(now * 2 * HD, 2 * HD, 128)
        for start in (0, rows):
            part = pl.ds(start, rows)
            mine = jnp.where(own, q_ref[part, :], jnp.zeros((1, 2 * HD), jnp.bfloat16))
            scores = dot_nt(mine, keys)
            query_places = lax.broadcasted_iota(jnp.int32, (rows, length), 0) + start
            key_places = lax.broadcasted_iota(jnp.int32, (rows, length), 1)
            scores = scores + jnp.where(key_places <= query_places, 0.0, hide_ref[...])
            top = jnp.max(scores, axis=1, keepdims=True)
            kept = low(jnp.exp2((scores - top) * (relax_factor * LOG2E)))
            weight_ref[head, part, :] = kept
            mixed = dot_nn(kept, values)
            inv = 1.0 / pltpu.roll(mixed, HD, 1)
            out = low(mixed * inv)
            mixed_ref[part, spot] = out if head == 0 else jnp.where(own, out, mixed_ref[part, spot])
            inv_ref[part, :] = inv if head == 0 else jnp.where(own, inv, inv_ref[part, :])

    @pl.when(now < mid)
    def _():
        pair = now
        load_pair(pair, all_qkv).wait()
        group, start = pair // (pairs // 2), pair % (pairs // 2) * 2 * HD
        parts_of = qkv_buf[pair % 2]
        projected = dot_nn(first_ref[...], jnp.concatenate([parts_of[0], parts_of[1], parts_of[2]], axis=1))
        bias_q = qv_all[group, 0:1, aligned(start, 2 * HD, 128)]
        bias_v = qv_all[group, 1:2, aligned(start, 2 * HD, 128)]
        q_ref[...] = low((projected[:, : 2 * HD] + bias_q) * query_scale)
        k_ref[...] = low(projected[:, 2 * HD : 4 * HD])
        v_ref[...] = low(projected[:, 4 * HD :] + bias_v)

    @pl.when(now < pairs // 2)
    def _():
        keep_pair(now).start()

    @pl.when(now < mid)
    def _():
        attend_head(0)

    for moment in range(mid):

        @pl.when(now == moment)
        def _(moment=moment):
            run_events(2 * moment + 1)

    @pl.when(now < mid)
    def _():
        attend_head(1)

    @pl.when((now >= 1) & (now <= pairs // 2))
    def _():
        keep_pair(now - 1).wait()

    @pl.when(now < pairs // 2 - 1)
    def _():
        load_pair(now + 1, own_qkv).start()

    @pl.when((now >= pairs // 2 - 1) & (now < mid - 1))
    def _():
        load_pair(now + 1, all_qkv).start()

    @pl.when(now == mid - 1)
    def _():
        for copy in out_loads:
            copy.start()

    @pl.when(now == mid)
    def _():
        for copy in load_chunk(0, own_up, own_down):
            copy.start()
        save_first.wait()
        take_cot.start()
        for copy in out_loads:
            copy.wait()
        keep_out.start()
        for part in blocks:
            attended = dot_nn(mixed_ref[part, :], out_buf[...]) + out_bias_ref[0:1, :]
            att_ref[part, :] = attended
            normed_two, _ = standardize(attended)
            residual = wide(tokens_ref[part, :]) + normed_two * gain(1) + shift(1)
            residual_ref[part, :] = residual
            normed_three, _ = standardize(residual)
            third_ref[part, :] = low(normed_three * gain(2) + shift(2))
            total[part, :] = jnp.broadcast_to(out_bias_ref[1:2, :], (step, width))
        for copy in saves:
            copy.start()

    @pl.when((now > mid) & (now < end))
    def _():
        for copy in load_chunk(now - mid - 1, all_up, all_down):
            copy.wait()

    @pl.when((now > mid + 1) & (now <= mid + 1 + chunks // 2))
    def _():
        for copy in keep_chunk(now - mid - 2):
            copy.wait()

    @pl.when((now > mid) & (now < mid + chunks // 2))
    def _():
        for copy in load_chunk(now - mid, own_up, own_down):
            copy.start()

    @pl.when((now >= mid + chunks // 2) & (now < end - 1))
    def _():
        for copy in load_chunk(now - mid, all_up, all_down):
            copy.start()

    @pl.when((now > mid) & (now <= mid + chunks // 2))
    def _():
        for copy in keep_chunk(now - mid - 1):
            copy.start()

    @pl.when((now > mid) & (now < end))
    def _():
        chunk = now - mid - 1
        slot = chunk % 2
        group, start = chunk // (chunks // 2), chunk % (chunks // 2) * size
        bias = up_bias_all[group, 0:1, aligned(start, size, 128)]
        for part in blocks:
            up = dot_nn(third_ref[part, :], up_buf[slot]) + bias
            value, slope = gelu_both(up)
            act = low(value)
            act_ref[part, :] = act
            slope_ref[part, :] = low(slope)
            total[part, :] += dot_nn(act, down_buf[slot])

    @pl.when(now == end)
    def _():
        take_cot.wait()
        keep_out.wait()
        for copy in saves:
            copy.wait()
        sums = [0.0, 0.0, 0.0]
        for index, part in enumerate(blocks):
            normed_four, scale_four = standardize(total[part, :])
            tokens_ref[part, :] = low(residual_ref[part, :] + normed_four * gain(3) + shift(3))
            grad_out = wide(first_ref[part, :])
            d_down = norm_back(grad_out, normed_four, scale_four, gain(3))
            mixed_ref[part, :] = low(d_down)
            for copy in end_copies(index):
                copy.start()
            terms = [grad_out * normed_four, grad_out, d_down]
            sums = [old + column_sum(term) for old, term in zip(sums, terms)]
        small_ref[...] = jnp.zeros_like(small_ref)
        small_ref[3:4, :] = sums[0]
        small_ref[7:8, :] = sums[1]
        small_ref[9:10, :] = sums[2]
        for index in range(parts):
            for copy in end_copies(index):
                copy.wait()


def front_events():
    starts = [0, 0, 1, 3, 4, 5, 7, 8, 10, 11, 13, 15]
    plan = {}
    for index, start in enumerate(starts):
        for stage, moment in enumerate((start, start + 2, start + 4, start + 5)):
            plan.setdefault(moment, []).append((index, stage))
    return {moment: sorted(items, key=lambda item: -item[1]) for moment, items in plan.items()}


def front(flags, lengths, tokens, cotangent, gains, shifts, out_biases, qv_bias, up_bias, w_qkv, w_out, w_up, w_down, query_scale):
    length, width = tokens.shape
    pairs = width // (2 * HD)
    ff = 2 * w_up.shape[1]
    size = 512
    chunks = ff // size
    kind, sem = jnp.bfloat16, pltpu.SemaphoreType.DMA

    def whole(shape):
        return pl.BlockSpec(shape, lambda i: (0,) * len(shape), pipeline_mode=pl.Buffered(1))

    hbm = pl.BlockSpec(memory_space=pl.ANY)
    smem = pl.BlockSpec(memory_space=pltpu.SMEM)
    column = pl.BlockSpec((length, 2 * HD), lambda i: (0, jnp.minimum(i, pairs - 1)))
    piece = pl.BlockSpec((length, size), lambda i: (0, jnp.clip(i - pairs - 1, 0, chunks - 1)))

    def low_like(*shape):
        return jax.ShapeDtypeStruct(shape, kind)

    def wide_like(*shape):
        return jax.ShapeDtypeStruct(shape, jnp.float32)

    return pl.pallas_call(
        partial(front_kernel, query_scale, front_events()),
        grid=(pairs + chunks + 2,),
        in_specs=[
            smem,
            smem,
            whole((4, width)),
            whole((4, width)),
            whole((2, width)),
            whole(qv_bias.shape),
            whole((1, ff // 2)),
            *[hbm] * 6,
        ],
        out_specs=[
            column,
            column,
            column,
            column,
            pl.BlockSpec((2, length, length), lambda i: (jnp.minimum(i, pairs - 1), 0, 0)),
            piece,
            piece,
            whole((16, width)),
            *[hbm] * 11,
        ],
        out_shape=[
            low_like(length, width),
            low_like(length, width),
            low_like(length, width),
            wide_like(length, width),
            low_like(2 * pairs, length, length),
            low_like(length, ff),
            low_like(length, ff),
            wide_like(16, width),
            low_like(length, width),
            low_like(length, width),
            wide_like(length, width),
            wide_like(length, width),
            low_like(length, width),
            low_like(length, width),
            low_like(length, width),
            low_like(3, width, width),
            low_like(width, width),
            low_like(width, ff),
            low_like(ff, width),
        ],
        scratch_shapes=[
            *[pltpu.VMEM((length, width), kind)] * 4,
            *[pltpu.VMEM((length, width), jnp.float32)] * 3,
            pltpu.VMEM((2, 3, width, 2 * HD), kind),
            pltpu.VMEM((width, width), kind),
            pltpu.VMEM((2, width, size), kind),
            pltpu.VMEM((2, size, width), kind),
            pltpu.VMEM((1, length), jnp.float32),
            pltpu.VMEM((2, *qv_bias.shape), jnp.float32),
            pltpu.VMEM((2, 1, ff // 2), jnp.float32),
            sem((2,)),
            sem((2,)),
            sem((2,)),
            sem((2,)),
            sem((2,)),
            sem,
            sem((2,)),
            sem((2,)),
            sem((2, 2)),
            sem((2, 12)),
            sem((2, 12)),
            sem((2, 12)),
            sem((2,)),
            sem((5,)),
            sem((2, 5)),
        ],
        compiler_params=pltpu.CompilerParams(
            collective_id=1, has_side_effects=True, vmem_limit_bytes=63 * 2**20
        ),
    )(
        flags, lengths, gains, shifts, out_biases, qv_bias, up_bias.reshape(1, -1), tokens, cotangent,
        w_qkv, w_out, w_up, w_down,
    )


def back_kernel(
    query_scale,
    q_ref,
    k_ref,
    v_ref,
    mixed_ref,
    grad_ref,
    inv_ref,
    weight_ref,
    w_ref,
    first_ref,
    tokens_ref,
    residual_ref,
    gain_ref,
    small_ref,
    g_down,
    g_up,
    g_out,
    input_ref,
    sums_ref,
    t_down,
    t_up,
    t_out,
    t_qkv,
    ds_ref,
    dqkv_ref,
    d_first,
    g_qkv,
    columns_of,
    small_out,
    small_in,
    mine,
    core_in,
    held,
    x_out,
    x_in,
    y_out,
    y_in,
    z_out,
    z_in,
    last,
    load_sem,
    core_sem,
    x_sem,
    y_sem,
    z_sem,
    zz_sem,
    yy_sem,
    cc_sem,
    keep_sem,
    small_sem,
):
    now = pl.program_id(0)
    place = lax.axis_index("dp")
    turn = lax.axis_index("mp")
    core, side, level = place % 2, (place // 2) % 2, place // 4
    levels = lax.axis_size("dp") // 4
    sibling = {"dp": place + 1 - 2 * core}
    across = {"mp": 1 - turn}
    beside = {"dp": place + 2 - 4 * side}
    floors = [{"dp": (level + step) % levels * 4 + place % 4} for step in range(1, levels)]
    half, piece = CHUNK // 2, CHUNK // 2 // levels
    width = d_first.shape[1]
    pairs = width // (2 * HD)
    q_down, q_up, q_out = t_down.shape[0] // 2, t_up.shape[0] // 2, t_out.shape[0] // 2
    wides = t_up.shape[1] // width
    n_down, n_up, n_out = q_down // CHUNK, q_up // CHUNK * wides, q_out // CHUNK
    n_head = t_qkv.shape[1] // 2 // CHUNK
    s_up = n_down
    s_out = s_up + n_up
    s_qkv = s_out + n_out
    chunks = s_qkv + 3 * n_head

    @pl.when(now == 0)
    def _():
        barrier = pltpu.get_barrier_semaphore()
        partners = [sibling, across, beside, *floors]
        for partner in partners:
            pl.semaphore_signal(barrier, inc=1, device_id=partner, device_id_type=MESH)
        pl.semaphore_wait(barrier, len(partners))


    def pick(chunk, action):
        @pl.when(chunk < s_up)
        def _():
            action(
                lambda group, which: g_down.at[
                    aligned((2 * group + which) * q_down + chunk * CHUNK, CHUNK), :
                ],
                lambda which, first, size: t_down.at[aligned(which * q_down + chunk * CHUNK + first, size), :],
            )

        @pl.when((chunk >= s_up) & (chunk < s_out))
        def _():
            row = (chunk - s_up) // wides * CHUNK
            column = (chunk - s_up) % wides * width
            action(
                lambda group, which: g_up.at[
                    aligned(which * q_up + row, CHUNK), aligned(group * wides * width + column, width, 128)
                ],
                lambda which, first, size: t_up.at[
                    aligned(which * q_up + row + first, size), aligned(column, width, 128)
                ],
            )

        @pl.when((chunk >= s_out) & (chunk < s_qkv))
        def _():
            action(
                lambda group, which: g_out.at[
                    aligned((2 * group + which) * q_out + (chunk - s_out) * CHUNK, CHUNK), :
                ],
                lambda which, first, size: t_out.at[
                    aligned(which * q_out + (chunk - s_out) * CHUNK + first, size), :
                ],
            )

        @pl.when(chunk >= s_qkv)
        def _():
            kind = (chunk - s_qkv) // n_head
            row = (chunk - s_qkv) % n_head * CHUNK
            action(
                lambda group, which: g_qkv.at[group, kind, aligned(which * n_head * CHUNK + row, CHUNK), :],
                lambda which, first, size: t_qkv.at[kind, aligned(which * n_head * CHUNK + row + first, size), :],
            )

    def any_source(group, which):
        return g_down.at[pl.ds(0, CHUNK), :]

    def any_target(which, first, size):
        return t_down.at[pl.ds(0, size), :]

    def loads(source, slot):
        copies = []
        for index, group in enumerate((1, 0)):
            copies.append(pltpu.make_async_copy(source(group, core), mine.at[index], load_sem.at[index]))
            copies.append(
                remote(source(group, 1 - core), core_in.at[slot, index], core_sem, (slot, index), sibling)
            )
        return copies

    def x_copy(slot):
        return remote(x_out, x_in.at[slot], x_sem, (slot,), across)

    def y_copy(slot):
        return remote(y_out.at[aligned((1 - side) * half, half)], y_in.at[slot], y_sem, (slot,), beside)

    def z_copies(slot):
        return [
            remote(
                z_out.at[aligned((level + step) % levels * piece, piece)],
                z_in.at[slot, step - 1],
                z_sem,
                (slot, step - 1),
                floors[step - 1],
            )
            for step in range(1, levels)
        ]

    def keep_copies(target, slot):
        part = target(core, side * half + level * piece, piece)
        copies = [pltpu.make_async_copy(last, part, keep_sem)]
        for step in range(1, levels):
            copies.append(remote(last, part, zz_sem, (slot, step - 1), floors[step - 1]))
        return copies

    def yy_copy(target, slot):
        part = target(core, side * half, half)
        return remote(part, part, yy_sem, (slot,), beside)

    def cc_copy(target, slot):
        part = target(core, 0, CHUNK)
        return remote(part, part, cc_sem, (slot,), sibling)

    def stage_7(chunk, slot):
        cc_copy(any_target, slot).wait()

    def stage_6(chunk, slot):
        yy_copy(any_target, slot).wait()
        pick(chunk, lambda source, target: cc_copy(target, slot).start())

    def stage_5(chunk, slot):
        for copy in keep_copies(any_target, slot):
            copy.wait()
        pick(chunk, lambda source, target: yy_copy(target, slot).start())

    def stage_4(chunk, slot):
        for copy in z_copies(slot):
            copy.wait()
        total = wide(z_out[aligned(level * piece, piece), :])
        for step in range(1, levels):
            total = total + wide(z_in[slot, step - 1])
        last[...] = low(total)

        def send(source, target):
            for copy in keep_copies(target, slot):
                copy.start()

        pick(chunk, send)

    def stage_3(chunk, slot):
        y_copy(slot).wait()
        z_out[...] = low(wide(y_out[aligned(side * half, half), :]) + wide(y_in[slot]))
        for copy in z_copies(slot):
            copy.start()

    def stage_2(chunk, slot):
        x_copy(slot).wait()
        y_out[...] = low(held[...] + wide(x_in[slot]))
        y_copy(slot).start()

    def stage_1(chunk, slot):
        for copy in loads(any_source, slot):
            copy.wait()
        x_out[...] = low(wide(mine[0]) + wide(core_in[slot, 0]))
        x_copy(slot).start()
        held[...] = wide(mine[1]) + wide(core_in[slot, 1])

    def stage_0(chunk, slot):
        def send(source, target):
            for copy in loads(source, slot):
                copy.start()

        pick(chunk, send)

    stages = [stage_0, stage_1, stage_2, stage_3, stage_4, stage_5, stage_6, stage_7]
    for stage in reversed(range(len(stages))):
        chunk = now - stage

        @pl.when((chunk >= 0) & (chunk < chunks))
        def _(stage=stage, chunk=chunk):
            stages[stage](chunk, chunk % 2)


    @pl.when(now < 2 * pairs)
    def _():
        head = now % 2
        pair = now // 2
        lane = lax.broadcasted_iota(jnp.int32, (1, 2 * HD), 1)
        own = (lane // HD) == head
        scaled = wide(grad_ref[...]) * inv_ref[...]
        grad = jnp.where(own, scaled * relax_factor, 0.0).astype(jnp.bfloat16)
        inner = jnp.sum(wide(grad) * wide(mixed_ref[...]), axis=1, keepdims=True)
        d_probs = dot_nt(grad, v_ref[...])
        ds_ref[...] = low(wide(weight_ref[0]) * (d_probs - inner))
        dq = low(dot_nn(ds_ref[...], k_ref[...]) * query_scale)
        dk = low(dot_tn(ds_ref[...], q_ref[...]))
        dv = low(dot_tn(weight_ref[0], low(scaled)))
        for index, value in enumerate((dq, dk, dv)):
            part = pl.ds(index * 2 * HD, 2 * HD)
            dqkv_ref[:, part] = jnp.where(own | (head == 0), value, dqkv_ref[:, part])

        @pl.when(head == 1)
        def _():
            d_qkv = dqkv_ref[...]
            grads = low(dot_tn(d_qkv, first_ref[...]))
            group, start = pair // (pairs // 2), pair % (pairs // 2) * 2 * HD
            for index in range(3):
                g_qkv[group, index, aligned(start, 2 * HD), :] = grads[index * 2 * HD : (index + 1) * 2 * HD]
            columns = jnp.sum(wide(d_qkv), axis=0, keepdims=True)
            columns_of[group, 0:1, aligned(start, 2 * HD, 128)] = columns[:, : 2 * HD]
            columns_of[group, 0:1, aligned(width // 2 + start, 2 * HD, 128)] = columns[:, 4 * HD :]
            weights = jnp.concatenate([w_ref[0], w_ref[1], w_ref[2]], axis=1)
            update = dot_nt(d_qkv, weights)

            @pl.when(pair == 0)
            def _():
                d_first[...] = update

            @pl.when(pair > 0)
            def _():
                d_first[...] += update

    small_at = 2 * pairs

    @pl.when(now == small_at)
    def _():
        normed, scale = standardize(wide(tokens_ref[...]))
        errors = d_first[...]
        input_ref[...] = residual_ref[...] + norm_back(errors, normed, scale, gain_ref[...])
        small_out[0:1, :] = jnp.sum(errors * normed, axis=0, keepdims=True)
        small_out[1:4, :] = small_ref[1:4, :]
        small_out[4:5, :] = jnp.sum(errors, axis=0, keepdims=True)
        small_out[5:10, :] = small_ref[5:10, :]
        small_out[10:11, :] = columns_of[0, 0:1, :]
        small_out[11:13, :] = small_ref[11:13, :]
        small_out[13:14, :] = columns_of[1, 0:1, :]
        small_out[14:16, :] = small_ref[14:16, :]


    def small_copies(stage):
        if stage < 3:
            return [remote(small_out, small_in.at[stage], small_sem, (stage,), (sibling, across, beside)[stage])]
        return [
            remote(small_out, small_in.at[3 + level], small_sem, (2 + step,), floors[step - 1])
            for step in range(1, levels)
        ]

    @pl.when(now == small_at)
    def _():
        small_copies(0)[0].start()

    @pl.when(now == small_at + 1)
    def _():
        small_copies(0)[0].wait()
        small_out[...] += small_in[0]
        small_copies(1)[0].start()

    @pl.when(now == small_at + 2)
    def _():
        small_copies(1)[0].wait()
        small_out[0:10, :] += small_in[1, 0:10, :]
        small_out[10:13, :] += small_in[1, 13:16, :]
        small_copies(2)[0].start()

    @pl.when(now == small_at + 3)
    def _():
        small_copies(2)[0].wait()
        small_out[...] += small_in[2]
        small_in[3 + level] = small_out[...]
        for copy in small_copies(3):
            copy.start()

    @pl.when(now == small_at + 4)
    def _():
        for copy in small_copies(3):
            copy.wait()
        total = small_in[3]
        for index in range(1, levels):
            total = total + small_in[3 + index]
        sums_ref[...] = total


def back_all(queries, keys, values, mixed, grad, inv, weights, w_qkv, first, tokens, residual, gain, small, g_down, g_up, g_out, query_scale):
    length, width = queries.shape
    pairs = width // (2 * HD)
    ff = g_down.shape[0]
    levels = lax.axis_size("dp") // 4
    half, piece = CHUNK // 2, CHUNK // 2 // levels
    chunks = (ff // 4 + width // 2 * ff // 2 // width + width // 4 + 3 * width // 4) // CHUNK
    kind, sem = jnp.bfloat16, pltpu.SemaphoreType.DMA
    column = pl.BlockSpec((length, 2 * HD), lambda i: (0, jnp.minimum(i // 2, pairs - 1)))

    def whole(shape):
        return pl.BlockSpec(shape, lambda i: (0,) * len(shape), pipeline_mode=pl.Buffered(1))

    hbm = pl.BlockSpec(memory_space=pl.ANY)
    return pl.pallas_call(
        partial(back_kernel, query_scale),
        grid=(chunks + 7,),
        in_specs=[
            *[column] * 6,
            pl.BlockSpec((1, length, length), lambda i: (jnp.minimum(i, 2 * pairs - 1), 0, 0)),
            pl.BlockSpec((3, width, 2 * HD), lambda i: (0, 0, jnp.minimum(i // 2, pairs - 1))),
            whole((length, width)),
            whole((length, width)),
            whole((length, width)),
            whole((1, width)),
            whole((16, width)),
            hbm,
            hbm,
            hbm,
        ],
        out_specs=[
            whole((length, width)),
            whole((16, width)),
            hbm,
            hbm,
            hbm,
            hbm,
        ],
        out_shape=[
            jax.ShapeDtypeStruct((length, width), jnp.float32),
            jax.ShapeDtypeStruct((16, width), jnp.float32),
            jax.ShapeDtypeStruct((ff // 2, width), kind),
            jax.ShapeDtypeStruct((width, ff // 2), kind),
            jax.ShapeDtypeStruct((width // 2, width), kind),
            jax.ShapeDtypeStruct((3, width // 2, width), kind),
        ],
        scratch_shapes=[
            pltpu.VMEM((length, length), kind),
            pltpu.VMEM((length, 6 * HD), kind),
            pltpu.VMEM((length, width), jnp.float32),
            pltpu.VMEM((2, 3, width // 2, width), kind),
            pltpu.VMEM((2, 8, width), jnp.float32),
            pltpu.VMEM((16, width), jnp.float32),
            pltpu.VMEM((3 + levels, 16, width), jnp.float32),
            pltpu.VMEM((2, CHUNK, width), kind),
            pltpu.VMEM((2, 2, CHUNK, width), kind),
            pltpu.VMEM((CHUNK, width), jnp.float32),
            pltpu.VMEM((CHUNK, width), kind),
            pltpu.VMEM((2, CHUNK, width), kind),
            pltpu.VMEM((CHUNK, width), kind),
            pltpu.VMEM((2, half, width), kind),
            pltpu.VMEM((half, width), kind),
            pltpu.VMEM((2, levels - 1, piece, width), kind),
            pltpu.VMEM((piece, width), kind),
            sem((2,)),
            sem((2, 2, 2)),
            sem((2, 2)),
            sem((2, 2)),
            sem((2, 2, levels - 1)),
            sem((2, 2, levels - 1)),
            sem((2, 2)),
            sem((2, 2)),
            sem,
            sem((2, 2 + levels)),
        ],
        compiler_params=pltpu.CompilerParams(
            collective_id=0, has_side_effects=True, vmem_limit_bytes=60 * 2**20
        ),
    )(queries, keys, values, mixed, grad, inv, weights, w_qkv, first, tokens, residual, gain, small, g_down, g_up, g_out)


def sequence_shards(
    tokens,
    cond_flags,
    seg_lengths,
    norm_gains,
    norm_biases,
    w_qkv,
    qv_bias,
    w_out,
    out_biases,
    w_up,
    up_bias,
    w_down,
    cotangent,
):
    width = tokens.shape[1]
    query_scale = 1.0 / (relax_factor * math.sqrt(HD))
    (
        queries, keys, values, inv, kept, acts, slopes, small, first_in, mixed, attended, residual, third_in, result,
        d_down, all_qkv, all_out, all_up, all_down,
    ) = front(
        cond_flags, seg_lengths, tokens, cotangent, norm_gains, norm_biases, out_biases, qv_bias, up_bias,
        w_qkv, w_out, w_up, w_down, query_scale,
    )
    d_residual, d_att_low, g_down, g_up, up_sums, small = layer_back(
        attended, residual, cotangent, norm_gains, d_down, third_in, acts, slopes, all_up, all_down, small
    )
    g_out = low(dot_tn(mixed, d_att_low))
    d_mixed = low(dot_nt(d_att_low, all_out))
    up_rows = up_sums.reshape(-1, width)
    blank = jnp.zeros((1, width), jnp.float32)
    small = jnp.concatenate([small[:10], blank, up_rows[:2], blank, up_rows[2:]])
    grad_input, sums, t_down, t_up, t_out, t_qkv = back_all(
        queries, keys, values, mixed, d_mixed, inv, kept, all_qkv, first_in, tokens, d_residual,
        norm_gains[:1], small, g_down, g_up, g_out, query_scale,
    )
    return (
        result,
        grad_input,
        sums[:4],
        sums[4:8],
        t_qkv.astype(jnp.float32).transpose(0, 2, 1),
        sums[10].reshape(2, -1),
        t_out.astype(jnp.float32),
        sums[8:10],
        t_up.astype(jnp.float32),
        sums[11:13].reshape(-1),
        t_down.astype(jnp.float32),
    )


def solution(mesh):
    in_specs = (
        P(("dp", "mp"), None),
        P("dp", None),
        P("dp", None),
        P(),
        P(),
        P(None, None, "mp"),
        P(None, "mp"),
        P("mp", None),
        P(),
        P(None, "mp"),
        P("mp"),
        P("mp", None),
        P(("dp", "mp"), None),
    )
    out_specs = (
        P(("dp", "mp"), None),
        P(("dp", "mp"), None),
        P(),
        P(),
        P(None, None, "mp"),
        P(None, "mp"),
        P("mp", None),
        P(),
        P(None, "mp"),
        P("mp"),
        P("mp", None),
    )
    per_device = mesh.shape["dp"] * mesh.shape["mp"]

    def step(*args):
        whole_sequences = args[1].shape[0] == per_device
        local = sequence_shards if whole_sequences and mesh.shape["mp"] == 2 and mesh.shape["dp"] == 16 else shards
        return jax.shard_map(
            local, mesh=mesh, in_specs=in_specs, out_specs=out_specs, check_vma=False
        )(*args)

    return step
```

```python
from functools import partial
import math

import jax
import jax.numpy as jnp
from jax import lax
from jax.experimental import pallas as pl
from jax.experimental.pallas import tpu as pltpu
from jax.sharding import PartitionSpec as P

HD = 64


epsilon = 1e-05
relax_factor = 32.0


def standardize(entries):
    average = jnp.mean(entries, axis=-1, keepdims=True)
    centred = entries - average
    spread = jnp.mean(centred * centred, axis=-1, keepdims=True)
    inv_std = lax.rsqrt(spread + epsilon)
    return (centred * inv_std, inv_std)


def norm_back(grad_in, normed, inv_std, gain_row):
    weighted = grad_in * gain_row
    return inv_std * (
        weighted
        - jnp.mean(weighted, axis=-1, keepdims=True)
        - normed * jnp.mean(weighted * normed, axis=-1, keepdims=True)
    )


def token_marks(seg_flags, lengths, length):
    position = jnp.arange(length, dtype=jnp.int32)
    segment = (position >= lengths[0]).astype(jnp.int32) + (
        position >= lengths[0] + lengths[1]
    ).astype(jnp.int32)
    segment_hits = (segment[:, None] == jnp.arange(3, dtype=jnp.int32)[None, :]).astype(jnp.int32)
    return jnp.sum(segment_hits * seg_flags[None, :], axis=1)


def block_mask(marks_seq, first_row, block_rows, length):
    query_places = first_row + jnp.arange(block_rows, dtype=jnp.int32)
    key_places = jnp.arange(length, dtype=jnp.int32)
    return (key_places[None, :] <= query_places[:, None]) | (marks_seq[None, :] == 1)


def shards(
    tokens,
    cond_flags,
    seg_lengths,
    norm_gains,
    norm_biases,
    w_qkv,
    qv_bias,
    w_out,
    out_biases,
    w_up,
    up_bias,
    w_down,
    cotangent,
):
    shard_rows = tokens.shape[0]
    group_rows = shard_rows * lax.axis_size("mp")
    seq_count = cond_flags.shape[0]
    length = group_rows // seq_count
    block_rows = length // 2
    head_count = w_qkv.shape[2] // HD
    local_width = head_count * HD
    query_scale = 1.0 / (relax_factor * math.sqrt(HD))
    all_marks = jax.vmap(lambda seg_flags, lengths: token_marks(seg_flags, lengths, length))(
        cond_flags, seg_lengths
    )
    numbers = jnp.arange(seq_count * 2, dtype=jnp.int32)
    source = tokens.astype(jnp.float32)
    normed_one, scale_one = standardize(source)
    first_in = (normed_one * norm_gains[0] + norm_biases[0]).astype(jnp.bfloat16)
    first_all = lax.all_gather(first_in, "mp", axis=0, tiled=True)
    bias_rows = jnp.stack([qv_bias[0], jnp.zeros_like(qv_bias[0]), qv_bias[1]])
    projected = (
        jnp.einsum("td,cde->cte", first_all, w_qkv, preferred_element_type=jnp.float32)
        + bias_rows[:, None, :]
    )
    queries = (
        (projected[0] * query_scale)
        .astype(jnp.bfloat16)
        .reshape(seq_count * 2, block_rows, head_count, HD)
    )
    key_all = projected[1].astype(jnp.bfloat16).reshape(seq_count, length, head_count, HD)
    value_all = projected[2].astype(jnp.bfloat16).reshape(seq_count, length, head_count, HD)

    def block_probs(query_block, number, row_top, row_total):
        sequence = number // 2
        first_row = number % 2 * block_rows
        key_seq = lax.dynamic_index_in_dim(key_all, sequence, 0, keepdims=False)
        allowed = block_mask(
            lax.dynamic_index_in_dim(all_marks, sequence, 0, keepdims=False),
            first_row,
            block_rows,
            length,
        )
        scores = jnp.einsum(
            "qhd,khd->hqk", query_block, key_seq, preferred_element_type=jnp.float32
        )
        if row_top is None:
            row_top = jnp.max(jnp.where(allowed[None], scores, -1e30), axis=-1, keepdims=True)
        weights = jnp.exp(jnp.where(allowed[None], (scores - row_top) * relax_factor, -30000.0))
        if row_total is None:
            row_total = jnp.sum(weights, axis=-1, keepdims=True)
        return (weights / row_total, row_top, row_total, key_seq)

    def forward_block(block_item):
        query_block, number = block_item
        probs, row_top, row_total, key_seq = block_probs(query_block, number, None, None)
        value_seq = lax.dynamic_index_in_dim(value_all, number // 2, 0, keepdims=False)
        mixed_block = jnp.einsum(
            "hqk,khd->qhd",
            probs.astype(jnp.bfloat16),
            value_seq,
            preferred_element_type=jnp.float32,
        )
        return (mixed_block.astype(jnp.bfloat16), row_top, row_total)

    mixed_heads, row_tops, row_totals = lax.map(forward_block, (queries, numbers))
    mixed_heads = mixed_heads.reshape(group_rows, local_width)
    attended = (
        lax.psum_scatter(
            jnp.dot(mixed_heads, w_out, preferred_element_type=jnp.float32),
            "mp",
            scatter_dimension=0,
            tiled=True,
        )
        + out_biases[0]
    )
    normed_two, scale_two = standardize(attended)
    residual = source + normed_two * norm_gains[1] + norm_biases[1]
    normed_three, scale_three = standardize(residual)
    third_in = (normed_three * norm_gains[2] + norm_biases[2]).astype(jnp.bfloat16)
    third_all = lax.all_gather(third_in, "mp", axis=0, tiled=True)
    up_value = jnp.dot(third_all, w_up, preferred_element_type=jnp.float32) + up_bias
    activated = jax.nn.gelu(up_value, approximate=True).astype(jnp.bfloat16)
    down = (
        lax.psum_scatter(
            jnp.dot(activated, w_down, preferred_element_type=jnp.float32),
            "mp",
            scatter_dimension=0,
            tiled=True,
        )
        + out_biases[1]
    )
    normed_four, scale_four = standardize(down)
    result = (residual + normed_four * norm_gains[3] + norm_biases[3]).astype(jnp.bfloat16)
    grad_out = cotangent.astype(jnp.float32)
    d_down = norm_back(grad_out, normed_four, scale_four, norm_gains[3])
    d_down_low = d_down.astype(jnp.bfloat16)
    d_down_all = lax.all_gather(d_down_low, "mp", axis=0, tiled=True)
    d_act = jnp.einsum("td,fd->tf", d_down_all, w_down, preferred_element_type=jnp.float32)
    grad_w_down = jnp.einsum("tf,td->fd", activated, d_down_all, preferred_element_type=jnp.float32)
    gelu_value, gelu_pull = jax.vjp(partial(jax.nn.gelu, approximate=True), up_value)
    d_up = gelu_pull(d_act)[0].astype(jnp.bfloat16)
    grad_w_up = jnp.einsum("td,tf->df", third_all, d_up, preferred_element_type=jnp.float32)
    grad_up_bias = jnp.sum(d_up, axis=0, dtype=jnp.float32)
    d_third = lax.psum_scatter(
        jnp.einsum("tf,df->td", d_up, w_up, preferred_element_type=jnp.float32),
        "mp",
        scatter_dimension=0,
        tiled=True,
    )
    d_residual = grad_out + norm_back(d_third, normed_three, scale_three, norm_gains[2])
    d_attended = norm_back(d_residual, normed_two, scale_two, norm_gains[1])
    d_att_low = d_attended.astype(jnp.bfloat16)
    d_att_all = lax.all_gather(d_att_low, "mp", axis=0, tiled=True)
    d_mixed = jnp.einsum("td,hd->th", d_att_all, w_out, preferred_element_type=jnp.float32).astype(
        jnp.bfloat16
    )
    grad_w_out = jnp.einsum("th,td->hd", mixed_heads, d_att_all, preferred_element_type=jnp.float32)
    d_mixed_blocks = d_mixed.reshape(seq_count * 2, block_rows, head_count, HD)

    def backward_block(block_item):
        query_block, d_block, row_top, row_total, number = block_item
        probs, kept_top, kept_total, key_seq = block_probs(query_block, number, row_top, row_total)
        value_seq = lax.dynamic_index_in_dim(value_all, number // 2, 0, keepdims=False)
        d_probs = jnp.einsum("qhd,khd->hqk", d_block, value_seq, preferred_element_type=jnp.float32)
        inner = jnp.sum(probs * d_probs, axis=-1, keepdims=True)
        d_scores = (relax_factor * probs * (d_probs - inner)).astype(jnp.bfloat16)
        d_query = (
            jnp.einsum("hqk,khd->qhd", d_scores, key_seq, preferred_element_type=jnp.float32)
            * query_scale
        )
        d_key = jnp.einsum(
            "hqk,qhd->khd", d_scores, query_block, preferred_element_type=jnp.float32
        )
        d_value = jnp.einsum(
            "hqk,qhd->khd", probs.astype(jnp.bfloat16), d_block, preferred_element_type=jnp.float32
        )
        return (d_query.astype(jnp.bfloat16), d_key, d_value)

    d_queries, d_keys, d_values = lax.map(
        backward_block, (queries, d_mixed_blocks, row_tops, row_totals, numbers)
    )
    d_keys = jnp.sum(d_keys.reshape(seq_count, 2, length, local_width), axis=1).reshape(
        group_rows, local_width
    )
    d_values = jnp.sum(d_values.reshape(seq_count, 2, length, local_width), axis=1).reshape(
        group_rows, local_width
    )
    d_qkv = jnp.stack(
        [
            d_queries.reshape(group_rows, local_width),
            d_keys.astype(jnp.bfloat16),
            d_values.astype(jnp.bfloat16),
        ]
    )
    grad_w_qkv = jnp.einsum("td,cte->cde", first_all, d_qkv, preferred_element_type=jnp.float32)
    grad_qv_bias = jnp.stack(
        [jnp.sum(d_qkv[0], axis=0, dtype=jnp.float32), jnp.sum(d_qkv[2], axis=0, dtype=jnp.float32)]
    )
    d_first = lax.psum_scatter(
        jnp.einsum("cte,cde->td", d_qkv, w_qkv, preferred_element_type=jnp.float32).astype(
            jnp.bfloat16
        ),
        "mp",
        scatter_dimension=0,
        tiled=True,
    ).astype(jnp.float32)
    grad_input = d_residual + norm_back(d_first, normed_one, scale_one, norm_gains[0])
    error_terms = (d_first, d_residual, d_third, grad_out)
    normed_terms = (normed_one, normed_two, normed_three, normed_four)
    gain_sums = jnp.stack(
        [
            jnp.sum(error_term * normed_term, axis=0)
            for error_term, normed_term in zip(error_terms, normed_terms)
        ]
    )
    bias_sums = jnp.stack([jnp.sum(error_term, axis=0) for error_term in error_terms])
    outer_sums = jnp.stack([jnp.sum(d_attended, axis=0), jnp.sum(d_down, axis=0)])
    gain_sums, bias_sums, outer_sums = lax.psum((gain_sums, bias_sums, outer_sums), ("dp", "mp"))
    grad_w_qkv, grad_qv_bias, grad_w_out, grad_w_up, grad_up_bias, grad_w_down = (
        lax.psum(grad_w_qkv.astype(jnp.bfloat16), "dp").astype(jnp.float32),
        lax.psum(grad_qv_bias.astype(jnp.bfloat16), "dp").astype(jnp.float32),
        lax.psum(grad_w_out.astype(jnp.bfloat16), "dp").astype(jnp.float32),
        lax.psum(grad_w_up.astype(jnp.bfloat16), "dp").astype(jnp.float32),
        lax.psum(grad_up_bias.astype(jnp.bfloat16), "dp").astype(jnp.float32),
        lax.psum(grad_w_down.astype(jnp.bfloat16), "dp").astype(jnp.float32),
    )
    return (
        result,
        grad_input,
        gain_sums,
        bias_sums,
        grad_w_qkv,
        grad_qv_bias,
        grad_w_out,
        outer_sums,
        grad_w_up,
        grad_up_bias,
        grad_w_down,
    )


LOG2E = 1.4426950408889634
HIDDEN = -1e30


def dot_nt(a, b):
    return lax.dot_general(a, b, (((1,), (1,)), ((), ())), preferred_element_type=jnp.float32)


def dot_nn(a, b):
    return lax.dot_general(a, b, (((1,), (0,)), ((), ())), preferred_element_type=jnp.float32)


def dot_tn(a, b):
    return lax.dot_general(a, b, (((0,), (0,)), ((), ())), preferred_element_type=jnp.float32)


def low(value):
    return value.astype(jnp.bfloat16)


MESH = pl.DeviceIdType.MESH
CHUNK = 128


def remote(source, target, sems, index, device):
    return pltpu.make_async_remote_copy(
        src_ref=source,
        dst_ref=target,
        send_sem=sems.at[(0, *index)],
        recv_sem=sems.at[(1, *index)],
        device_id=device,
        device_id_type=MESH,
    )


def aligned(start, size, unit=16):
    return pl.ds(pl.multiple_of(start, unit), size)


def wide(value):
    return value.astype(jnp.float32)


GELU_SCALE = math.sqrt(2.0 / math.pi)
GELU_CUBE = 0.044715


def gelu_both(up):
    square = up * up
    half = 0.5 * jnp.tanh(up * (GELU_SCALE + GELU_SCALE * GELU_CUBE * square)) + 0.5
    value = up * half
    slope = half + value * (1.0 - half) * (2.0 * GELU_SCALE + 6.0 * GELU_SCALE * GELU_CUBE * square)
    return value, slope


def column_sum(value):
    return jnp.sum(value, axis=0, keepdims=True)


def front_kernel(
    query_scale,
    events,
    flags_ref,
    lengths_ref,
    gain_ref,
    shift_ref,
    out_bias_ref,
    qv_bias_ref,
    up_bias_ref,
    tokens_in,
    cot_in,
    own_qkv,
    own_out,
    own_up,
    own_down,
    q_ref,
    k_ref,
    v_ref,
    inv_ref,
    weight_ref,
    act_ref,
    slope_ref,
    small_ref,
    first_out,
    mixed_out,
    att_out,
    residual_out,
    third_out,
    result_out,
    d_down_out,
    all_qkv,
    all_out,
    all_up,
    all_down,
    first_ref,
    mixed_ref,
    tokens_ref,
    third_ref,
    att_ref,
    residual_ref,
    total,
    qkv_buf,
    out_buf,
    up_buf,
    down_buf,
    hide_ref,
    qv_all,
    up_bias_all,
    qkv_load,
    out_load,
    up_load,
    down_load,
    qkv_keep,
    out_keep,
    up_keep,
    down_keep,
    bias_sem,
    x_sem,
    y_sem,
    c_sem,
    in_sem,
    save_sem,
    end_sem,
):
    now = pl.program_id(0)
    place = lax.axis_index("dp")
    turn = lax.axis_index("mp")
    core, side = place % 2, (place // 2) % 2
    sibling = {"dp": place + 1 - 2 * core}
    across = {"mp": 1 - turn}
    beside = {"dp": place + 2 - 4 * side}
    length, width = tokens_ref.shape
    pairs = width // (2 * HD)
    size = act_ref.shape[1]
    ff = all_up.shape[1]
    chunks = ff // size
    mid = pairs
    end = mid + chunks + 1
    parts = 5
    step = length // parts
    blocks = [pl.ds(start, step) for start in range(0, length, step)]

    def gain(index):
        return gain_ref[index : index + 1, :]

    def shift(index):
        return shift_ref[index : index + 1, :]


    q_qkv, q_out, q_up, q_down = width // 8, width // 8, ff // 8, ff // 8
    row_up = width // 4

    def places(index, quarter, count):
        if index < 3:
            cols = aligned(quarter * q_qkv, count * q_qkv, 128)
            far = aligned(width // 2 + quarter * q_qkv, count * q_qkv, 128)
            return own_qkv.at[index, :, cols], all_qkv.at[index, :, far]
        if index < 4:
            rows = aligned(quarter * q_out, count * q_out)
            return own_out.at[rows, :], all_out.at[aligned(width // 2 + quarter * q_out, count * q_out), :]
        if index < 8:
            rows = pl.ds((index - 4) * row_up, row_up)
            cols = aligned(quarter * q_up, count * q_up, 128)
            return own_up.at[rows, cols], all_up.at[rows, aligned(ff // 2 + quarter * q_up, count * q_up, 128)]
        cols = pl.ds((index - 8) * (width // 4), width // 4)
        rows = aligned(quarter * q_down, count * q_down)
        return own_down.at[rows, cols], all_down.at[aligned(ff // 2 + quarter * q_down, count * q_down), cols]

    def hop(index, stage):
        if stage == 0:
            source, target = places(index, 2 * core + side, 1)
            return remote(source, target, x_sem, (index,), across)
        if stage == 1:
            part = places(index, 2 * core + side, 1)[1]
            return remote(part, part, y_sem, (index,), beside)
        part = places(index, 2 * core, 2)[1]
        return remote(part, part, c_sem, (index,), sibling)

    bias_copies = [
        remote(qv_bias_ref, qv_all.at[1], bias_sem, (0,), across),
        remote(up_bias_ref, up_bias_all.at[1], bias_sem, (1,), across),
    ]
    def load_pair(pair, ref):
        start = pair % (pairs // 2) * 2 * HD if ref is own_qkv else pair * 2 * HD
        return pltpu.make_async_copy(
            ref.at[:, :, aligned(start, 2 * HD, 128)], qkv_buf.at[pair % 2], qkv_load.at[pair % 2]
        )

    def load_chunk(chunk, up, down):
        slot = chunk % 2
        return [
            pltpu.make_async_copy(up.at[:, aligned(chunk * size, size, 128)], up_buf.at[slot], up_load.at[slot]),
            pltpu.make_async_copy(down.at[aligned(chunk * size, size), :], down_buf.at[slot], down_load.at[slot]),
        ]

    out_loads = [
        pltpu.make_async_copy(
            own_out, out_buf.at[pl.ds(0, width // 2), :], out_load.at[0]
        ),
        pltpu.make_async_copy(
            all_out.at[pl.ds(width // 2, width // 2), :], out_buf.at[pl.ds(width // 2, width // 2), :], out_load.at[1]
        ),
    ]

    def keep_pair(pair):
        return pltpu.make_async_copy(
            qkv_buf.at[pair % 2], all_qkv.at[:, :, aligned(pair * 2 * HD, 2 * HD, 128)], qkv_keep.at[pair % 2]
        )

    def keep_chunk(chunk):
        slot = chunk % 2
        return [
            pltpu.make_async_copy(up_buf.at[slot], all_up.at[:, aligned(chunk * size, size, 128)], up_keep.at[slot]),
            pltpu.make_async_copy(down_buf.at[slot], all_down.at[aligned(chunk * size, size), :], down_keep.at[slot]),
        ]

    keep_out = pltpu.make_async_copy(
        out_buf.at[pl.ds(0, width // 2), :], all_out.at[pl.ds(0, width // 2), :], out_keep
    )
    take_tokens = pltpu.make_async_copy(tokens_in, tokens_ref, in_sem.at[0])
    take_cot = pltpu.make_async_copy(cot_in, first_ref, in_sem.at[1])
    save_first = pltpu.make_async_copy(first_ref, first_out, save_sem.at[0])
    saves = [
        pltpu.make_async_copy(mixed_ref, mixed_out, save_sem.at[1]),
        pltpu.make_async_copy(att_ref, att_out, save_sem.at[2]),
        pltpu.make_async_copy(residual_ref, residual_out, save_sem.at[3]),
        pltpu.make_async_copy(third_ref, third_out, save_sem.at[4]),
    ]

    def end_copies(index):
        part = blocks[index]
        return [
            pltpu.make_async_copy(tokens_ref.at[part, :], result_out.at[part, :], end_sem.at[0, index]),
            pltpu.make_async_copy(mixed_ref.at[part, :], d_down_out.at[part, :], end_sem.at[1, index]),
        ]

    def run_events(slot):
        for index, stage in events.get(slot, []):
            if stage > 0:
                hop(index, stage - 1).wait()
            if stage < 3:
                hop(index, stage).start()

    @pl.when(now == 0)
    def _():
        take_tokens.start()
        load_pair(0, own_qkv).start()
        barrier = pltpu.get_barrier_semaphore()
        partners = [sibling, across, beside]
        for partner in partners:
            pl.semaphore_signal(barrier, inc=1, device_id=partner, device_id_type=MESH)
        pl.semaphore_wait(barrier, len(partners))
        for copy in bias_copies:
            copy.start()

    for moment in range(end):

        @pl.when(now == moment)
        def _(moment=moment):
            run_events(2 * moment if moment < mid else moment + mid)

    @pl.when(now == 0)
    def _():
        qv_all[0] = qv_bias_ref[...]
        up_bias_all[0] = up_bias_ref[...]
        spots = lax.broadcasted_iota(jnp.int32, (1, length), 1)
        one = lengths_ref[turn, 0]
        two = one + lengths_ref[turn, 1]
        marks = jnp.where(
            spots < one, flags_ref[turn, 0], jnp.where(spots < two, flags_ref[turn, 1], flags_ref[turn, 2])
        )
        hide_ref[...] = jnp.where(marks == 1, 0.0, HIDDEN)
        take_tokens.wait()
        for part in blocks:
            normed, _ = standardize(wide(tokens_ref[part, :]))
            first_ref[part, :] = low(normed * gain(0) + shift(0))
        save_first.start()

    @pl.when(now == pairs // 2)
    def _():
        bias_copies[0].wait()

    @pl.when(now == mid)
    def _():
        bias_copies[1].wait()


    def attend_head(head):
        lane = lax.broadcasted_iota(jnp.int32, (1, 2 * HD), 1)
        own = (lane // HD) == head
        keys = k_ref[...]
        values = jnp.where(own, v_ref[...], jnp.ones((1, 2 * HD), jnp.bfloat16))
        rows = length // 2
        spot = aligned(now * 2 * HD, 2 * HD, 128)
        for start in (0, rows):
            part = pl.ds(start, rows)
            mine = jnp.where(own, q_ref[part, :], jnp.zeros((1, 2 * HD), jnp.bfloat16))
            scores = dot_nt(mine, keys)
            query_places = lax.broadcasted_iota(jnp.int32, (rows, length), 0) + start
            key_places = lax.broadcasted_iota(jnp.int32, (rows, length), 1)
            scores = scores + jnp.where(key_places <= query_places, 0.0, hide_ref[...])
            top = jnp.max(scores, axis=1, keepdims=True)
            kept = low(jnp.exp2((scores - top) * (relax_factor * LOG2E)))
            weight_ref[head, part, :] = kept
            mixed = dot_nn(kept, values)
            inv = 1.0 / pltpu.roll(mixed, HD, 1)
            out = low(mixed * inv)
            mixed_ref[part, spot] = out if head == 0 else jnp.where(own, out, mixed_ref[part, spot])
            inv_ref[part, :] = inv if head == 0 else jnp.where(own, inv, inv_ref[part, :])

    @pl.when(now < mid)
    def _():
        pair = now
        load_pair(pair, all_qkv).wait()
        group, start = pair // (pairs // 2), pair % (pairs // 2) * 2 * HD
        parts_of = qkv_buf[pair % 2]
        projected = dot_nn(first_ref[...], jnp.concatenate([parts_of[0], parts_of[1], parts_of[2]], axis=1))
        bias_q = qv_all[group, 0:1, aligned(start, 2 * HD, 128)]
        bias_v = qv_all[group, 1:2, aligned(start, 2 * HD, 128)]
        q_ref[...] = low((projected[:, : 2 * HD] + bias_q) * query_scale)
        k_ref[...] = low(projected[:, 2 * HD : 4 * HD])
        v_ref[...] = low(projected[:, 4 * HD :] + bias_v)

    @pl.when(now < pairs // 2)
    def _():
        keep_pair(now).start()

    @pl.when(now < mid)
    def _():
        attend_head(0)

    for moment in range(mid):

        @pl.when(now == moment)
        def _(moment=moment):
            run_events(2 * moment + 1)

    @pl.when(now < mid)
    def _():
        attend_head(1)

    @pl.when((now >= 1) & (now <= pairs // 2))
    def _():
        keep_pair(now - 1).wait()

    @pl.when(now < pairs // 2 - 1)
    def _():
        load_pair(now + 1, own_qkv).start()

    @pl.when((now >= pairs // 2 - 1) & (now < mid - 1))
    def _():
        load_pair(now + 1, all_qkv).start()

    @pl.when(now == mid - 1)
    def _():
        for copy in out_loads:
            copy.start()

    @pl.when(now == mid)
    def _():
        for copy in load_chunk(0, own_up, own_down):
            copy.start()
        save_first.wait()
        take_cot.start()
        for copy in out_loads:
            copy.wait()
        keep_out.start()
        for part in blocks:
            attended = dot_nn(mixed_ref[part, :], out_buf[...]) + out_bias_ref[0:1, :]
            att_ref[part, :] = attended
            normed_two, _ = standardize(attended)
            residual = wide(tokens_ref[part, :]) + normed_two * gain(1) + shift(1)
            residual_ref[part, :] = residual
            normed_three, _ = standardize(residual)
            third_ref[part, :] = low(normed_three * gain(2) + shift(2))
            total[part, :] = jnp.broadcast_to(out_bias_ref[1:2, :], (step, width))
        for copy in saves:
            copy.start()

    @pl.when((now > mid) & (now < end))
    def _():
        for copy in load_chunk(now - mid - 1, all_up, all_down):
            copy.wait()

    @pl.when((now > mid + 1) & (now <= mid + 1 + chunks // 2))
    def _():
        for copy in keep_chunk(now - mid - 2):
            copy.wait()

    @pl.when((now > mid) & (now < mid + chunks // 2))
    def _():
        for copy in load_chunk(now - mid, own_up, own_down):
            copy.start()

    @pl.when((now >= mid + chunks // 2) & (now < end - 1))
    def _():
        for copy in load_chunk(now - mid, all_up, all_down):
            copy.start()

    @pl.when((now > mid) & (now <= mid + chunks // 2))
    def _():
        for copy in keep_chunk(now - mid - 1):
            copy.start()

    @pl.when((now > mid) & (now < end))
    def _():
        chunk = now - mid - 1
        slot = chunk % 2
        group, start = chunk // (chunks // 2), chunk % (chunks // 2) * size
        bias = up_bias_all[group, 0:1, aligned(start, size, 128)]
        for part in (pl.ds(0, length // 2), pl.ds(length // 2, length // 2)):
            up = dot_nn(third_ref[part, :], up_buf[slot]) + bias
            value, slope = gelu_both(up)
            act = low(value)
            act_ref[part, :] = act
            slope_ref[part, :] = low(slope)
            total[part, :] += dot_nn(act, down_buf[slot])

    @pl.when(now == end)
    def _():
        take_cot.wait()
        keep_out.wait()
        for copy in saves:
            copy.wait()
        sums = [0.0, 0.0, 0.0]
        for index, part in enumerate(blocks):
            normed_four, scale_four = standardize(total[part, :])
            tokens_ref[part, :] = low(residual_ref[part, :] + normed_four * gain(3) + shift(3))
            grad_out = wide(first_ref[part, :])
            d_down = norm_back(grad_out, normed_four, scale_four, gain(3))
            mixed_ref[part, :] = low(d_down)
            for copy in end_copies(index):
                copy.start()
            terms = [grad_out * normed_four, grad_out, d_down]
            sums = [old + column_sum(term) for old, term in zip(sums, terms)]
        small_ref[...] = jnp.zeros_like(small_ref)
        small_ref[3:4, :] = sums[0]
        small_ref[7:8, :] = sums[1]
        small_ref[9:10, :] = sums[2]
        for index in range(parts):
            for copy in end_copies(index):
                copy.wait()


def front_events():
    starts = [0, 0, 1, 3, 4, 5, 7, 8, 10, 11, 13, 15]
    plan = {}
    for index, start in enumerate(starts):
        for stage, moment in enumerate((start, start + 2, start + 4, start + 5)):
            plan.setdefault(moment, []).append((index, stage))
    return {moment: sorted(items, key=lambda item: -item[1]) for moment, items in plan.items()}


def front(flags, lengths, tokens, cotangent, gains, shifts, out_biases, qv_bias, up_bias, w_qkv, w_out, w_up, w_down, query_scale):
    length, width = tokens.shape
    pairs = width // (2 * HD)
    ff = 2 * w_up.shape[1]
    size = 512
    chunks = ff // size
    kind, sem = jnp.bfloat16, pltpu.SemaphoreType.DMA

    def whole(shape):
        return pl.BlockSpec(shape, lambda i: (0,) * len(shape), pipeline_mode=pl.Buffered(1))

    hbm = pl.BlockSpec(memory_space=pl.ANY)
    smem = pl.BlockSpec(memory_space=pltpu.SMEM)
    column = pl.BlockSpec((length, 2 * HD), lambda i: (0, jnp.minimum(i, pairs - 1)))
    piece = pl.BlockSpec((length, size), lambda i: (0, jnp.clip(i - pairs - 1, 0, chunks - 1)))

    def low_like(*shape):
        return jax.ShapeDtypeStruct(shape, kind)

    def wide_like(*shape):
        return jax.ShapeDtypeStruct(shape, jnp.float32)

    return pl.pallas_call(
        partial(front_kernel, query_scale, front_events()),
        grid=(pairs + chunks + 2,),
        in_specs=[
            smem,
            smem,
            whole((4, width)),
            whole((4, width)),
            whole((2, width)),
            whole(qv_bias.shape),
            whole((1, ff // 2)),
            *[hbm] * 6,
        ],
        out_specs=[
            column,
            column,
            column,
            column,
            pl.BlockSpec((2, length, length), lambda i: (jnp.minimum(i, pairs - 1), 0, 0)),
            piece,
            piece,
            whole((16, width)),
            *[hbm] * 11,
        ],
        out_shape=[
            low_like(length, width),
            low_like(length, width),
            low_like(length, width),
            wide_like(length, width),
            low_like(2 * pairs, length, length),
            low_like(length, ff),
            low_like(length, ff),
            wide_like(16, width),
            low_like(length, width),
            low_like(length, width),
            wide_like(length, width),
            wide_like(length, width),
            low_like(length, width),
            low_like(length, width),
            low_like(length, width),
            low_like(3, width, width),
            low_like(width, width),
            low_like(width, ff),
            low_like(ff, width),
        ],
        scratch_shapes=[
            *[pltpu.VMEM((length, width), kind)] * 4,
            *[pltpu.VMEM((length, width), jnp.float32)] * 3,
            pltpu.VMEM((2, 3, width, 2 * HD), kind),
            pltpu.VMEM((width, width), kind),
            pltpu.VMEM((2, width, size), kind),
            pltpu.VMEM((2, size, width), kind),
            pltpu.VMEM((1, length), jnp.float32),
            pltpu.VMEM((2, *qv_bias.shape), jnp.float32),
            pltpu.VMEM((2, 1, ff // 2), jnp.float32),
            sem((2,)),
            sem((2,)),
            sem((2,)),
            sem((2,)),
            sem((2,)),
            sem,
            sem((2,)),
            sem((2,)),
            sem((2, 2)),
            sem((2, 12)),
            sem((2, 12)),
            sem((2, 12)),
            sem((2,)),
            sem((5,)),
            sem((2, 5)),
        ],
        compiler_params=pltpu.CompilerParams(
            collective_id=1, has_side_effects=True, vmem_limit_bytes=63 * 2**20
        ),
    )(
        flags, lengths, gains, shifts, out_biases, qv_bias, up_bias.reshape(1, -1), tokens, cotangent,
        w_qkv, w_out, w_up, w_down,
    )


STAGE_STEPS = (0, 1, 3, 5, 7, 9, 11, 12)


def braid(own, other, axis):
    cut = partial(lax.slice_in_dim, axis=axis)
    return jnp.concatenate(
        [cut(own, 0, CHUNK), cut(other, 0, CHUNK), cut(own, CHUNK, 2 * CHUNK), cut(other, CHUNK, 2 * CHUNK)], axis=axis
    )


def rear_kernel(
    query_scale,
    act_own,
    act_other,
    slope_own,
    slope_other,
    up_own,
    up_other,
    down_own,
    down_other,
    q_ref,
    k_ref,
    v_ref,
    inv_ref,
    weight_ref,
    w_ref,
    gain_ref,
    front_sums,
    third_in,
    d_down_in,
    cot_in,
    mixed_in,
    first_in,
    tokens_in,
    att_in,
    residual_in,
    w_out_in,
    sums_ref,
    input_out,
    whole,
    grads,
    third_ref,
    d_down_ref,
    cot_ref,
    mixed_ref,
    att_ref,
    residual_ref,
    total,
    out_buf,
    d_up_ref,
    stage_down,
    stage_up,
    ds_ref,
    dqkv_ref,
    up_sums,
    columns_of,
    small_out,
    small_in,
    mine,
    core_in,
    held,
    x_out,
    x_in,
    y_out,
    y_in,
    z_out,
    z_in,
    last,
    take_sem,
    att_sem,
    stage_sem,
    out_sem,
    head_sem,
    end_sem,
    load_sem,
    core_sem,
    x_sem,
    y_sem,
    z_sem,
    zz_sem,
    yy_sem,
    cc_sem,
    keep_sem,
    small_sem,
):
    now = pl.program_id(0)
    place = lax.axis_index("dp")
    turn = lax.axis_index("mp")
    core, side, level = place % 2, (place // 2) % 2, place // 4
    levels = lax.axis_size("dp") // 4
    sibling = {"dp": place + 1 - 2 * core}
    across = {"mp": 1 - turn}
    beside = {"dp": place + 2 - 4 * side}
    floors = [{"dp": (level + step) % levels * 4 + place % 4} for step in range(1, levels)]
    half, piece = CHUNK // 2, CHUNK // 2 // levels
    length, width = total.shape
    pairs = width // (2 * HD)
    units = d_up_ref.shape[1] // 2
    ffs = up_sums.shape[2] // units
    outs = width // 2 // (2 * CHUNK)
    s_mid, s_att = ffs, ffs + 2
    small_at = s_att + 2 * pairs
    first_head = 2 * ffs + outs
    early = first_head + 3
    gap = small_at - 1 - early
    parts = 5
    step = length // parts
    blocks = [pl.ds(start, step) for start in range(0, length, step)]

    def gain(index):
        return gain_ref[index : index + 1, :]

    takes = [
        pltpu.make_async_copy(source, target, take_sem.at[index])
        for index, (source, target) in enumerate(
            (
                (third_in, third_ref),
                (d_down_in, d_down_ref),
                (cot_in, cot_ref),
                (mixed_in, mixed_ref),
                (residual_in, residual_ref),
                (w_out_in, out_buf),
                (first_in, cot_ref),
                (tokens_in, d_down_ref),
            )
        )
    ]

    def take_att(index):
        return pltpu.make_async_copy(att_in.at[blocks[index], :], att_ref.at[index % 2], att_sem.at[index % 2])

    def save_down(chunk):
        return pltpu.make_async_copy(stage_down, grads.at[2 * chunk], stage_sem.at[0])

    def save_up(chunk):
        return pltpu.make_async_copy(stage_up, grads.at[2 * chunk + 1], stage_sem.at[1])

    out_saves = [
        pltpu.make_async_copy(
            out_buf.at[pl.ds(group * width // 2 + (index * 2 + which) * CHUNK, CHUNK), :],
            grads.at[2 * ffs + index, pl.ds((2 * which + group) * CHUNK, CHUNK), :],
            out_sem.at[group, index, which],
        )
        for group in range(2)
        for index in range(outs)
        for which in range(2)
    ]

    def head_saves(turn_of):
        return [
            pltpu.make_async_copy(
                stage_down.at[pl.ds(kind * CHUNK, CHUNK), :],
                grads.at[first_head + turn_of // 4 * 3 + kind, aligned(turn_of % 4 * CHUNK, CHUNK), :],
                head_sem.at[kind],
            )
            for kind in range(3)
        ]

    save_input = pltpu.make_async_copy(residual_ref, input_out, end_sem)

    @pl.when(now == 0)
    def _():
        for copy in takes[:2]:
            copy.start()
        barrier = pltpu.get_barrier_semaphore()
        partners = [sibling, across, beside, *floors]
        for partner in partners:
            pl.semaphore_signal(barrier, inc=1, device_id=partner, device_id_type=MESH)
        pl.semaphore_wait(barrier, len(partners))
        takes[0].wait()
        takes[1].wait()
        for copy in takes[2:6]:
            copy.start()
        take_att(0).start()
        take_att(1).start()

    @pl.when((now >= 1) & (now <= ffs))
    def _():
        save_down(now - 1).wait()

    @pl.when((now >= s_att + 2) & (now <= small_at) & ((now - s_att) % 2 == 0))
    def _():
        for copy in head_saves((now - s_att) // 2 - 1):
            copy.wait()


    def loads(chunk, slot):
        kept = grads.at[chunk, aligned(core * 2 * CHUNK, 2 * CHUNK), :]
        sent = grads.at[chunk, aligned((1 - core) * 2 * CHUNK, 2 * CHUNK), :]
        return [
            pltpu.make_async_copy(kept, mine, load_sem),
            remote(sent, core_in.at[slot], core_sem, (slot,), sibling),
        ]

    def x_copy(slot):
        return remote(x_out.at[slot % 2], x_in.at[slot], x_sem, (slot,), across)

    def y_copy(slot):
        return remote(
            y_out.at[slot % 2, aligned((1 - side) * half, half)], y_in.at[slot], y_sem, (slot,), beside
        )

    def z_copies(slot):
        return [
            remote(
                z_out.at[slot % 2, aligned((level + move) % levels * piece, piece)],
                z_in.at[slot, move - 1],
                z_sem,
                (slot, move - 1),
                floors[move - 1],
            )
            for move in range(1, levels)
        ]

    def target(chunk, first, size):
        return whole.at[aligned((2 * chunk + core) * CHUNK + first, size), :]

    def keep_copies(chunk, slot):
        part = target(chunk, side * half + level * piece, piece)
        copies = [pltpu.make_async_copy(last.at[slot % 2], part, keep_sem.at[slot % 2])]
        for move in range(1, levels):
            copies.append(remote(last.at[slot % 2], part, zz_sem, (slot, move - 1), floors[move - 1]))
        return copies

    def yy_copy(chunk, slot):
        part = target(chunk, side * half, half)
        return remote(part, part, yy_sem, (slot,), beside)

    def cc_copy(chunk, slot):
        part = target(chunk, 0, CHUNK)
        return remote(part, part, cc_sem, (slot,), sibling)

    def stage_7(chunk, slot):
        cc_copy(chunk, slot).wait()

    def stage_6(chunk, slot):
        yy_copy(chunk, slot).wait()
        cc_copy(chunk, slot).start()

    def stage_5(chunk, slot):
        for copy in keep_copies(chunk, slot):
            copy.wait()
        yy_copy(chunk, slot).start()

    def stage_4(chunk, slot):
        for copy in z_copies(slot):
            copy.wait()
        summed = wide(z_out[slot % 2, aligned(level * piece, piece), :])
        for move in range(1, levels):
            summed = summed + wide(z_in[slot, move - 1])
        last[slot % 2] = low(summed)
        for copy in keep_copies(chunk, slot):
            copy.start()

    def stage_3(chunk, slot):
        y_copy(slot).wait()
        z_out[slot % 2] = low(wide(y_out[slot % 2, aligned(side * half, half), :]) + wide(y_in[slot]))
        for copy in z_copies(slot):
            copy.start()

    def stage_2(chunk, slot):
        x_copy(slot).wait()
        y_out[slot % 2] = low(held[slot % 2] + wide(x_in[slot]))
        y_copy(slot).start()

    def stage_1(chunk, slot):
        for copy in loads(chunk, slot):
            copy.wait()
        x_out[slot % 2] = low(wide(mine[CHUNK:]) + wide(core_in[slot, CHUNK:]))
        x_copy(slot).start()
        held[slot % 2] = wide(mine[:CHUNK]) + wide(core_in[slot, :CHUNK])

    def stage_0(chunk, slot):
        for copy in loads(chunk, slot):
            copy.start()

    stages = [stage_0, stage_1, stage_2, stage_3, stage_4, stage_5, stage_6, stage_7]

    def advance(moment):
        for stage in reversed(range(len(stages))):
            spot = moment - 1 - STAGE_STEPS[stage]
            chunk = spot - spot // (early + gap) * gap

            @pl.when(((spot >= 0) & (spot < early)) | ((spot >= early + gap) & (spot < early + gap + 3 * (outs - 1))))
            def _(stage=stage, chunk=chunk):
                stages[stage](chunk, chunk % 4)

    advance(now)


    @pl.when(now < ffs)
    def _():
        act = braid(act_own[...], act_other[...], 1)
        stage_down[...] = low(dot_tn(act, d_down_ref[...]))
        save_down(now).start()
        w_down = braid(down_own[...], down_other[...], 0)
        w_up = braid(up_own[...], up_other[...], 1)
        for part in (pl.ds(0, length // 2), pl.ds(length // 2, length // 2)):
            d_act = dot_nt(d_down_ref[part, :], w_down)
            slope = braid(slope_own[part, :], slope_other[part, :], 1)
            d_up = low(d_act * wide(slope))
            d_up_ref[part, :] = d_up
            update = dot_nt(d_up, w_up)
            total[part, :] = jnp.where(now == 0, update, update + total[part, :])
        sums = column_sum(wide(d_up_ref[...]))
        for group in range(2):
            for which in range(2):
                first = (2 * which + group) * CHUNK
                spot = aligned(now * units + which * CHUNK, CHUNK, 128)
                up_sums[group, 0:1, spot] = sums[:, first : first + CHUNK]

    @pl.when((now >= 1) & (now <= ffs))
    def _():
        save_up(now - 1).wait()

    @pl.when(now < ffs)
    def _():
        stage_up[...] = low(dot_tn(d_up_ref[...], third_ref[...]))
        save_up(now).start()


    @pl.when(now == s_mid)
    def _():
        for copy in takes[2:6]:
            copy.wait()
        sums = [0.0] * 5
        for index, part in enumerate(blocks):
            take_att(index).wait()
            normed_three, scale_three = standardize(residual_ref[part, :])
            normed_two, scale_two = standardize(att_ref[index % 2])
            d_third = total[part, :]
            d_residual = wide(cot_ref[part, :]) + norm_back(d_third, normed_three, scale_three, gain(2))
            residual_ref[part, :] = d_residual
            d_attended = norm_back(d_residual, normed_two, scale_two, gain(1))
            d_down_ref[part, :] = low(d_attended)
            if index + 2 < parts:
                take_att(index + 2).start()
            terms = [d_residual * normed_two, d_third * normed_three, d_residual, d_third, d_attended]
            sums = [old + column_sum(term) for old, term in zip(sums, terms)]
        small_out[...] = front_sums[...]
        for index, row in enumerate((1, 2, 5, 6, 8)):
            small_out[row : row + 1, :] = sums[index]
        takes[6].start()


    @pl.when(now == s_mid + 1)
    def _():
        for part in blocks:
            third_ref[part, :] = low(dot_nt(d_down_ref[part, :], out_buf[...]))
        out_buf[...] = low(dot_tn(mixed_ref[...], d_down_ref[...]))
        for copy in out_saves:
            copy.start()

    @pl.when(now == s_att)
    def _():
        for copy in out_saves:
            copy.wait()
        takes[7].start()
        takes[6].wait()


    @pl.when((now >= s_att) & (now < small_at))
    def _():
        head = (now - s_att) % 2
        turn_of = (now - s_att) // 2
        pair = turn_of % 2 * (pairs // 2) + turn_of // 4 * 2 + turn_of % 4 // 2
        spot = aligned(pair * 2 * HD, 2 * HD, 128)
        lane = lax.broadcasted_iota(jnp.int32, (1, 2 * HD), 1)
        own = (lane // HD) == head
        scaled = wide(third_ref[:, spot]) * inv_ref[...]
        grad = jnp.where(own, scaled * relax_factor, 0.0).astype(jnp.bfloat16)
        inner = jnp.sum(wide(grad) * wide(mixed_ref[:, spot]), axis=1, keepdims=True)
        d_probs = dot_nt(grad, v_ref[...])
        ds_ref[...] = low(wide(weight_ref[0]) * (d_probs - inner))
        dq = low(dot_nn(ds_ref[...], k_ref[...]) * query_scale)
        dk = low(dot_tn(ds_ref[...], q_ref[...]))
        dv = low(dot_tn(weight_ref[0], low(scaled)))
        for index, value in enumerate((dq, dk, dv)):
            part = pl.ds(index * 2 * HD, 2 * HD)
            dqkv_ref[:, part] = jnp.where(own | (head == 0), value, dqkv_ref[:, part])

        @pl.when(head == 1)
        def _():
            d_qkv = dqkv_ref[...]
            stage_down[pl.ds(0, 6 * HD), :] = low(dot_tn(d_qkv, cot_ref[...]))
            for copy in head_saves(turn_of):
                copy.start()
            group, start = pair // (pairs // 2), pair % (pairs // 2) * 2 * HD
            sums = column_sum(wide(d_qkv))
            columns_of[group, 0:1, aligned(start, 2 * HD, 128)] = sums[:, : 2 * HD]
            columns_of[group, 0:1, aligned(width // 2 + start, 2 * HD, 128)] = sums[:, 4 * HD :]
            weights = jnp.concatenate([w_ref[0], w_ref[1], w_ref[2]], axis=1)
            update = dot_nt(d_qkv, weights)

            @pl.when(turn_of == 0)
            def _():
                total[...] = update

            @pl.when(turn_of > 0)
            def _():
                total[...] += update


    @pl.when(now == small_at)
    def _():
        takes[7].wait()
        sums = [0.0, 0.0]
        for part in blocks:
            normed, scale = standardize(wide(d_down_ref[part, :]))
            errors = total[part, :]
            residual_ref[part, :] += norm_back(errors, normed, scale, gain(0))
            sums = [sums[0] + column_sum(errors * normed), sums[1] + column_sum(errors)]
        save_input.start()
        small_out[0:1, :] = sums[0]
        small_out[4:5, :] = sums[1]
        for group in range(2):
            small_out[10 + 3 * group : 11 + 3 * group, :] = columns_of[group, 0:1, :]
            for index in range(2):
                row = 11 + 3 * group + index
                small_out[row : row + 1, :] = up_sums[group, 0:1, index * width : (index + 1) * width]


    def small_copies(stage):
        if stage < 3:
            return [remote(small_out, small_in.at[stage], small_sem, (stage,), (sibling, across, beside)[stage])]
        return [
            remote(small_out, small_in.at[3 + level], small_sem, (2 + move,), floors[move - 1])
            for move in range(1, levels)
        ]

    def small_step_1():
        small_copies(0)[0].wait()
        small_out[...] += small_in[0]
        small_copies(1)[0].start()

    def small_step_2():
        small_copies(1)[0].wait()
        small_out[0:10, :] += small_in[1, 0:10, :]
        small_out[10:13, :] += small_in[1, 13:16, :]
        small_copies(2)[0].start()

    def small_step_3():
        small_copies(2)[0].wait()
        small_out[...] += small_in[2]
        small_in[3 + level] = small_out[...]
        for copy in small_copies(3):
            copy.start()

    def small_step_4():
        for copy in small_copies(3):
            copy.wait()
        summed = small_in[3]
        for index in range(1, levels):
            summed = summed + small_in[3 + index]
        sums_ref[...] = summed


    @pl.when(now == small_at)
    def _():
        small_copies(0)[0].start()

        @pl.loop(small_at + 1, small_at + 3 * (outs - 1) + STAGE_STEPS[-1])
        def _(moment):
            advance(moment)
            for index, small_step in enumerate((small_step_1, small_step_2, small_step_3, small_step_4)):
                pl.when(moment == small_at + 1 + 2 * index)(small_step)

        save_input.wait()


def rear(
    acts, slopes, w_up, w_down, queries, keys, values, inv, weights, w_qkv, gains, sums, third, d_down, cotangent, mixed,
    first, tokens, attended, residual, w_out, query_scale,
):
    length, width = queries.shape
    pairs = width // (2 * HD)
    ff = w_up.shape[1]
    units = 2 * CHUNK
    ffs = ff // 2 // units
    outs = width // 2 // units
    levels = lax.axis_size("dp") // 4
    half, piece = CHUNK // 2, CHUNK // 2 // levels
    s_att = ffs + 2
    small_at = s_att + 2 * pairs
    chunks = 2 * ffs + outs + 3 * outs
    kind, sem = jnp.bfloat16, pltpu.SemaphoreType.DMA

    def pair_of(i):
        turn_of = jnp.clip(i - s_att, 0, 2 * pairs - 1) // 2
        return turn_of % 2 * (pairs // 2) + turn_of // 4 * 2 + turn_of % 4 // 2

    def head_of(i):
        return pair_of(i) * 2 + jnp.clip(i - s_att, 0, 2 * pairs - 1) % 2

    def fixed(shape):
        return pl.BlockSpec(shape, lambda i: (0,) * len(shape), pipeline_mode=pl.Buffered(1))

    def unit_of(i):
        return jnp.minimum(i, ffs - 1)

    def lanes(rows):
        return [
            pl.BlockSpec((rows, units), lambda i: (0, unit_of(i))),
            pl.BlockSpec((rows, units), lambda i: (0, ffs + unit_of(i))),
        ]

    column = pl.BlockSpec((length, 2 * HD), lambda i: (0, pair_of(i)))
    hbm = pl.BlockSpec(memory_space=pl.ANY)
    return pl.pallas_call(
        partial(rear_kernel, query_scale),
        grid=(small_at + 1,),
        in_specs=[
            *lanes(length),
            *lanes(length),
            *lanes(width),
            pl.BlockSpec((units, width), lambda i: (unit_of(i), 0)),
            pl.BlockSpec((units, width), lambda i: (ffs + unit_of(i), 0)),
            *[column] * 4,
            pl.BlockSpec((1, length, length), lambda i: (head_of(i), 0, 0)),
            pl.BlockSpec((3, width, 2 * HD), lambda i: (0, 0, pair_of(i))),
            fixed((4, width)),
            fixed((16, width)),
            *[hbm] * 9,
        ],
        out_specs=[fixed((16, width)), hbm, hbm, hbm],
        out_shape=[
            jax.ShapeDtypeStruct((16, width), jnp.float32),
            jax.ShapeDtypeStruct((length, width), jnp.float32),
            jax.ShapeDtypeStruct((chunks * 2 * CHUNK, width), kind),
            jax.ShapeDtypeStruct((chunks, 4 * CHUNK, width), kind),
        ],
        scratch_shapes=[
            *[pltpu.VMEM((length, width), kind)] * 4,
            pltpu.VMEM((2, length // 5, width), jnp.float32),
            pltpu.VMEM((length, width), jnp.float32),
            pltpu.VMEM((length, width), jnp.float32),
            pltpu.VMEM((width, width), kind),
            pltpu.VMEM((length, 2 * units), kind),
            pltpu.VMEM((4 * CHUNK, width), kind),
            pltpu.VMEM((4 * CHUNK, width), kind),
            pltpu.VMEM((length, length), kind),
            pltpu.VMEM((length, 6 * HD), kind),
            pltpu.VMEM((2, 8, ff // 2), jnp.float32),
            pltpu.VMEM((2, 8, width), jnp.float32),
            pltpu.VMEM((16, width), jnp.float32),
            pltpu.VMEM((3 + levels, 16, width), jnp.float32),
            pltpu.VMEM((2 * CHUNK, width), kind),
            pltpu.VMEM((4, 2 * CHUNK, width), kind),
            pltpu.VMEM((2, CHUNK, width), jnp.float32),
            pltpu.VMEM((2, CHUNK, width), kind),
            pltpu.VMEM((4, CHUNK, width), kind),
            pltpu.VMEM((2, CHUNK, width), kind),
            pltpu.VMEM((4, half, width), kind),
            pltpu.VMEM((2, half, width), kind),
            pltpu.VMEM((4, levels - 1, piece, width), kind),
            pltpu.VMEM((2, piece, width), kind),
            sem((8,)),
            sem((2,)),
            sem((2,)),
            sem((2, outs, 2)),
            sem((3,)),
            sem,
            sem,
            sem((2, 4)),
            sem((2, 4)),
            sem((2, 4)),
            sem((2, 4, levels - 1)),
            sem((2, 4, levels - 1)),
            sem((2, 4)),
            sem((2, 4)),
            sem((2,)),
            sem((2, 2 + levels)),
        ],
        compiler_params=pltpu.CompilerParams(
            collective_id=0, has_side_effects=True, vmem_limit_bytes=63 * 2**20
        ),
    )(
        acts, acts, slopes, slopes, w_up, w_up, w_down, w_down, queries, keys, values, inv, weights, w_qkv, gains, sums,
        third, d_down, cotangent, mixed, first, tokens, attended, residual, w_out,
    )[:3]


def unpack_kernel(ffs, outs, whole_ref, down_ref, up_ref, out_ref, qkv_ref):
    now = pl.program_id(0)
    value = wide(whole_ref[...])

    @pl.when((now < 2 * ffs) & (now % 2 == 0))
    def _():
        down_ref[...] = value

    @pl.when((now < 2 * ffs) & (now % 2 == 1))
    def _():
        up_ref[...] = value.T

    @pl.when((now >= 2 * ffs) & (now < 2 * ffs + outs))
    def _():
        out_ref[...] = value

    @pl.when(now >= 2 * ffs + outs)
    def _():
        qkv_ref[0] = value.T


def unpack(whole, ff, width):
    units = 2 * CHUNK
    ffs = ff // 2 // units
    outs = width // 2 // units
    first_head = 2 * ffs + outs

    def head_turn(i):
        return jnp.maximum(i - first_head, 0)

    return pl.pallas_call(
        partial(unpack_kernel, ffs, outs),
        grid=(first_head + 3 * outs,),
        in_specs=[pl.BlockSpec((units, width), lambda i: (i, 0))],
        out_specs=[
            pl.BlockSpec((units, width), lambda i: (jnp.minimum(i // 2, ffs - 1), 0)),
            pl.BlockSpec((width, units), lambda i: (0, jnp.minimum(i // 2, ffs - 1))),
            pl.BlockSpec((units, width), lambda i: (jnp.clip(i - 2 * ffs, 0, outs - 1), 0)),
            pl.BlockSpec((1, width, units), lambda i: (head_turn(i) % 3, 0, head_turn(i) // 3)),
        ],
        out_shape=[
            jax.ShapeDtypeStruct((ff // 2, width), jnp.float32),
            jax.ShapeDtypeStruct((width, ff // 2), jnp.float32),
            jax.ShapeDtypeStruct((width // 2, width), jnp.float32),
            jax.ShapeDtypeStruct((3, width, width // 2), jnp.float32),
        ],
        compiler_params=pltpu.CompilerParams(vmem_limit_bytes=32 * 2**20),
    )(whole)


def sequence_shards(
    tokens,
    cond_flags,
    seg_lengths,
    norm_gains,
    norm_biases,
    w_qkv,
    qv_bias,
    w_out,
    out_biases,
    w_up,
    up_bias,
    w_down,
    cotangent,
):
    width = tokens.shape[1]
    query_scale = 1.0 / (relax_factor * math.sqrt(HD))
    (
        queries, keys, values, inv, kept, acts, slopes, small, first_in, mixed, attended, residual, third_in, result,
        d_down, all_qkv, all_out, all_up, all_down,
    ) = front(
        cond_flags, seg_lengths, tokens, cotangent, norm_gains, norm_biases, out_biases, qv_bias, up_bias,
        w_qkv, w_out, w_up, w_down, query_scale,
    )
    sums, grad_input, whole = rear(
        acts, slopes, all_up, all_down, queries, keys, values, inv, kept, all_qkv, norm_gains, small, third_in, d_down,
        cotangent, mixed, first_in, tokens, attended, residual, all_out, query_scale,
    )
    grad_w_down, grad_w_up, grad_w_out, grad_w_qkv = unpack(whole, all_up.shape[1], width)
    return (
        result,
        grad_input,
        sums[:4],
        sums[4:8],
        grad_w_qkv,
        sums[10].reshape(2, -1),
        grad_w_out,
        sums[8:10],
        grad_w_up,
        sums[11:13].reshape(-1),
        grad_w_down,
    )


def solution(mesh):
    in_specs = (
        P(("dp", "mp"), None),
        P("dp", None),
        P("dp", None),
        P(),
        P(),
        P(None, None, "mp"),
        P(None, "mp"),
        P("mp", None),
        P(),
        P(None, "mp"),
        P("mp"),
        P("mp", None),
        P(("dp", "mp"), None),
    )
    out_specs = (
        P(("dp", "mp"), None),
        P(("dp", "mp"), None),
        P(),
        P(),
        P(None, None, "mp"),
        P(None, "mp"),
        P("mp", None),
        P(),
        P(None, "mp"),
        P("mp"),
        P("mp", None),
    )
    per_device = mesh.shape["dp"] * mesh.shape["mp"]

    def step(*args):
        whole_sequences = args[1].shape[0] == per_device
        local = sequence_shards if whole_sequences and mesh.shape["mp"] == 2 and mesh.shape["dp"] == 16 else shards
        return jax.shard_map(
            local, mesh=mesh, in_specs=in_specs, out_specs=out_specs, check_vma=False
        )(*args)

    return step
```

```python
from functools import partial
import math

import jax
import jax.numpy as jnp
from jax import lax
from jax.experimental import pallas as pl
from jax.experimental.pallas import tpu as pltpu
from jax.sharding import PartitionSpec as P

HD = 64


epsilon = 1e-05
relax_factor = 32.0


def standardize(entries):
    average = jnp.mean(entries, axis=-1, keepdims=True)
    centred = entries - average
    spread = jnp.mean(centred * centred, axis=-1, keepdims=True)
    inv_std = lax.rsqrt(spread + epsilon)
    return (centred * inv_std, inv_std)


def norm_back(grad_in, normed, inv_std, gain_row):
    weighted = grad_in * gain_row
    return inv_std * (
        weighted
        - jnp.mean(weighted, axis=-1, keepdims=True)
        - normed * jnp.mean(weighted * normed, axis=-1, keepdims=True)
    )


def token_marks(seg_flags, lengths, length):
    position = jnp.arange(length, dtype=jnp.int32)
    segment = (position >= lengths[0]).astype(jnp.int32) + (
        position >= lengths[0] + lengths[1]
    ).astype(jnp.int32)
    segment_hits = (segment[:, None] == jnp.arange(3, dtype=jnp.int32)[None, :]).astype(jnp.int32)
    return jnp.sum(segment_hits * seg_flags[None, :], axis=1)


def block_mask(marks_seq, first_row, block_rows, length):
    query_places = first_row + jnp.arange(block_rows, dtype=jnp.int32)
    key_places = jnp.arange(length, dtype=jnp.int32)
    return (key_places[None, :] <= query_places[:, None]) | (marks_seq[None, :] == 1)


def shards(
    tokens,
    cond_flags,
    seg_lengths,
    norm_gains,
    norm_biases,
    w_qkv,
    qv_bias,
    w_out,
    out_biases,
    w_up,
    up_bias,
    w_down,
    cotangent,
):
    shard_rows = tokens.shape[0]
    group_rows = shard_rows * lax.axis_size("mp")
    seq_count = cond_flags.shape[0]
    length = group_rows // seq_count
    block_rows = length // 2
    head_count = w_qkv.shape[2] // HD
    local_width = head_count * HD
    query_scale = 1.0 / (relax_factor * math.sqrt(HD))
    all_marks = jax.vmap(lambda seg_flags, lengths: token_marks(seg_flags, lengths, length))(
        cond_flags, seg_lengths
    )
    numbers = jnp.arange(seq_count * 2, dtype=jnp.int32)
    source = tokens.astype(jnp.float32)
    normed_one, scale_one = standardize(source)
    first_in = (normed_one * norm_gains[0] + norm_biases[0]).astype(jnp.bfloat16)
    first_all = lax.all_gather(first_in, "mp", axis=0, tiled=True)
    bias_rows = jnp.stack([qv_bias[0], jnp.zeros_like(qv_bias[0]), qv_bias[1]])
    projected = (
        jnp.einsum("td,cde->cte", first_all, w_qkv, preferred_element_type=jnp.float32)
        + bias_rows[:, None, :]
    )
    queries = (
        (projected[0] * query_scale)
        .astype(jnp.bfloat16)
        .reshape(seq_count * 2, block_rows, head_count, HD)
    )
    key_all = projected[1].astype(jnp.bfloat16).reshape(seq_count, length, head_count, HD)
    value_all = projected[2].astype(jnp.bfloat16).reshape(seq_count, length, head_count, HD)

    def block_probs(query_block, number, row_top, row_total):
        sequence = number // 2
        first_row = number % 2 * block_rows
        key_seq = lax.dynamic_index_in_dim(key_all, sequence, 0, keepdims=False)
        allowed = block_mask(
            lax.dynamic_index_in_dim(all_marks, sequence, 0, keepdims=False),
            first_row,
            block_rows,
            length,
        )
        scores = jnp.einsum(
            "qhd,khd->hqk", query_block, key_seq, preferred_element_type=jnp.float32
        )
        if row_top is None:
            row_top = jnp.max(jnp.where(allowed[None], scores, -1e30), axis=-1, keepdims=True)
        weights = jnp.exp(jnp.where(allowed[None], (scores - row_top) * relax_factor, -30000.0))
        if row_total is None:
            row_total = jnp.sum(weights, axis=-1, keepdims=True)
        return (weights / row_total, row_top, row_total, key_seq)

    def forward_block(block_item):
        query_block, number = block_item
        probs, row_top, row_total, key_seq = block_probs(query_block, number, None, None)
        value_seq = lax.dynamic_index_in_dim(value_all, number // 2, 0, keepdims=False)
        mixed_block = jnp.einsum(
            "hqk,khd->qhd",
            probs.astype(jnp.bfloat16),
            value_seq,
            preferred_element_type=jnp.float32,
        )
        return (mixed_block.astype(jnp.bfloat16), row_top, row_total)

    mixed_heads, row_tops, row_totals = lax.map(forward_block, (queries, numbers))
    mixed_heads = mixed_heads.reshape(group_rows, local_width)
    attended = (
        lax.psum_scatter(
            jnp.dot(mixed_heads, w_out, preferred_element_type=jnp.float32),
            "mp",
            scatter_dimension=0,
            tiled=True,
        )
        + out_biases[0]
    )
    normed_two, scale_two = standardize(attended)
    residual = source + normed_two * norm_gains[1] + norm_biases[1]
    normed_three, scale_three = standardize(residual)
    third_in = (normed_three * norm_gains[2] + norm_biases[2]).astype(jnp.bfloat16)
    third_all = lax.all_gather(third_in, "mp", axis=0, tiled=True)
    up_value = jnp.dot(third_all, w_up, preferred_element_type=jnp.float32) + up_bias
    activated = jax.nn.gelu(up_value, approximate=True).astype(jnp.bfloat16)
    down = (
        lax.psum_scatter(
            jnp.dot(activated, w_down, preferred_element_type=jnp.float32),
            "mp",
            scatter_dimension=0,
            tiled=True,
        )
        + out_biases[1]
    )
    normed_four, scale_four = standardize(down)
    result = (residual + normed_four * norm_gains[3] + norm_biases[3]).astype(jnp.bfloat16)
    grad_out = cotangent.astype(jnp.float32)
    d_down = norm_back(grad_out, normed_four, scale_four, norm_gains[3])
    d_down_low = d_down.astype(jnp.bfloat16)
    d_down_all = lax.all_gather(d_down_low, "mp", axis=0, tiled=True)
    d_act = jnp.einsum("td,fd->tf", d_down_all, w_down, preferred_element_type=jnp.float32)
    grad_w_down = jnp.einsum("tf,td->fd", activated, d_down_all, preferred_element_type=jnp.float32)
    gelu_value, gelu_pull = jax.vjp(partial(jax.nn.gelu, approximate=True), up_value)
    d_up = gelu_pull(d_act)[0].astype(jnp.bfloat16)
    grad_w_up = jnp.einsum("td,tf->df", third_all, d_up, preferred_element_type=jnp.float32)
    grad_up_bias = jnp.sum(d_up, axis=0, dtype=jnp.float32)
    d_third = lax.psum_scatter(
        jnp.einsum("tf,df->td", d_up, w_up, preferred_element_type=jnp.float32),
        "mp",
        scatter_dimension=0,
        tiled=True,
    )
    d_residual = grad_out + norm_back(d_third, normed_three, scale_three, norm_gains[2])
    d_attended = norm_back(d_residual, normed_two, scale_two, norm_gains[1])
    d_att_low = d_attended.astype(jnp.bfloat16)
    d_att_all = lax.all_gather(d_att_low, "mp", axis=0, tiled=True)
    d_mixed = jnp.einsum("td,hd->th", d_att_all, w_out, preferred_element_type=jnp.float32).astype(
        jnp.bfloat16
    )
    grad_w_out = jnp.einsum("th,td->hd", mixed_heads, d_att_all, preferred_element_type=jnp.float32)
    d_mixed_blocks = d_mixed.reshape(seq_count * 2, block_rows, head_count, HD)

    def backward_block(block_item):
        query_block, d_block, row_top, row_total, number = block_item
        probs, kept_top, kept_total, key_seq = block_probs(query_block, number, row_top, row_total)
        value_seq = lax.dynamic_index_in_dim(value_all, number // 2, 0, keepdims=False)
        d_probs = jnp.einsum("qhd,khd->hqk", d_block, value_seq, preferred_element_type=jnp.float32)
        inner = jnp.sum(probs * d_probs, axis=-1, keepdims=True)
        d_scores = (relax_factor * probs * (d_probs - inner)).astype(jnp.bfloat16)
        d_query = (
            jnp.einsum("hqk,khd->qhd", d_scores, key_seq, preferred_element_type=jnp.float32)
            * query_scale
        )
        d_key = jnp.einsum(
            "hqk,qhd->khd", d_scores, query_block, preferred_element_type=jnp.float32
        )
        d_value = jnp.einsum(
            "hqk,qhd->khd", probs.astype(jnp.bfloat16), d_block, preferred_element_type=jnp.float32
        )
        return (d_query.astype(jnp.bfloat16), d_key, d_value)

    d_queries, d_keys, d_values = lax.map(
        backward_block, (queries, d_mixed_blocks, row_tops, row_totals, numbers)
    )
    d_keys = jnp.sum(d_keys.reshape(seq_count, 2, length, local_width), axis=1).reshape(
        group_rows, local_width
    )
    d_values = jnp.sum(d_values.reshape(seq_count, 2, length, local_width), axis=1).reshape(
        group_rows, local_width
    )
    d_qkv = jnp.stack(
        [
            d_queries.reshape(group_rows, local_width),
            d_keys.astype(jnp.bfloat16),
            d_values.astype(jnp.bfloat16),
        ]
    )
    grad_w_qkv = jnp.einsum("td,cte->cde", first_all, d_qkv, preferred_element_type=jnp.float32)
    grad_qv_bias = jnp.stack(
        [jnp.sum(d_qkv[0], axis=0, dtype=jnp.float32), jnp.sum(d_qkv[2], axis=0, dtype=jnp.float32)]
    )
    d_first = lax.psum_scatter(
        jnp.einsum("cte,cde->td", d_qkv, w_qkv, preferred_element_type=jnp.float32).astype(
            jnp.bfloat16
        ),
        "mp",
        scatter_dimension=0,
        tiled=True,
    ).astype(jnp.float32)
    grad_input = d_residual + norm_back(d_first, normed_one, scale_one, norm_gains[0])
    error_terms = (d_first, d_residual, d_third, grad_out)
    normed_terms = (normed_one, normed_two, normed_three, normed_four)
    gain_sums = jnp.stack(
        [
            jnp.sum(error_term * normed_term, axis=0)
            for error_term, normed_term in zip(error_terms, normed_terms)
        ]
    )
    bias_sums = jnp.stack([jnp.sum(error_term, axis=0) for error_term in error_terms])
    outer_sums = jnp.stack([jnp.sum(d_attended, axis=0), jnp.sum(d_down, axis=0)])
    gain_sums, bias_sums, outer_sums = lax.psum((gain_sums, bias_sums, outer_sums), ("dp", "mp"))
    grad_w_qkv, grad_qv_bias, grad_w_out, grad_w_up, grad_up_bias, grad_w_down = (
        lax.psum(grad_w_qkv.astype(jnp.bfloat16), "dp").astype(jnp.float32),
        lax.psum(grad_qv_bias.astype(jnp.bfloat16), "dp").astype(jnp.float32),
        lax.psum(grad_w_out.astype(jnp.bfloat16), "dp").astype(jnp.float32),
        lax.psum(grad_w_up.astype(jnp.bfloat16), "dp").astype(jnp.float32),
        lax.psum(grad_up_bias.astype(jnp.bfloat16), "dp").astype(jnp.float32),
        lax.psum(grad_w_down.astype(jnp.bfloat16), "dp").astype(jnp.float32),
    )
    return (
        result,
        grad_input,
        gain_sums,
        bias_sums,
        grad_w_qkv,
        grad_qv_bias,
        grad_w_out,
        outer_sums,
        grad_w_up,
        grad_up_bias,
        grad_w_down,
    )


LOG2E = 1.4426950408889634
HIDDEN = -1e30


def dot_nt(a, b):
    return lax.dot_general(a, b, (((1,), (1,)), ((), ())), preferred_element_type=jnp.float32)


def dot_nn(a, b):
    return lax.dot_general(a, b, (((1,), (0,)), ((), ())), preferred_element_type=jnp.float32)


def dot_tn(a, b):
    return lax.dot_general(a, b, (((0,), (0,)), ((), ())), preferred_element_type=jnp.float32)


def low(value):
    return value.astype(jnp.bfloat16)


MESH = pl.DeviceIdType.MESH
CHUNK = 128


def remote(source, target, sems, index, device):
    return pltpu.make_async_remote_copy(
        src_ref=source,
        dst_ref=target,
        send_sem=sems.at[(0, *index)],
        recv_sem=sems.at[(1, *index)],
        device_id=device,
        device_id_type=MESH,
    )


def aligned(start, size, unit=16):
    return pl.ds(pl.multiple_of(start, unit), size)


def wide(value):
    return value.astype(jnp.float32)


GELU_SCALE = math.sqrt(2.0 / math.pi)
GELU_CUBE = 0.044715


def gelu_both(up):
    square = up * up
    half = 0.5 * jnp.tanh(up * (GELU_SCALE + GELU_SCALE * GELU_CUBE * square)) + 0.5
    value = up * half
    slope = half + value * (1.0 - half) * (2.0 * GELU_SCALE + 6.0 * GELU_SCALE * GELU_CUBE * square)
    return value, slope


def column_sum(value):
    return jnp.sum(value, axis=0, keepdims=True)


def front_kernel(
    query_scale,
    events,
    flags_ref,
    lengths_ref,
    gain_ref,
    shift_ref,
    out_bias_ref,
    qv_bias_ref,
    up_bias_ref,
    tokens_in,
    cot_in,
    own_qkv,
    own_out,
    own_up,
    own_down,
    q_ref,
    k_ref,
    v_ref,
    inv_ref,
    weight_ref,
    act_ref,
    slope_ref,
    small_ref,
    first_out,
    mixed_out,
    att_out,
    residual_out,
    third_out,
    result_out,
    d_down_out,
    all_qkv,
    all_out,
    all_up,
    all_down,
    first_ref,
    mixed_ref,
    tokens_ref,
    third_ref,
    att_ref,
    residual_ref,
    total,
    qkv_buf,
    out_buf,
    up_buf,
    down_buf,
    hide_ref,
    qv_all,
    up_bias_all,
    qkv_load,
    out_load,
    up_load,
    down_load,
    qkv_keep,
    out_keep,
    up_keep,
    down_keep,
    bias_sem,
    x_sem,
    y_sem,
    z_sem,
    c_sem,
    in_sem,
    save_sem,
    end_sem,
):
    now = pl.program_id(0)
    place = lax.axis_index("dp")
    turn = lax.axis_index("mp")
    core, side, odd = place % 2, (place // 2) % 2, place // 4 % 2
    above = {"dp": place + 4 - 8 * odd}
    sibling = {"dp": place + 1 - 2 * core}
    across = {"mp": 1 - turn}
    beside = {"dp": place + 2 - 4 * side}
    length, width = tokens_ref.shape
    pairs = width // (2 * HD)
    size = act_ref.shape[1]
    ff = all_up.shape[1]
    chunks = ff // size
    mid = pairs
    end = mid + chunks + 1
    parts = 5
    step = length // parts
    blocks = [pl.ds(start, step) for start in range(0, length, step)]

    def gain(index):
        return gain_ref[index : index + 1, :]

    def shift(index):
        return shift_ref[index : index + 1, :]


    q_qkv, q_out, q_up, q_down = width // 8, width // 8, ff // 8, ff // 8
    row_up = width // 4

    def places(index, quarter, count, narrow):
        if index < 3:
            cols = aligned(quarter * q_qkv, count * q_qkv, 128)
            far = aligned(width // 2 + quarter * q_qkv, count * q_qkv, 128)
            return own_qkv.at[index, :, cols], all_qkv.at[index, :, far]
        if index < 4:
            rows = aligned(quarter * q_out, count * q_out)
            return own_out.at[rows, :], all_out.at[aligned(width // 2 + quarter * q_out, count * q_out), :]
        first, span = (index - 4) % 4 * row_up, row_up
        if narrow:
            first, span = first + odd * (row_up // 2), row_up // 2
        if index < 8:
            rows = aligned(first, span)
            cols = aligned(quarter * q_up, count * q_up, 128)
            return own_up.at[rows, cols], all_up.at[rows, aligned(ff // 2 + quarter * q_up, count * q_up, 128)]
        cols = aligned(first, span, 128)
        rows = aligned(quarter * q_down, count * q_down)
        return own_down.at[rows, cols], all_down.at[aligned(ff // 2 + quarter * q_down, count * q_down), cols]

    def hop(index, stage):
        narrow = FLOORED[0] <= index < FLOORED[1]
        if stage == 0:
            source, target = places(index, 2 * core + side, 1, narrow)
            return remote(source, target, x_sem, (index,), across)
        if stage == 1:
            part = places(index, 2 * core + side, 1, narrow)[1]
            return remote(part, part, y_sem, (index,), beside)
        part = places(index, 2 * core, 2, narrow and stage == 2)[1]
        if narrow and stage == 2:
            return remote(part, part, z_sem, (index,), above)
        return remote(part, part, c_sem, (index,), sibling)

    bias_copies = [
        remote(qv_bias_ref, qv_all.at[1], bias_sem, (0,), across),
        remote(up_bias_ref, up_bias_all.at[1], bias_sem, (1,), across),
    ]
    def load_pair(pair, ref):
        start = pair % (pairs // 2) * 2 * HD if ref is own_qkv else pair * 2 * HD
        return pltpu.make_async_copy(
            ref.at[:, :, aligned(start, 2 * HD, 128)], qkv_buf.at[pair % 2], qkv_load.at[pair % 2]
        )

    def load_chunk(chunk, up, down):
        slot = chunk % 2
        return [
            pltpu.make_async_copy(up.at[:, aligned(chunk * size, size, 128)], up_buf.at[slot], up_load.at[slot]),
            pltpu.make_async_copy(down.at[aligned(chunk * size, size), :], down_buf.at[slot], down_load.at[slot]),
        ]

    out_loads = [
        pltpu.make_async_copy(
            own_out, out_buf.at[pl.ds(0, width // 2), :], out_load.at[0]
        ),
        pltpu.make_async_copy(
            all_out.at[pl.ds(width // 2, width // 2), :], out_buf.at[pl.ds(width // 2, width // 2), :], out_load.at[1]
        ),
    ]

    def keep_pair(pair):
        return pltpu.make_async_copy(
            qkv_buf.at[pair % 2], all_qkv.at[:, :, aligned(pair * 2 * HD, 2 * HD, 128)], qkv_keep.at[pair % 2]
        )

    def keep_chunk(chunk):
        slot = chunk % 2
        return [
            pltpu.make_async_copy(up_buf.at[slot], all_up.at[:, aligned(chunk * size, size, 128)], up_keep.at[slot]),
            pltpu.make_async_copy(down_buf.at[slot], all_down.at[aligned(chunk * size, size), :], down_keep.at[slot]),
        ]

    keep_out = pltpu.make_async_copy(
        out_buf.at[pl.ds(0, width // 2), :], all_out.at[pl.ds(0, width // 2), :], out_keep
    )
    take_tokens = pltpu.make_async_copy(tokens_in, tokens_ref, in_sem.at[0])
    take_cot = pltpu.make_async_copy(cot_in, first_ref, in_sem.at[1])
    save_first = pltpu.make_async_copy(first_ref, first_out, save_sem.at[0])
    saves = [
        pltpu.make_async_copy(mixed_ref, mixed_out, save_sem.at[1]),
        pltpu.make_async_copy(att_ref, att_out, save_sem.at[2]),
        pltpu.make_async_copy(residual_ref, residual_out, save_sem.at[3]),
        pltpu.make_async_copy(third_ref, third_out, save_sem.at[4]),
    ]

    def end_copies(index):
        part = blocks[index]
        return [
            pltpu.make_async_copy(tokens_ref.at[part, :], result_out.at[part, :], end_sem.at[0, index]),
            pltpu.make_async_copy(mixed_ref.at[part, :], d_down_out.at[part, :], end_sem.at[1, index]),
        ]

    def run_events(slot):
        for index, stage in events.get(slot, []):
            hops = 4 if FLOORED[0] <= index < FLOORED[1] else 3
            if stage > 0:
                hop(index, stage - 1).wait()
            if stage < hops:
                hop(index, stage).start()

    @pl.when(now == 0)
    def _():
        take_tokens.start()
        load_pair(0, own_qkv).start()
        barrier = pltpu.get_barrier_semaphore()
        partners = [sibling, across, beside, above]
        for partner in partners:
            pl.semaphore_signal(barrier, inc=1, device_id=partner, device_id_type=MESH)
        pl.semaphore_wait(barrier, len(partners))
        for copy in bias_copies:
            copy.start()

    for moment in range(end):

        @pl.when(now == moment)
        def _(moment=moment):
            run_events(2 * moment if moment < mid else moment + mid)

    @pl.when(now == 0)
    def _():
        qv_all[0] = qv_bias_ref[...]
        up_bias_all[0] = up_bias_ref[...]
        spots = lax.broadcasted_iota(jnp.int32, (1, length), 1)
        one = lengths_ref[turn, 0]
        two = one + lengths_ref[turn, 1]
        marks = jnp.where(
            spots < one, flags_ref[turn, 0], jnp.where(spots < two, flags_ref[turn, 1], flags_ref[turn, 2])
        )
        hide_ref[...] = jnp.where(marks == 1, 0.0, HIDDEN)
        take_tokens.wait()
        for part in blocks:
            normed, _ = standardize(wide(tokens_ref[part, :]))
            first_ref[part, :] = low(normed * gain(0) + shift(0))
        save_first.start()

    @pl.when(now == pairs // 2)
    def _():
        bias_copies[0].wait()

    @pl.when(now == mid)
    def _():
        bias_copies[1].wait()


    def attend_head(head):
        lane = lax.broadcasted_iota(jnp.int32, (1, 2 * HD), 1)
        own = (lane // HD) == head
        keys = k_ref[...]
        values = jnp.where(own, v_ref[...], jnp.ones((1, 2 * HD), jnp.bfloat16))
        rows = length // 2
        spot = aligned(now * 2 * HD, 2 * HD, 128)
        for start in (0, rows):
            part = pl.ds(start, rows)
            mine = jnp.where(own, q_ref[part, :], jnp.zeros((1, 2 * HD), jnp.bfloat16))
            scores = dot_nt(mine, keys)
            query_places = lax.broadcasted_iota(jnp.int32, (rows, length), 0) + start
            key_places = lax.broadcasted_iota(jnp.int32, (rows, length), 1)
            scores = scores + jnp.where(key_places <= query_places, 0.0, hide_ref[...])
            top = jnp.max(scores, axis=1, keepdims=True)
            kept = low(jnp.exp2((scores - top) * (relax_factor * LOG2E)))
            weight_ref[head, part, :] = kept
            mixed = dot_nn(kept, values)
            inv = 1.0 / pltpu.roll(mixed, HD, 1)
            out = low(mixed * inv)
            mixed_ref[part, spot] = out if head == 0 else jnp.where(own, out, mixed_ref[part, spot])
            inv_ref[part, :] = inv if head == 0 else jnp.where(own, inv, inv_ref[part, :])

    @pl.when(now < mid)
    def _():
        pair = now
        load_pair(pair, all_qkv).wait()
        group, start = pair // (pairs // 2), pair % (pairs // 2) * 2 * HD
        parts_of = qkv_buf[pair % 2]
        projected = dot_nn(first_ref[...], jnp.concatenate([parts_of[0], parts_of[1], parts_of[2]], axis=1))
        bias_q = qv_all[group, 0:1, aligned(start, 2 * HD, 128)]
        bias_v = qv_all[group, 1:2, aligned(start, 2 * HD, 128)]
        q_ref[...] = low((projected[:, : 2 * HD] + bias_q) * query_scale)
        k_ref[...] = low(projected[:, 2 * HD : 4 * HD])
        v_ref[...] = low(projected[:, 4 * HD :] + bias_v)

    @pl.when(now < pairs // 2)
    def _():
        keep_pair(now).start()

    @pl.when(now < mid)
    def _():
        attend_head(0)

    for moment in range(mid):

        @pl.when(now == moment)
        def _(moment=moment):
            run_events(2 * moment + 1)

    @pl.when((now >= 1) & (now <= pairs // 2))
    def _():
        keep_pair(now - 1).wait()

    @pl.when(now < pairs // 2 - 1)
    def _():
        load_pair(now + 1, own_qkv).start()

    @pl.when((now >= pairs // 2 - 1) & (now < mid - 1))
    def _():
        load_pair(now + 1, all_qkv).start()

    @pl.when(now == mid - 1)
    def _():
        for copy in out_loads:
            copy.start()

    @pl.when(now < mid)
    def _():
        attend_head(1)

    @pl.when(now == mid)
    def _():
        for copy in load_chunk(0, own_up, own_down):
            copy.start()
        save_first.wait()
        take_cot.start()
        for copy in out_loads:
            copy.wait()
        keep_out.start()
        for part in blocks:
            attended = dot_nn(mixed_ref[part, :], out_buf[...]) + out_bias_ref[0:1, :]
            att_ref[part, :] = attended
            normed_two, _ = standardize(attended)
            residual = wide(tokens_ref[part, :]) + normed_two * gain(1) + shift(1)
            residual_ref[part, :] = residual
            normed_three, _ = standardize(residual)
            third_ref[part, :] = low(normed_three * gain(2) + shift(2))
            total[part, :] = jnp.broadcast_to(out_bias_ref[1:2, :], (step, width))
        for copy in saves:
            copy.start()

    @pl.when((now > mid) & (now < end))
    def _():
        for copy in load_chunk(now - mid - 1, all_up, all_down):
            copy.wait()

    @pl.when((now > mid + 1) & (now <= mid + 1 + chunks // 2))
    def _():
        for copy in keep_chunk(now - mid - 2):
            copy.wait()

    @pl.when((now > mid) & (now < mid + chunks // 2))
    def _():
        for copy in load_chunk(now - mid, own_up, own_down):
            copy.start()

    @pl.when((now >= mid + chunks // 2) & (now < end - 1))
    def _():
        for copy in load_chunk(now - mid, all_up, all_down):
            copy.start()

    @pl.when((now > mid) & (now <= mid + chunks // 2))
    def _():
        for copy in keep_chunk(now - mid - 1):
            copy.start()

    @pl.when((now > mid) & (now < end))
    def _():
        chunk = now - mid - 1
        slot = chunk % 2
        group, start = chunk // (chunks // 2), chunk % (chunks // 2) * size
        bias = up_bias_all[group, 0:1, aligned(start, size, 128)]
        for part in (pl.ds(0, length // 2), pl.ds(length // 2, length // 2)):
            up = dot_nn(third_ref[part, :], up_buf[slot]) + bias
            value, slope = gelu_both(up)
            act = low(value)
            act_ref[part, :] = act
            slope_ref[part, :] = low(slope)
            total[part, :] += dot_nn(act, down_buf[slot])

    @pl.when(now == end)
    def _():
        take_cot.wait()
        keep_out.wait()
        for copy in saves:
            copy.wait()
        sums = [0.0, 0.0, 0.0]
        for index, part in enumerate(blocks):
            normed_four, scale_four = standardize(total[part, :])
            tokens_ref[part, :] = low(residual_ref[part, :] + normed_four * gain(3) + shift(3))
            grad_out = wide(first_ref[part, :])
            d_down = norm_back(grad_out, normed_four, scale_four, gain(3))
            mixed_ref[part, :] = low(d_down)
            for copy in end_copies(index):
                copy.start()
            terms = [grad_out * normed_four, grad_out, d_down]
            sums = [old + column_sum(term) for old, term in zip(sums, terms)]
        small_ref[...] = jnp.zeros_like(small_ref)
        small_ref[3:4, :] = sums[0]
        small_ref[7:8, :] = sums[1]
        small_ref[9:10, :] = sums[2]
        for index in range(parts):
            for copy in end_copies(index):
                copy.wait()


FLOORED = (4, 10)


def front_events():
    times = (
        (0, 1, 3, 4), (0, 3, 5, 6), (0, 4, 6, 7), (6, 10, 12, 13),
        (2, 6, 7, 9, 10), (3, 7, 8, 11, 12), (4, 8, 9, 13, 14), (5, 9, 10, 14, 15),
        (8, 12, 13, 16, 17), (9, 13, 14, 17, 18), (11, 14, 16, 17), (12, 16, 18, 19),
    )
    plan = {}
    for index, moments in enumerate(times):
        for stage, moment in enumerate(moments):
            plan.setdefault(moment, []).append((index, stage))
    return {moment: sorted(items, key=lambda item: -item[1]) for moment, items in plan.items()}


def front(flags, lengths, tokens, cotangent, gains, shifts, out_biases, qv_bias, up_bias, w_qkv, w_out, w_up, w_down, query_scale):
    length, width = tokens.shape
    pairs = width // (2 * HD)
    ff = 2 * w_up.shape[1]
    size = 512
    chunks = ff // size
    kind, sem = jnp.bfloat16, pltpu.SemaphoreType.DMA

    def whole(shape):
        return pl.BlockSpec(shape, lambda i: (0,) * len(shape), pipeline_mode=pl.Buffered(1))

    hbm = pl.BlockSpec(memory_space=pl.ANY)
    smem = pl.BlockSpec(memory_space=pltpu.SMEM)
    column = pl.BlockSpec((length, 2 * HD), lambda i: (0, jnp.minimum(i, pairs - 1)))
    piece = pl.BlockSpec((length, size), lambda i: (0, jnp.clip(i - pairs - 1, 0, chunks - 1)))

    def low_like(*shape):
        return jax.ShapeDtypeStruct(shape, kind)

    def wide_like(*shape):
        return jax.ShapeDtypeStruct(shape, jnp.float32)

    return pl.pallas_call(
        partial(front_kernel, query_scale, front_events()),
        grid=(pairs + chunks + 2,),
        in_specs=[
            smem,
            smem,
            whole((4, width)),
            whole((4, width)),
            whole((2, width)),
            whole(qv_bias.shape),
            whole((1, ff // 2)),
            *[hbm] * 6,
        ],
        out_specs=[
            column,
            column,
            column,
            column,
            pl.BlockSpec((2, length, length), lambda i: (jnp.minimum(i, pairs - 1), 0, 0)),
            piece,
            piece,
            whole((16, width)),
            *[hbm] * 11,
        ],
        out_shape=[
            low_like(length, width),
            low_like(length, width),
            low_like(length, width),
            wide_like(length, width),
            low_like(2 * pairs, length, length),
            low_like(length, ff),
            low_like(length, ff),
            wide_like(16, width),
            low_like(length, width),
            low_like(length, width),
            wide_like(length, width),
            wide_like(length, width),
            low_like(length, width),
            low_like(length, width),
            low_like(length, width),
            low_like(3, width, width),
            low_like(width, width),
            low_like(width, ff),
            low_like(ff, width),
        ],
        scratch_shapes=[
            *[pltpu.VMEM((length, width), kind)] * 4,
            *[pltpu.VMEM((length, width), jnp.float32)] * 3,
            pltpu.VMEM((2, 3, width, 2 * HD), kind),
            pltpu.VMEM((width, width), kind),
            pltpu.VMEM((2, width, size), kind),
            pltpu.VMEM((2, size, width), kind),
            pltpu.VMEM((1, length), jnp.float32),
            pltpu.VMEM((2, *qv_bias.shape), jnp.float32),
            pltpu.VMEM((2, 1, ff // 2), jnp.float32),
            sem((2,)),
            sem((2,)),
            sem((2,)),
            sem((2,)),
            sem((2,)),
            sem,
            sem((2,)),
            sem((2,)),
            sem((2, 2)),
            sem((2, 12)),
            sem((2, 12)),
            sem((2, 12)),
            sem((2, 12)),
            sem((2,)),
            sem((5,)),
            sem((2, 5)),
        ],
        compiler_params=pltpu.CompilerParams(
            collective_id=1, has_side_effects=True, vmem_limit_bytes=63 * 2**20
        ),
    )(
        flags, lengths, gains, shifts, out_biases, qv_bias, up_bias.reshape(1, -1), tokens, cotangent,
        w_qkv, w_out, w_up, w_down,
    )


STAGE_STEPS = (0, 1, 3, 5, 7, 9, 11, 12)


def braid(own, other, axis):
    cut = partial(lax.slice_in_dim, axis=axis)
    return jnp.concatenate(
        [cut(own, 0, CHUNK), cut(other, 0, CHUNK), cut(own, CHUNK, 2 * CHUNK), cut(other, CHUNK, 2 * CHUNK)], axis=axis
    )


def rear_kernel(
    query_scale,
    act_own,
    act_other,
    slope_own,
    slope_other,
    up_own,
    up_other,
    down_own,
    down_other,
    q_ref,
    k_ref,
    v_ref,
    inv_ref,
    weight_ref,
    w_ref,
    gain_ref,
    front_sums,
    third_in,
    d_down_in,
    cot_in,
    mixed_in,
    first_in,
    tokens_in,
    att_in,
    residual_in,
    w_out_in,
    sums_ref,
    input_out,
    whole,
    grads,
    third_ref,
    d_down_ref,
    cot_ref,
    mixed_ref,
    att_ref,
    residual_ref,
    total,
    out_buf,
    d_up_ref,
    stage_down,
    stage_up,
    ds_ref,
    dqkv_ref,
    up_sums,
    columns_of,
    small_out,
    small_in,
    mine,
    core_in,
    held,
    x_out,
    x_in,
    y_out,
    y_in,
    z_out,
    z_in,
    last,
    take_sem,
    att_sem,
    stage_sem,
    out_sem,
    head_sem,
    end_sem,
    load_sem,
    core_sem,
    x_sem,
    y_sem,
    z_sem,
    zz_sem,
    yy_sem,
    cc_sem,
    keep_sem,
    small_sem,
):
    now = pl.program_id(0)
    place = lax.axis_index("dp")
    turn = lax.axis_index("mp")
    core, side, level = place % 2, (place // 2) % 2, place // 4
    levels = lax.axis_size("dp") // 4
    sibling = {"dp": place + 1 - 2 * core}
    across = {"mp": 1 - turn}
    beside = {"dp": place + 2 - 4 * side}
    floors = [{"dp": (level + step) % levels * 4 + place % 4} for step in range(1, levels)]
    half, piece = CHUNK // 2, CHUNK // 2 // levels
    length, width = total.shape
    pairs = width // (2 * HD)
    units = d_up_ref.shape[1] // 2
    ffs = up_sums.shape[2] // units
    outs = width // 2 // (2 * CHUNK)
    s_mid, s_att = ffs, ffs + 2
    small_at = s_att + 2 * pairs
    first_head = 2 * ffs + outs
    early = first_head + 3
    gap = small_at - 1 - early
    parts = 5
    step = length // parts
    blocks = [pl.ds(start, step) for start in range(0, length, step)]

    def gain(index):
        return gain_ref[index : index + 1, :]

    takes = [
        pltpu.make_async_copy(source, target, take_sem.at[index])
        for index, (source, target) in enumerate(
            (
                (third_in, third_ref),
                (d_down_in, d_down_ref),
                (cot_in, cot_ref),
                (mixed_in, mixed_ref),
                (residual_in, residual_ref),
                (w_out_in, out_buf),
                (first_in, cot_ref),
                (tokens_in, d_down_ref),
            )
        )
    ]

    def take_att(index):
        return pltpu.make_async_copy(att_in.at[blocks[index], :], att_ref.at[index % 2], att_sem.at[index % 2])

    def save_down(chunk):
        return pltpu.make_async_copy(stage_down, grads.at[2 * chunk], stage_sem.at[0])

    def save_up(chunk):
        return pltpu.make_async_copy(stage_up, grads.at[2 * chunk + 1], stage_sem.at[1])

    out_saves = [
        pltpu.make_async_copy(
            out_buf.at[pl.ds(group * width // 2 + (index * 2 + which) * CHUNK, CHUNK), :],
            grads.at[2 * ffs + index, pl.ds((2 * which + group) * CHUNK, CHUNK), :],
            out_sem.at[group, index, which],
        )
        for group in range(2)
        for index in range(outs)
        for which in range(2)
    ]

    def head_saves(turn_of):
        return [
            pltpu.make_async_copy(
                stage_down.at[pl.ds(kind * CHUNK, CHUNK), :],
                grads.at[first_head + turn_of // 4 * 3 + kind, aligned(turn_of % 4 * CHUNK, CHUNK), :],
                head_sem.at[kind],
            )
            for kind in range(3)
        ]

    save_input = pltpu.make_async_copy(residual_ref, input_out, end_sem)

    @pl.when(now == 0)
    def _():
        for copy in takes[:2]:
            copy.start()
        barrier = pltpu.get_barrier_semaphore()
        partners = [sibling, across, beside, *floors]
        for partner in partners:
            pl.semaphore_signal(barrier, inc=1, device_id=partner, device_id_type=MESH)
        pl.semaphore_wait(barrier, len(partners))
        takes[0].wait()
        takes[1].wait()
        for copy in takes[2:6]:
            copy.start()
        take_att(0).start()
        take_att(1).start()

    @pl.when((now >= 1) & (now <= ffs))
    def _():
        save_down(now - 1).wait()

    @pl.when((now >= s_att + 2) & (now <= small_at) & ((now - s_att) % 2 == 0))
    def _():
        for copy in head_saves((now - s_att) // 2 - 1):
            copy.wait()


    def loads(chunk, slot):
        kept = grads.at[chunk, aligned(core * 2 * CHUNK, 2 * CHUNK), :]
        sent = grads.at[chunk, aligned((1 - core) * 2 * CHUNK, 2 * CHUNK), :]
        return [
            pltpu.make_async_copy(kept, mine, load_sem),
            remote(sent, core_in.at[slot], core_sem, (slot,), sibling),
        ]

    def x_copy(slot):
        return remote(x_out.at[slot % 2], x_in.at[slot], x_sem, (slot,), across)

    def y_copy(slot):
        return remote(
            y_out.at[slot % 2, aligned((1 - side) * half, half)], y_in.at[slot], y_sem, (slot,), beside
        )

    def z_copies(slot):
        return [
            remote(
                z_out.at[slot % 2, aligned((level + move) % levels * piece, piece)],
                z_in.at[slot, move - 1],
                z_sem,
                (slot, move - 1),
                floors[move - 1],
            )
            for move in range(1, levels)
        ]

    def target(chunk, first, size):
        return whole.at[aligned((2 * chunk + core) * CHUNK + first, size), :]

    def keep_copies(chunk, slot):
        part = target(chunk, side * half + level * piece, piece)
        copies = [pltpu.make_async_copy(last.at[slot % 2], part, keep_sem.at[slot % 2])]
        for move in range(1, levels):
            copies.append(remote(last.at[slot % 2], part, zz_sem, (slot, move - 1), floors[move - 1]))
        return copies

    def yy_copy(chunk, slot):
        part = target(chunk, side * half, half)
        return remote(part, part, yy_sem, (slot,), beside)

    def cc_copy(chunk, slot):
        part = target(chunk, 0, CHUNK)
        return remote(part, part, cc_sem, (slot,), sibling)

    def stage_7(chunk, slot):
        cc_copy(chunk, slot).wait()

    def stage_6(chunk, slot):
        yy_copy(chunk, slot).wait()
        cc_copy(chunk, slot).start()

    def stage_5(chunk, slot):
        for copy in keep_copies(chunk, slot):
            copy.wait()
        yy_copy(chunk, slot).start()

    def stage_4(chunk, slot):
        for copy in z_copies(slot):
            copy.wait()
        summed = wide(z_out[slot % 2, aligned(level * piece, piece), :])
        for move in range(1, levels):
            summed = summed + wide(z_in[slot, move - 1])
        last[slot % 2] = low(summed)
        for copy in keep_copies(chunk, slot):
            copy.start()

    def stage_3(chunk, slot):
        y_copy(slot).wait()
        z_out[slot % 2] = low(wide(y_out[slot % 2, aligned(side * half, half), :]) + wide(y_in[slot]))
        for copy in z_copies(slot):
            copy.start()

    def stage_2(chunk, slot):
        x_copy(slot).wait()
        y_out[slot % 2] = low(held[slot % 2] + wide(x_in[slot]))
        y_copy(slot).start()

    def stage_1(chunk, slot):
        for copy in loads(chunk, slot):
            copy.wait()
        x_out[slot % 2] = low(wide(mine[CHUNK:]) + wide(core_in[slot, CHUNK:]))
        x_copy(slot).start()
        held[slot % 2] = wide(mine[:CHUNK]) + wide(core_in[slot, :CHUNK])

    def stage_0(chunk, slot):
        for copy in loads(chunk, slot):
            copy.start()

    stages = [stage_0, stage_1, stage_2, stage_3, stage_4, stage_5, stage_6, stage_7]

    def advance(moment):
        for stage in reversed(range(len(stages))):
            spot = moment - 1 - STAGE_STEPS[stage]
            chunk = spot - spot // (early + gap) * gap

            @pl.when(((spot >= 0) & (spot < early)) | ((spot >= early + gap) & (spot < early + gap + 3 * (outs - 1))))
            def _(stage=stage, chunk=chunk):
                stages[stage](chunk, chunk % 4)

    advance(now)


    @pl.when(now < ffs)
    def _():
        act = braid(act_own[...], act_other[...], 1)
        stage_down[...] = low(dot_tn(act, d_down_ref[...]))
        save_down(now).start()
        w_down = braid(down_own[...], down_other[...], 0)
        w_up = braid(up_own[...], up_other[...], 1)
        for part in (pl.ds(0, length // 2), pl.ds(length // 2, length // 2)):
            d_act = dot_nt(d_down_ref[part, :], w_down)
            slope = braid(slope_own[part, :], slope_other[part, :], 1)
            d_up = low(d_act * wide(slope))
            d_up_ref[part, :] = d_up
            update = dot_nt(d_up, w_up)
            total[part, :] = jnp.where(now == 0, update, update + total[part, :])
        sums = column_sum(wide(d_up_ref[...]))
        for group in range(2):
            for which in range(2):
                first = (2 * which + group) * CHUNK
                spot = aligned(now * units + which * CHUNK, CHUNK, 128)
                up_sums[group, 0:1, spot] = sums[:, first : first + CHUNK]

    @pl.when((now >= 1) & (now <= ffs))
    def _():
        save_up(now - 1).wait()

    @pl.when(now < ffs)
    def _():
        stage_up[...] = low(dot_tn(d_up_ref[...], third_ref[...]))
        save_up(now).start()


    @pl.when(now == s_mid)
    def _():
        for copy in takes[2:6]:
            copy.wait()
        sums = [0.0] * 5
        for index, part in enumerate(blocks):
            take_att(index).wait()
            normed_three, scale_three = standardize(residual_ref[part, :])
            normed_two, scale_two = standardize(att_ref[index % 2])
            d_third = total[part, :]
            d_residual = wide(cot_ref[part, :]) + norm_back(d_third, normed_three, scale_three, gain(2))
            residual_ref[part, :] = d_residual
            d_attended = norm_back(d_residual, normed_two, scale_two, gain(1))
            d_down_ref[part, :] = low(d_attended)
            if index + 2 < parts:
                take_att(index + 2).start()
            terms = [d_residual * normed_two, d_third * normed_three, d_residual, d_third, d_attended]
            sums = [old + column_sum(term) for old, term in zip(sums, terms)]
        small_out[...] = front_sums[...]
        for index, row in enumerate((1, 2, 5, 6, 8)):
            small_out[row : row + 1, :] = sums[index]
        takes[6].start()


    @pl.when(now == s_mid + 1)
    def _():
        for part in blocks:
            third_ref[part, :] = low(dot_nt(d_down_ref[part, :], out_buf[...]))
        out_buf[...] = low(dot_tn(mixed_ref[...], d_down_ref[...]))
        for copy in out_saves:
            copy.start()

    @pl.when(now == s_att)
    def _():
        for copy in out_saves:
            copy.wait()
        takes[7].start()
        takes[6].wait()


    @pl.when((now >= s_att) & (now < small_at))
    def _():
        head = (now - s_att) % 2
        turn_of = (now - s_att) // 2
        pair = turn_of % 2 * (pairs // 2) + turn_of // 4 * 2 + turn_of % 4 // 2
        spot = aligned(pair * 2 * HD, 2 * HD, 128)
        lane = lax.broadcasted_iota(jnp.int32, (1, 2 * HD), 1)
        own = (lane // HD) == head
        scaled = wide(third_ref[:, spot]) * inv_ref[...]
        grad = jnp.where(own, scaled * relax_factor, 0.0).astype(jnp.bfloat16)
        inner = jnp.sum(wide(grad) * wide(mixed_ref[:, spot]), axis=1, keepdims=True)
        d_probs = dot_nt(grad, v_ref[...])
        ds_ref[...] = low(wide(weight_ref[0]) * (d_probs - inner))
        dq = low(dot_nn(ds_ref[...], k_ref[...]) * query_scale)
        dk = low(dot_tn(ds_ref[...], q_ref[...]))
        dv = low(dot_tn(weight_ref[0], low(scaled)))
        for index, value in enumerate((dq, dk, dv)):
            part = pl.ds(index * 2 * HD, 2 * HD)
            dqkv_ref[:, part] = jnp.where(own | (head == 0), value, dqkv_ref[:, part])

        @pl.when(head == 1)
        def _():
            d_qkv = dqkv_ref[...]
            stage_down[pl.ds(0, 6 * HD), :] = low(dot_tn(d_qkv, cot_ref[...]))
            for copy in head_saves(turn_of):
                copy.start()
            group, start = pair // (pairs // 2), pair % (pairs // 2) * 2 * HD
            sums = column_sum(wide(d_qkv))
            columns_of[group, 0:1, aligned(start, 2 * HD, 128)] = sums[:, : 2 * HD]
            columns_of[group, 0:1, aligned(width // 2 + start, 2 * HD, 128)] = sums[:, 4 * HD :]
            weights = jnp.concatenate([w_ref[0], w_ref[1], w_ref[2]], axis=1)
            update = dot_nt(d_qkv, weights)

            @pl.when(turn_of == 0)
            def _():
                total[...] = update

            @pl.when(turn_of > 0)
            def _():
                total[...] += update


    @pl.when(now == small_at)
    def _():
        takes[7].wait()
        sums = [0.0, 0.0]
        for part in blocks:
            normed, scale = standardize(wide(d_down_ref[part, :]))
            errors = total[part, :]
            residual_ref[part, :] += norm_back(errors, normed, scale, gain(0))
            sums = [sums[0] + column_sum(errors * normed), sums[1] + column_sum(errors)]
        save_input.start()
        small_out[0:1, :] = sums[0]
        small_out[4:5, :] = sums[1]
        for group in range(2):
            small_out[10 + 3 * group : 11 + 3 * group, :] = columns_of[group, 0:1, :]
            for index in range(2):
                row = 11 + 3 * group + index
                small_out[row : row + 1, :] = up_sums[group, 0:1, index * width : (index + 1) * width]


    def small_copies(stage):
        if stage < 3:
            return [remote(small_out, small_in.at[stage], small_sem, (stage,), (sibling, across, beside)[stage])]
        return [
            remote(small_out, small_in.at[3 + level], small_sem, (2 + move,), floors[move - 1])
            for move in range(1, levels)
        ]

    def small_step_1():
        small_copies(0)[0].wait()
        small_out[...] += small_in[0]
        small_copies(1)[0].start()

    def small_step_2():
        small_copies(1)[0].wait()
        small_out[0:10, :] += small_in[1, 0:10, :]
        small_out[10:13, :] += small_in[1, 13:16, :]
        small_copies(2)[0].start()

    def small_step_3():
        small_copies(2)[0].wait()
        small_out[...] += small_in[2]
        small_in[3 + level] = small_out[...]
        for copy in small_copies(3):
            copy.start()

    def small_step_4():
        for copy in small_copies(3):
            copy.wait()
        summed = small_in[3]
        for index in range(1, levels):
            summed = summed + small_in[3 + index]
        sums_ref[...] = summed


    @pl.when(now == small_at)
    def _():
        small_copies(0)[0].start()

        @pl.loop(small_at + 1, small_at + 3 * (outs - 1) + STAGE_STEPS[-1])
        def _(moment):
            advance(moment)
            for index, small_step in enumerate((small_step_1, small_step_2, small_step_3, small_step_4)):
                pl.when(moment == small_at + 1 + 2 * index)(small_step)

        save_input.wait()


def rear(
    acts, slopes, w_up, w_down, queries, keys, values, inv, weights, w_qkv, gains, sums, third, d_down, cotangent, mixed,
    first, tokens, attended, residual, w_out, query_scale,
):
    length, width = queries.shape
    pairs = width // (2 * HD)
    ff = w_up.shape[1]
    units = 2 * CHUNK
    ffs = ff // 2 // units
    outs = width // 2 // units
    levels = lax.axis_size("dp") // 4
    half, piece = CHUNK // 2, CHUNK // 2 // levels
    s_att = ffs + 2
    small_at = s_att + 2 * pairs
    chunks = 2 * ffs + outs + 3 * outs
    kind, sem = jnp.bfloat16, pltpu.SemaphoreType.DMA

    def pair_of(i):
        turn_of = jnp.clip(i - s_att, 0, 2 * pairs - 1) // 2
        return turn_of % 2 * (pairs // 2) + turn_of // 4 * 2 + turn_of % 4 // 2

    def head_of(i):
        return pair_of(i) * 2 + jnp.clip(i - s_att, 0, 2 * pairs - 1) % 2

    def fixed(shape):
        return pl.BlockSpec(shape, lambda i: (0,) * len(shape), pipeline_mode=pl.Buffered(1))

    def unit_of(i):
        return jnp.minimum(i, ffs - 1)

    def lanes(rows):
        return [
            pl.BlockSpec((rows, units), lambda i: (0, unit_of(i))),
            pl.BlockSpec((rows, units), lambda i: (0, ffs + unit_of(i))),
        ]

    column = pl.BlockSpec((length, 2 * HD), lambda i: (0, pair_of(i)))
    hbm = pl.BlockSpec(memory_space=pl.ANY)
    return pl.pallas_call(
        partial(rear_kernel, query_scale),
        grid=(small_at + 1,),
        in_specs=[
            *lanes(length),
            *lanes(length),
            *lanes(width),
            pl.BlockSpec((units, width), lambda i: (unit_of(i), 0)),
            pl.BlockSpec((units, width), lambda i: (ffs + unit_of(i), 0)),
            *[column] * 4,
            pl.BlockSpec((1, length, length), lambda i: (head_of(i), 0, 0)),
            pl.BlockSpec((3, width, 2 * HD), lambda i: (0, 0, pair_of(i))),
            fixed((4, width)),
            fixed((16, width)),
            *[hbm] * 9,
        ],
        out_specs=[fixed((16, width)), hbm, hbm, hbm],
        out_shape=[
            jax.ShapeDtypeStruct((16, width), jnp.float32),
            jax.ShapeDtypeStruct((length, width), jnp.float32),
            jax.ShapeDtypeStruct((chunks * 2 * CHUNK, width), kind),
            jax.ShapeDtypeStruct((chunks, 4 * CHUNK, width), kind),
        ],
        scratch_shapes=[
            *[pltpu.VMEM((length, width), kind)] * 4,
            pltpu.VMEM((2, length // 5, width), jnp.float32),
            pltpu.VMEM((length, width), jnp.float32),
            pltpu.VMEM((length, width), jnp.float32),
            pltpu.VMEM((width, width), kind),
            pltpu.VMEM((length, 2 * units), kind),
            pltpu.VMEM((4 * CHUNK, width), kind),
            pltpu.VMEM((4 * CHUNK, width), kind),
            pltpu.VMEM((length, length), kind),
            pltpu.VMEM((length, 6 * HD), kind),
            pltpu.VMEM((2, 8, ff // 2), jnp.float32),
            pltpu.VMEM((2, 8, width), jnp.float32),
            pltpu.VMEM((16, width), jnp.float32),
            pltpu.VMEM((3 + levels, 16, width), jnp.float32),
            pltpu.VMEM((2 * CHUNK, width), kind),
            pltpu.VMEM((4, 2 * CHUNK, width), kind),
            pltpu.VMEM((2, CHUNK, width), jnp.float32),
            pltpu.VMEM((2, CHUNK, width), kind),
            pltpu.VMEM((4, CHUNK, width), kind),
            pltpu.VMEM((2, CHUNK, width), kind),
            pltpu.VMEM((4, half, width), kind),
            pltpu.VMEM((2, half, width), kind),
            pltpu.VMEM((4, levels - 1, piece, width), kind),
            pltpu.VMEM((2, piece, width), kind),
            sem((8,)),
            sem((2,)),
            sem((2,)),
            sem((2, outs, 2)),
            sem((3,)),
            sem,
            sem,
            sem((2, 4)),
            sem((2, 4)),
            sem((2, 4)),
            sem((2, 4, levels - 1)),
            sem((2, 4, levels - 1)),
            sem((2, 4)),
            sem((2, 4)),
            sem((2,)),
            sem((2, 2 + levels)),
        ],
        compiler_params=pltpu.CompilerParams(
            collective_id=0, has_side_effects=True, vmem_limit_bytes=63 * 2**20
        ),
    )(
        acts, acts, slopes, slopes, w_up, w_up, w_down, w_down, queries, keys, values, inv, weights, w_qkv, gains, sums,
        third, d_down, cotangent, mixed, first, tokens, attended, residual, w_out,
    )[:3]


def unpack_kernel(
    ffs,
    outs,
    whole_ref,
    grad_ref,
    result_ref,
    sums_ref,
    down_ref,
    up_ref,
    out_ref,
    qkv_ref,
    input_ref,
    output_ref,
    gains_ref,
    shifts_ref,
    outer_ref,
    qv_ref,
    bias_ref,
):
    now = pl.program_id(0)
    value = wide(whole_ref[...])

    @pl.when(now < 5)
    def _():
        input_ref[...] = grad_ref[...]
        output_ref[...] = result_ref[...]

    @pl.when(now == 0)
    def _():
        width = sums_ref.shape[1]
        gains_ref[...] = sums_ref[0:4, :]
        shifts_ref[...] = sums_ref[4:8, :]
        outer_ref[...] = sums_ref[8:10, :]
        for index in range(2):
            qv_ref[index : index + 1, :] = sums_ref[10:11, index * width // 2 : (index + 1) * width // 2]
            bias_ref[:, index * width : (index + 1) * width] = sums_ref[11 + index : 12 + index, :]

    @pl.when((now < 2 * ffs) & (now % 2 == 0))
    def _():
        down_ref[...] = value

    @pl.when((now < 2 * ffs) & (now % 2 == 1))
    def _():
        up_ref[...] = value.T

    @pl.when((now >= 2 * ffs) & (now < 2 * ffs + outs))
    def _():
        out_ref[...] = value

    @pl.when(now >= 2 * ffs + outs)
    def _():
        qkv_ref[0] = value.T


def unpack(whole, grad_input, result, sums, ff):
    length, width = result.shape
    units = 2 * CHUNK
    ffs = ff // 2 // units
    outs = width // 2 // units
    first_head = 2 * ffs + outs

    def head_turn(i):
        return jnp.maximum(i - first_head, 0)

    def fixed(*shape):
        return pl.BlockSpec(shape, lambda i: (0,) * len(shape), pipeline_mode=pl.Buffered(1))

    rows = pl.BlockSpec((length // 5, width), lambda i: (jnp.minimum(i, 4), 0))

    def wide_like(*shape):
        return jax.ShapeDtypeStruct(shape, jnp.float32)

    return pl.pallas_call(
        partial(unpack_kernel, ffs, outs),
        grid=(first_head + 3 * outs,),
        in_specs=[pl.BlockSpec((units, width), lambda i: (i, 0)), rows, rows, fixed(16, width)],
        out_specs=[
            pl.BlockSpec((units, width), lambda i: (jnp.minimum(i // 2, ffs - 1), 0)),
            pl.BlockSpec((width, units), lambda i: (0, jnp.minimum(i // 2, ffs - 1))),
            pl.BlockSpec((units, width), lambda i: (jnp.clip(i - 2 * ffs, 0, outs - 1), 0)),
            pl.BlockSpec((1, width, units), lambda i: (head_turn(i) % 3, 0, head_turn(i) // 3)),
            rows,
            rows,
            fixed(4, width),
            fixed(4, width),
            fixed(2, width),
            fixed(2, width // 2),
            fixed(1, ff // 2),
        ],
        out_shape=[
            wide_like(ff // 2, width),
            wide_like(width, ff // 2),
            wide_like(width // 2, width),
            wide_like(3, width, width // 2),
            wide_like(length, width),
            jax.ShapeDtypeStruct((length, width), jnp.bfloat16),
            wide_like(4, width),
            wide_like(4, width),
            wide_like(2, width),
            wide_like(2, width // 2),
            wide_like(1, ff // 2),
        ],
        compiler_params=pltpu.CompilerParams(vmem_limit_bytes=48 * 2**20),
    )(whole, grad_input, result, sums)


def sequence_shards(
    tokens,
    cond_flags,
    seg_lengths,
    norm_gains,
    norm_biases,
    w_qkv,
    qv_bias,
    w_out,
    out_biases,
    w_up,
    up_bias,
    w_down,
    cotangent,
):
    width = tokens.shape[1]
    query_scale = 1.0 / (relax_factor * math.sqrt(HD))
    (
        queries, keys, values, inv, kept, acts, slopes, small, first_in, mixed, attended, residual, third_in, result,
        d_down, all_qkv, all_out, all_up, all_down,
    ) = front(
        cond_flags, seg_lengths, tokens, cotangent, norm_gains, norm_biases, out_biases, qv_bias, up_bias,
        w_qkv, w_out, w_up, w_down, query_scale,
    )
    sums, grad_input, whole = rear(
        acts, slopes, all_up, all_down, queries, keys, values, inv, kept, all_qkv, norm_gains, small, third_in, d_down,
        cotangent, mixed, first_in, tokens, attended, residual, all_out, query_scale,
    )
    (
        grad_w_down, grad_w_up, grad_w_out, grad_w_qkv, grad_input, result, grad_gains, grad_shifts, grad_outer, grad_qv,
        grad_up_bias,
    ) = unpack(whole, grad_input, result, sums, all_up.shape[1])
    return (
        result,
        grad_input,
        grad_gains,
        grad_shifts,
        grad_w_qkv,
        grad_qv,
        grad_w_out,
        grad_outer,
        grad_w_up,
        grad_up_bias.reshape(-1),
        grad_w_down,
    )


def solution(mesh):
    in_specs = (
        P(("dp", "mp"), None),
        P("dp", None),
        P("dp", None),
        P(),
        P(),
        P(None, None, "mp"),
        P(None, "mp"),
        P("mp", None),
        P(),
        P(None, "mp"),
        P("mp"),
        P("mp", None),
        P(("dp", "mp"), None),
    )
    out_specs = (
        P(("dp", "mp"), None),
        P(("dp", "mp"), None),
        P(),
        P(),
        P(None, None, "mp"),
        P(None, "mp"),
        P("mp", None),
        P(),
        P(None, "mp"),
        P("mp"),
        P("mp", None),
    )
    per_device = mesh.shape["dp"] * mesh.shape["mp"]

    def step(*args):
        whole_sequences = args[1].shape[0] == per_device
        local = sequence_shards if whole_sequences and mesh.shape["mp"] == 2 and mesh.shape["dp"] == 16 else shards
        return jax.shard_map(
            local, mesh=mesh, in_specs=in_specs, out_specs=out_specs, check_vma=False
        )(*args)

    return step
```

```python
from functools import partial
import math

import jax
import jax.numpy as jnp
from jax import lax
from jax.experimental import pallas as pl
from jax.experimental.pallas import tpu as pltpu
from jax.sharding import PartitionSpec as P

HD = 64


epsilon = 1e-05
relax_factor = 32.0


def standardize(entries):
    average = jnp.mean(entries, axis=-1, keepdims=True)
    centred = entries - average
    spread = jnp.mean(centred * centred, axis=-1, keepdims=True)
    inv_std = lax.rsqrt(spread + epsilon)
    return (centred * inv_std, inv_std)


def norm_back(grad_in, normed, inv_std, gain_row):
    weighted = grad_in * gain_row
    return inv_std * (
        weighted
        - jnp.mean(weighted, axis=-1, keepdims=True)
        - normed * jnp.mean(weighted * normed, axis=-1, keepdims=True)
    )


def token_marks(seg_flags, lengths, length):
    position = jnp.arange(length, dtype=jnp.int32)
    segment = (position >= lengths[0]).astype(jnp.int32) + (
        position >= lengths[0] + lengths[1]
    ).astype(jnp.int32)
    segment_hits = (segment[:, None] == jnp.arange(3, dtype=jnp.int32)[None, :]).astype(jnp.int32)
    return jnp.sum(segment_hits * seg_flags[None, :], axis=1)


def block_mask(marks_seq, first_row, block_rows, length):
    query_places = first_row + jnp.arange(block_rows, dtype=jnp.int32)
    key_places = jnp.arange(length, dtype=jnp.int32)
    return (key_places[None, :] <= query_places[:, None]) | (marks_seq[None, :] == 1)


def shards(
    tokens,
    cond_flags,
    seg_lengths,
    norm_gains,
    norm_biases,
    w_qkv,
    qv_bias,
    w_out,
    out_biases,
    w_up,
    up_bias,
    w_down,
    cotangent,
):
    shard_rows = tokens.shape[0]
    group_rows = shard_rows * lax.axis_size("mp")
    seq_count = cond_flags.shape[0]
    length = group_rows // seq_count
    block_rows = length // 2
    head_count = w_qkv.shape[2] // HD
    local_width = head_count * HD
    query_scale = 1.0 / (relax_factor * math.sqrt(HD))
    all_marks = jax.vmap(lambda seg_flags, lengths: token_marks(seg_flags, lengths, length))(
        cond_flags, seg_lengths
    )
    numbers = jnp.arange(seq_count * 2, dtype=jnp.int32)
    source = tokens.astype(jnp.float32)
    normed_one, scale_one = standardize(source)
    first_in = (normed_one * norm_gains[0] + norm_biases[0]).astype(jnp.bfloat16)
    first_all = lax.all_gather(first_in, "mp", axis=0, tiled=True)
    bias_rows = jnp.stack([qv_bias[0], jnp.zeros_like(qv_bias[0]), qv_bias[1]])
    projected = (
        jnp.einsum("td,cde->cte", first_all, w_qkv, preferred_element_type=jnp.float32)
        + bias_rows[:, None, :]
    )
    queries = (
        (projected[0] * query_scale)
        .astype(jnp.bfloat16)
        .reshape(seq_count * 2, block_rows, head_count, HD)
    )
    key_all = projected[1].astype(jnp.bfloat16).reshape(seq_count, length, head_count, HD)
    value_all = projected[2].astype(jnp.bfloat16).reshape(seq_count, length, head_count, HD)

    def block_probs(query_block, number, row_top, row_total):
        sequence = number // 2
        first_row = number % 2 * block_rows
        key_seq = lax.dynamic_index_in_dim(key_all, sequence, 0, keepdims=False)
        allowed = block_mask(
            lax.dynamic_index_in_dim(all_marks, sequence, 0, keepdims=False),
            first_row,
            block_rows,
            length,
        )
        scores = jnp.einsum(
            "qhd,khd->hqk", query_block, key_seq, preferred_element_type=jnp.float32
        )
        if row_top is None:
            row_top = jnp.max(jnp.where(allowed[None], scores, -1e30), axis=-1, keepdims=True)
        weights = jnp.exp(jnp.where(allowed[None], (scores - row_top) * relax_factor, -30000.0))
        if row_total is None:
            row_total = jnp.sum(weights, axis=-1, keepdims=True)
        return (weights / row_total, row_top, row_total, key_seq)

    def forward_block(block_item):
        query_block, number = block_item
        probs, row_top, row_total, key_seq = block_probs(query_block, number, None, None)
        value_seq = lax.dynamic_index_in_dim(value_all, number // 2, 0, keepdims=False)
        mixed_block = jnp.einsum(
            "hqk,khd->qhd",
            probs.astype(jnp.bfloat16),
            value_seq,
            preferred_element_type=jnp.float32,
        )
        return (mixed_block.astype(jnp.bfloat16), row_top, row_total)

    mixed_heads, row_tops, row_totals = lax.map(forward_block, (queries, numbers))
    mixed_heads = mixed_heads.reshape(group_rows, local_width)
    attended = (
        lax.psum_scatter(
            jnp.dot(mixed_heads, w_out, preferred_element_type=jnp.float32),
            "mp",
            scatter_dimension=0,
            tiled=True,
        )
        + out_biases[0]
    )
    normed_two, scale_two = standardize(attended)
    residual = source + normed_two * norm_gains[1] + norm_biases[1]
    normed_three, scale_three = standardize(residual)
    third_in = (normed_three * norm_gains[2] + norm_biases[2]).astype(jnp.bfloat16)
    third_all = lax.all_gather(third_in, "mp", axis=0, tiled=True)
    up_value = jnp.dot(third_all, w_up, preferred_element_type=jnp.float32) + up_bias
    activated = jax.nn.gelu(up_value, approximate=True).astype(jnp.bfloat16)
    down = (
        lax.psum_scatter(
            jnp.dot(activated, w_down, preferred_element_type=jnp.float32),
            "mp",
            scatter_dimension=0,
            tiled=True,
        )
        + out_biases[1]
    )
    normed_four, scale_four = standardize(down)
    result = (residual + normed_four * norm_gains[3] + norm_biases[3]).astype(jnp.bfloat16)
    grad_out = cotangent.astype(jnp.float32)
    d_down = norm_back(grad_out, normed_four, scale_four, norm_gains[3])
    d_down_low = d_down.astype(jnp.bfloat16)
    d_down_all = lax.all_gather(d_down_low, "mp", axis=0, tiled=True)
    d_act = jnp.einsum("td,fd->tf", d_down_all, w_down, preferred_element_type=jnp.float32)
    grad_w_down = jnp.einsum("tf,td->fd", activated, d_down_all, preferred_element_type=jnp.float32)
    gelu_value, gelu_pull = jax.vjp(partial(jax.nn.gelu, approximate=True), up_value)
    d_up = gelu_pull(d_act)[0].astype(jnp.bfloat16)
    grad_w_up = jnp.einsum("td,tf->df", third_all, d_up, preferred_element_type=jnp.float32)
    grad_up_bias = jnp.sum(d_up, axis=0, dtype=jnp.float32)
    d_third = lax.psum_scatter(
        jnp.einsum("tf,df->td", d_up, w_up, preferred_element_type=jnp.float32),
        "mp",
        scatter_dimension=0,
        tiled=True,
    )
    d_residual = grad_out + norm_back(d_third, normed_three, scale_three, norm_gains[2])
    d_attended = norm_back(d_residual, normed_two, scale_two, norm_gains[1])
    d_att_low = d_attended.astype(jnp.bfloat16)
    d_att_all = lax.all_gather(d_att_low, "mp", axis=0, tiled=True)
    d_mixed = jnp.einsum("td,hd->th", d_att_all, w_out, preferred_element_type=jnp.float32).astype(
        jnp.bfloat16
    )
    grad_w_out = jnp.einsum("th,td->hd", mixed_heads, d_att_all, preferred_element_type=jnp.float32)
    d_mixed_blocks = d_mixed.reshape(seq_count * 2, block_rows, head_count, HD)

    def backward_block(block_item):
        query_block, d_block, row_top, row_total, number = block_item
        probs, kept_top, kept_total, key_seq = block_probs(query_block, number, row_top, row_total)
        value_seq = lax.dynamic_index_in_dim(value_all, number // 2, 0, keepdims=False)
        d_probs = jnp.einsum("qhd,khd->hqk", d_block, value_seq, preferred_element_type=jnp.float32)
        inner = jnp.sum(probs * d_probs, axis=-1, keepdims=True)
        d_scores = (relax_factor * probs * (d_probs - inner)).astype(jnp.bfloat16)
        d_query = (
            jnp.einsum("hqk,khd->qhd", d_scores, key_seq, preferred_element_type=jnp.float32)
            * query_scale
        )
        d_key = jnp.einsum(
            "hqk,qhd->khd", d_scores, query_block, preferred_element_type=jnp.float32
        )
        d_value = jnp.einsum(
            "hqk,qhd->khd", probs.astype(jnp.bfloat16), d_block, preferred_element_type=jnp.float32
        )
        return (d_query.astype(jnp.bfloat16), d_key, d_value)

    d_queries, d_keys, d_values = lax.map(
        backward_block, (queries, d_mixed_blocks, row_tops, row_totals, numbers)
    )
    d_keys = jnp.sum(d_keys.reshape(seq_count, 2, length, local_width), axis=1).reshape(
        group_rows, local_width
    )
    d_values = jnp.sum(d_values.reshape(seq_count, 2, length, local_width), axis=1).reshape(
        group_rows, local_width
    )
    d_qkv = jnp.stack(
        [
            d_queries.reshape(group_rows, local_width),
            d_keys.astype(jnp.bfloat16),
            d_values.astype(jnp.bfloat16),
        ]
    )
    grad_w_qkv = jnp.einsum("td,cte->cde", first_all, d_qkv, preferred_element_type=jnp.float32)
    grad_qv_bias = jnp.stack(
        [jnp.sum(d_qkv[0], axis=0, dtype=jnp.float32), jnp.sum(d_qkv[2], axis=0, dtype=jnp.float32)]
    )
    d_first = lax.psum_scatter(
        jnp.einsum("cte,cde->td", d_qkv, w_qkv, preferred_element_type=jnp.float32).astype(
            jnp.bfloat16
        ),
        "mp",
        scatter_dimension=0,
        tiled=True,
    ).astype(jnp.float32)
    grad_input = d_residual + norm_back(d_first, normed_one, scale_one, norm_gains[0])
    error_terms = (d_first, d_residual, d_third, grad_out)
    normed_terms = (normed_one, normed_two, normed_three, normed_four)
    gain_sums = jnp.stack(
        [
            jnp.sum(error_term * normed_term, axis=0)
            for error_term, normed_term in zip(error_terms, normed_terms)
        ]
    )
    bias_sums = jnp.stack([jnp.sum(error_term, axis=0) for error_term in error_terms])
    outer_sums = jnp.stack([jnp.sum(d_attended, axis=0), jnp.sum(d_down, axis=0)])
    gain_sums, bias_sums, outer_sums = lax.psum((gain_sums, bias_sums, outer_sums), ("dp", "mp"))
    grad_w_qkv, grad_qv_bias, grad_w_out, grad_w_up, grad_up_bias, grad_w_down = (
        lax.psum(grad_w_qkv.astype(jnp.bfloat16), "dp").astype(jnp.float32),
        lax.psum(grad_qv_bias.astype(jnp.bfloat16), "dp").astype(jnp.float32),
        lax.psum(grad_w_out.astype(jnp.bfloat16), "dp").astype(jnp.float32),
        lax.psum(grad_w_up.astype(jnp.bfloat16), "dp").astype(jnp.float32),
        lax.psum(grad_up_bias.astype(jnp.bfloat16), "dp").astype(jnp.float32),
        lax.psum(grad_w_down.astype(jnp.bfloat16), "dp").astype(jnp.float32),
    )
    return (
        result,
        grad_input,
        gain_sums,
        bias_sums,
        grad_w_qkv,
        grad_qv_bias,
        grad_w_out,
        outer_sums,
        grad_w_up,
        grad_up_bias,
        grad_w_down,
    )


LOG2E = 1.4426950408889634
HIDDEN = -1e30


def dot_nt(a, b):
    return lax.dot_general(a, b, (((1,), (1,)), ((), ())), preferred_element_type=jnp.float32)


def dot_nn(a, b):
    return lax.dot_general(a, b, (((1,), (0,)), ((), ())), preferred_element_type=jnp.float32)


def dot_tn(a, b):
    return lax.dot_general(a, b, (((0,), (0,)), ((), ())), preferred_element_type=jnp.float32)


def low(value):
    return value.astype(jnp.bfloat16)


MESH = pl.DeviceIdType.MESH
CHUNK = 128


def remote(source, target, sems, index, device):
    return pltpu.make_async_remote_copy(
        src_ref=source,
        dst_ref=target,
        send_sem=sems.at[(0, *index)],
        recv_sem=sems.at[(1, *index)],
        device_id=device,
        device_id_type=MESH,
    )


def aligned(start, size, unit=16):
    return pl.ds(pl.multiple_of(start, unit), size)


def wide(value):
    return value.astype(jnp.float32)


GELU_SCALE = math.sqrt(2.0 / math.pi)
GELU_CUBE = 0.044715


def gelu_both(up):
    square = up * up
    half = 0.5 * jnp.tanh(up * (GELU_SCALE + GELU_SCALE * GELU_CUBE * square)) + 0.5
    value = up * half
    slope = half + value * (1.0 - half) * (2.0 * GELU_SCALE + 6.0 * GELU_SCALE * GELU_CUBE * square)
    return value, slope


def column_sum(value):
    return jnp.sum(value, axis=0, keepdims=True)


def front_kernel(
    query_scale,
    events,
    flags_ref,
    lengths_ref,
    gain_ref,
    shift_ref,
    out_bias_ref,
    qv_bias_ref,
    up_bias_ref,
    tokens_in,
    cot_in,
    own_qkv,
    own_out,
    own_up,
    own_down,
    q_ref,
    k_ref,
    v_ref,
    inv_ref,
    weight_ref,
    act_ref,
    slope_ref,
    small_ref,
    first_out,
    mixed_out,
    att_out,
    residual_out,
    third_out,
    result_out,
    d_down_out,
    all_qkv,
    all_out,
    all_up,
    all_down,
    first_ref,
    mixed_ref,
    tokens_ref,
    third_ref,
    att_ref,
    residual_ref,
    total,
    qkv_buf,
    out_buf,
    up_buf,
    down_buf,
    hide_ref,
    qv_all,
    up_bias_all,
    qkv_load,
    out_load,
    up_load,
    down_load,
    qkv_keep,
    out_keep,
    up_keep,
    down_keep,
    bias_sem,
    x_sem,
    y_sem,
    z_sem,
    c_sem,
    in_sem,
    save_sem,
    end_sem,
):
    now = pl.program_id(0)
    place = lax.axis_index("dp")
    turn = lax.axis_index("mp")
    core, side, odd = place % 2, (place // 2) % 2, place // 4 % 2
    above = {"dp": place + 4 - 8 * odd}
    sibling = {"dp": place + 1 - 2 * core}
    across = {"mp": 1 - turn}
    beside = {"dp": place + 2 - 4 * side}
    length, width = tokens_ref.shape
    pairs = width // (2 * HD)
    size = act_ref.shape[1]
    ff = all_up.shape[1]
    chunks = ff // size
    mid = pairs
    end = mid + chunks + 1
    parts = 5
    step = length // parts
    blocks = [pl.ds(start, step) for start in range(0, length, step)]

    def gain(index):
        return gain_ref[index : index + 1, :]

    def shift(index):
        return shift_ref[index : index + 1, :]


    q_qkv, q_out, q_up, q_down = width // 8, width // 8, ff // 8, ff // 8
    row_up = width // 4

    def places(index, quarter, count, narrow):
        if index < 3:
            cols = aligned(quarter * q_qkv, count * q_qkv, 128)
            far = aligned(width // 2 + quarter * q_qkv, count * q_qkv, 128)
            return own_qkv.at[index, :, cols], all_qkv.at[index, :, far]
        if index < 4:
            rows = aligned(quarter * q_out, count * q_out)
            return own_out.at[rows, :], all_out.at[aligned(width // 2 + quarter * q_out, count * q_out), :]
        first, span = (index - 4) % 4 * row_up, row_up
        if narrow:
            first, span = first + odd * (row_up // 2), row_up // 2
        if index < 8:
            rows = aligned(first, span)
            cols = aligned(quarter * q_up, count * q_up, 128)
            return own_up.at[rows, cols], all_up.at[rows, aligned(ff // 2 + quarter * q_up, count * q_up, 128)]
        cols = aligned(first, span, 128)
        rows = aligned(quarter * q_down, count * q_down)
        return own_down.at[rows, cols], all_down.at[aligned(ff // 2 + quarter * q_down, count * q_down), cols]

    def hop(index, stage):
        narrow = FLOORED[0] <= index < FLOORED[1]
        if stage == 0:
            source, target = places(index, 2 * core + side, 1, narrow)
            return remote(source, target, x_sem, (index,), across)
        if stage == 1:
            part = places(index, 2 * core + side, 1, narrow)[1]
            return remote(part, part, y_sem, (index,), beside)
        part = places(index, 2 * core, 2, narrow and stage == 2)[1]
        if narrow and stage == 2:
            return remote(part, part, z_sem, (index,), above)
        return remote(part, part, c_sem, (index,), sibling)

    bias_copies = [
        remote(qv_bias_ref, qv_all.at[1], bias_sem, (0,), across),
        remote(up_bias_ref, up_bias_all.at[1], bias_sem, (1,), across),
    ]
    def load_pair(pair, ref):
        start = pair % (pairs // 2) * 2 * HD if ref is own_qkv else pair * 2 * HD
        return pltpu.make_async_copy(
            ref.at[:, :, aligned(start, 2 * HD, 128)], qkv_buf.at[pair % 2], qkv_load.at[pair % 2]
        )

    def load_chunk(chunk, up, down):
        slot = chunk % 2
        return [
            pltpu.make_async_copy(up.at[:, aligned(chunk * size, size, 128)], up_buf.at[slot], up_load.at[slot]),
            pltpu.make_async_copy(down.at[aligned(chunk * size, size), :], down_buf.at[slot], down_load.at[slot]),
        ]

    out_loads = [
        pltpu.make_async_copy(
            own_out, out_buf.at[pl.ds(0, width // 2), :], out_load.at[0]
        ),
        pltpu.make_async_copy(
            all_out.at[pl.ds(width // 2, width // 2), :], out_buf.at[pl.ds(width // 2, width // 2), :], out_load.at[1]
        ),
    ]

    def keep_pair(pair):
        return pltpu.make_async_copy(
            qkv_buf.at[pair % 2], all_qkv.at[:, :, aligned(pair * 2 * HD, 2 * HD, 128)], qkv_keep.at[pair % 2]
        )

    def keep_chunk(chunk):
        slot = chunk % 2
        return [
            pltpu.make_async_copy(up_buf.at[slot], all_up.at[:, aligned(chunk * size, size, 128)], up_keep.at[slot]),
            pltpu.make_async_copy(down_buf.at[slot], all_down.at[aligned(chunk * size, size), :], down_keep.at[slot]),
        ]

    keep_out = pltpu.make_async_copy(
        out_buf.at[pl.ds(0, width // 2), :], all_out.at[pl.ds(0, width // 2), :], out_keep
    )
    take_tokens = pltpu.make_async_copy(tokens_in, tokens_ref, in_sem.at[0])
    take_cot = pltpu.make_async_copy(cot_in, first_ref, in_sem.at[1])
    save_first = pltpu.make_async_copy(first_ref, first_out, save_sem.at[0])
    saves = [
        pltpu.make_async_copy(mixed_ref, mixed_out, save_sem.at[1]),
        pltpu.make_async_copy(att_ref, att_out, save_sem.at[2]),
        pltpu.make_async_copy(residual_ref, residual_out, save_sem.at[3]),
        pltpu.make_async_copy(third_ref, third_out, save_sem.at[4]),
    ]

    def end_copies(index):
        part = blocks[index]
        return [
            pltpu.make_async_copy(tokens_ref.at[part, :], result_out.at[part, :], end_sem.at[0, index]),
            pltpu.make_async_copy(mixed_ref.at[part, :], d_down_out.at[part, :], end_sem.at[1, index]),
        ]

    def run_events(slot):
        for index, stage in events.get(slot, []):
            hops = 4 if FLOORED[0] <= index < FLOORED[1] else 3
            if stage > 0:
                hop(index, stage - 1).wait()
            if stage < hops:
                hop(index, stage).start()

    @pl.when(now == 0)
    def _():
        take_tokens.start()
        load_pair(0, own_qkv).start()
        barrier = pltpu.get_barrier_semaphore()
        partners = [sibling, across, beside, above]
        for partner in partners:
            pl.semaphore_signal(barrier, inc=1, device_id=partner, device_id_type=MESH)
        pl.semaphore_wait(barrier, len(partners))
        for copy in bias_copies:
            copy.start()

    for moment in range(end):

        @pl.when(now == moment)
        def _(moment=moment):
            run_events(2 * moment if moment < mid else moment + mid)

    @pl.when(now == 0)
    def _():
        qv_all[0] = qv_bias_ref[...]
        up_bias_all[0] = up_bias_ref[...]
        spots = lax.broadcasted_iota(jnp.int32, (1, length), 1)
        one = lengths_ref[turn, 0]
        two = one + lengths_ref[turn, 1]
        marks = jnp.where(
            spots < one, flags_ref[turn, 0], jnp.where(spots < two, flags_ref[turn, 1], flags_ref[turn, 2])
        )
        hide_ref[...] = jnp.where(marks == 1, 0.0, HIDDEN)
        take_tokens.wait()
        for part in blocks:
            normed, _ = standardize(wide(tokens_ref[part, :]))
            first_ref[part, :] = low(normed * gain(0) + shift(0))
        save_first.start()

    @pl.when(now == pairs // 2)
    def _():
        bias_copies[0].wait()

    @pl.when(now == mid)
    def _():
        bias_copies[1].wait()


    def attend_head(head):
        lane = lax.broadcasted_iota(jnp.int32, (1, 2 * HD), 1)
        own = (lane // HD) == head
        keys = k_ref[...]
        values = jnp.where(own, v_ref[...], jnp.ones((1, 2 * HD), jnp.bfloat16))
        rows = length // 2
        spot = aligned(now * 2 * HD, 2 * HD, 128)
        for start in (0, rows):
            part = pl.ds(start, rows)
            mine = jnp.where(own, q_ref[part, :], jnp.zeros((1, 2 * HD), jnp.bfloat16))
            scores = dot_nt(mine, keys)
            query_places = lax.broadcasted_iota(jnp.int32, (rows, length), 0) + start
            key_places = lax.broadcasted_iota(jnp.int32, (rows, length), 1)
            scores = scores + jnp.where(key_places <= query_places, 0.0, hide_ref[...])
            top = jnp.max(scores, axis=1, keepdims=True)
            kept = low(jnp.exp2((scores - top) * (relax_factor * LOG2E)))
            weight_ref[head, part, :] = kept
            mixed = dot_nn(kept, values)
            inv = 1.0 / pltpu.roll(mixed, HD, 1)
            out = low(mixed * inv)
            mixed_ref[part, spot] = out if head == 0 else jnp.where(own, out, mixed_ref[part, spot])
            inv_ref[part, :] = inv if head == 0 else jnp.where(own, inv, inv_ref[part, :])

    @pl.when(now < mid)
    def _():
        pair = now
        load_pair(pair, all_qkv).wait()
        group, start = pair // (pairs // 2), pair % (pairs // 2) * 2 * HD
        parts_of = qkv_buf[pair % 2]
        projected = dot_nn(first_ref[...], jnp.concatenate([parts_of[0], parts_of[1], parts_of[2]], axis=1))
        bias_q = qv_all[group, 0:1, aligned(start, 2 * HD, 128)]
        bias_v = qv_all[group, 1:2, aligned(start, 2 * HD, 128)]
        q_ref[...] = low((projected[:, : 2 * HD] + bias_q) * query_scale)
        k_ref[...] = low(projected[:, 2 * HD : 4 * HD])
        v_ref[...] = low(projected[:, 4 * HD :] + bias_v)

    @pl.when(now < pairs // 2)
    def _():
        keep_pair(now).start()

    @pl.when(now < mid)
    def _():
        attend_head(0)

    for moment in range(mid):

        @pl.when(now == moment)
        def _(moment=moment):
            run_events(2 * moment + 1)

    @pl.when((now >= 1) & (now <= pairs // 2))
    def _():
        keep_pair(now - 1).wait()

    @pl.when(now < pairs // 2 - 1)
    def _():
        load_pair(now + 1, own_qkv).start()

    @pl.when((now >= pairs // 2 - 1) & (now < mid - 1))
    def _():
        load_pair(now + 1, all_qkv).start()

    @pl.when(now == mid - 1)
    def _():
        for copy in out_loads:
            copy.start()

    @pl.when(now < mid)
    def _():
        attend_head(1)

    @pl.when(now == mid)
    def _():
        for copy in load_chunk(0, own_up, own_down):
            copy.start()
        save_first.wait()
        take_cot.start()
        for copy in out_loads:
            copy.wait()
        keep_out.start()
        for part in blocks:
            attended = dot_nn(mixed_ref[part, :], out_buf[...]) + out_bias_ref[0:1, :]
            att_ref[part, :] = attended
            normed_two, _ = standardize(attended)
            residual = wide(tokens_ref[part, :]) + normed_two * gain(1) + shift(1)
            residual_ref[part, :] = residual
            normed_three, _ = standardize(residual)
            third_ref[part, :] = low(normed_three * gain(2) + shift(2))
            total[part, :] = jnp.broadcast_to(out_bias_ref[1:2, :], (step, width))
        for copy in saves:
            copy.start()

    @pl.when((now > mid) & (now < end))
    def _():
        for copy in load_chunk(now - mid - 1, all_up, all_down):
            copy.wait()

    @pl.when((now > mid + 1) & (now <= mid + 1 + chunks // 2))
    def _():
        for copy in keep_chunk(now - mid - 2):
            copy.wait()

    @pl.when((now > mid) & (now < mid + chunks // 2))
    def _():
        for copy in load_chunk(now - mid, own_up, own_down):
            copy.start()

    @pl.when((now >= mid + chunks // 2) & (now < end - 1))
    def _():
        for copy in load_chunk(now - mid, all_up, all_down):
            copy.start()

    @pl.when((now > mid) & (now <= mid + chunks // 2))
    def _():
        for copy in keep_chunk(now - mid - 1):
            copy.start()

    @pl.when((now > mid) & (now < end))
    def _():
        chunk = now - mid - 1
        slot = chunk % 2
        group, start = chunk // (chunks // 2), chunk % (chunks // 2) * size
        bias = up_bias_all[group, 0:1, aligned(start, size, 128)]
        for part in (pl.ds(0, length // 2), pl.ds(length // 2, length // 2)):
            up = dot_nn(third_ref[part, :], up_buf[slot]) + bias
            value, slope = gelu_both(up)
            act = low(value)
            act_ref[part, :] = act
            slope_ref[part, :] = low(slope)
            total[part, :] += dot_nn(act, down_buf[slot])

    @pl.when(now == end)
    def _():
        take_cot.wait()
        keep_out.wait()
        for copy in saves:
            copy.wait()
        sums = [0.0, 0.0, 0.0]
        for index, part in enumerate(blocks):
            normed_four, scale_four = standardize(total[part, :])
            tokens_ref[part, :] = low(residual_ref[part, :] + normed_four * gain(3) + shift(3))
            grad_out = wide(first_ref[part, :])
            d_down = norm_back(grad_out, normed_four, scale_four, gain(3))
            mixed_ref[part, :] = low(d_down)
            for copy in end_copies(index):
                copy.start()
            terms = [grad_out * normed_four, grad_out, d_down]
            sums = [old + column_sum(term) for old, term in zip(sums, terms)]
        small_ref[...] = jnp.zeros_like(small_ref)
        small_ref[3:4, :] = sums[0]
        small_ref[7:8, :] = sums[1]
        small_ref[9:10, :] = sums[2]
        for index in range(parts):
            for copy in end_copies(index):
                copy.wait()


FLOORED = (4, 10)


def front_events():
    times = (
        (0, 1, 3, 4), (0, 3, 5, 6), (0, 4, 6, 7), (6, 10, 12, 13),
        (2, 6, 7, 9, 10), (3, 7, 8, 11, 12), (4, 8, 9, 13, 14), (5, 9, 10, 14, 15),
        (8, 12, 13, 16, 17), (9, 13, 14, 17, 18), (11, 14, 16, 17), (12, 16, 18, 19),
    )
    plan = {}
    for index, moments in enumerate(times):
        for stage, moment in enumerate(moments):
            plan.setdefault(moment, []).append((index, stage))
    return {moment: sorted(items, key=lambda item: -item[1]) for moment, items in plan.items()}


def front(flags, lengths, tokens, cotangent, gains, shifts, out_biases, qv_bias, up_bias, w_qkv, w_out, w_up, w_down, query_scale):
    length, width = tokens.shape
    pairs = width // (2 * HD)
    ff = 2 * w_up.shape[1]
    size = 512
    chunks = ff // size
    kind, sem = jnp.bfloat16, pltpu.SemaphoreType.DMA

    def whole(shape):
        return pl.BlockSpec(shape, lambda i: (0,) * len(shape), pipeline_mode=pl.Buffered(1))

    hbm = pl.BlockSpec(memory_space=pl.ANY)
    smem = pl.BlockSpec(memory_space=pltpu.SMEM)
    column = pl.BlockSpec((length, 2 * HD), lambda i: (0, jnp.minimum(i, pairs - 1)))
    piece = pl.BlockSpec((length, size), lambda i: (0, jnp.clip(i - pairs - 1, 0, chunks - 1)))

    def low_like(*shape):
        return jax.ShapeDtypeStruct(shape, kind)

    def wide_like(*shape):
        return jax.ShapeDtypeStruct(shape, jnp.float32)

    return pl.pallas_call(
        partial(front_kernel, query_scale, front_events()),
        grid=(pairs + chunks + 2,),
        in_specs=[
            smem,
            smem,
            whole((4, width)),
            whole((4, width)),
            whole((2, width)),
            whole(qv_bias.shape),
            whole((1, ff // 2)),
            *[hbm] * 6,
        ],
        out_specs=[
            column,
            column,
            column,
            column,
            pl.BlockSpec((2, length, length), lambda i: (jnp.minimum(i, pairs - 1), 0, 0)),
            piece,
            piece,
            whole((16, width)),
            *[hbm] * 11,
        ],
        out_shape=[
            low_like(length, width),
            low_like(length, width),
            low_like(length, width),
            wide_like(length, width),
            low_like(2 * pairs, length, length),
            low_like(length, ff),
            low_like(length, ff),
            wide_like(16, width),
            low_like(length, width),
            low_like(length, width),
            wide_like(length, width),
            wide_like(length, width),
            low_like(length, width),
            low_like(length, width),
            low_like(length, width),
            low_like(3, width, width),
            low_like(width, width),
            low_like(width, ff),
            low_like(ff, width),
        ],
        scratch_shapes=[
            *[pltpu.VMEM((length, width), kind)] * 4,
            *[pltpu.VMEM((length, width), jnp.float32)] * 3,
            pltpu.VMEM((2, 3, width, 2 * HD), kind),
            pltpu.VMEM((width, width), kind),
            pltpu.VMEM((2, width, size), kind),
            pltpu.VMEM((2, size, width), kind),
            pltpu.VMEM((1, length), jnp.float32),
            pltpu.VMEM((2, *qv_bias.shape), jnp.float32),
            pltpu.VMEM((2, 1, ff // 2), jnp.float32),
            sem((2,)),
            sem((2,)),
            sem((2,)),
            sem((2,)),
            sem((2,)),
            sem,
            sem((2,)),
            sem((2,)),
            sem((2, 2)),
            sem((2, 12)),
            sem((2, 12)),
            sem((2, 12)),
            sem((2, 12)),
            sem((2,)),
            sem((5,)),
            sem((2, 5)),
        ],
        compiler_params=pltpu.CompilerParams(
            collective_id=1, has_side_effects=True, vmem_limit_bytes=63 * 2**20
        ),
    )(
        flags, lengths, gains, shifts, out_biases, qv_bias, up_bias.reshape(1, -1), tokens, cotangent,
        w_qkv, w_out, w_up, w_down,
    )


STAGE_STEPS = (0, 1, 3, 5, 7, 9, 11, 12)


def braid(own, other, axis):
    cut = partial(lax.slice_in_dim, axis=axis)
    return jnp.concatenate(
        [cut(own, 0, CHUNK), cut(other, 0, CHUNK), cut(own, CHUNK, 2 * CHUNK), cut(other, CHUNK, 2 * CHUNK)], axis=axis
    )


def rear_kernel(
    query_scale,
    act_own,
    act_other,
    slope_own,
    slope_other,
    up_own,
    up_other,
    down_own,
    down_other,
    q_ref,
    k_ref,
    v_ref,
    inv_ref,
    weight_ref,
    gain_ref,
    front_sums,
    third_in,
    d_down_in,
    cot_in,
    mixed_in,
    first_in,
    tokens_in,
    att_in,
    residual_in,
    w_out_in,
    w_qkv_in,
    sums_ref,
    input_out,
    whole,
    grads,
    kept_pairs,
    third_ref,
    d_down_ref,
    cot_ref,
    mixed_ref,
    att_ref,
    residual_ref,
    total,
    out_buf,
    d_up_ref,
    stage_down,
    stage_up,
    ds_ref,
    dqkv_ref,
    pair_buf,
    w_buf,
    up_sums,
    columns_of,
    small_out,
    small_in,
    mine,
    core_in,
    held,
    x_out,
    x_in,
    y_out,
    y_in,
    z_out,
    z_in,
    last,
    take_sem,
    att_sem,
    stage_sem,
    out_sem,
    head_sem,
    end_sem,
    pair_sem,
    back_sem,
    w_sem,
    load_sem,
    core_sem,
    x_sem,
    y_sem,
    z_sem,
    zz_sem,
    yy_sem,
    cc_sem,
    keep_sem,
    small_sem,
):
    now = pl.program_id(0)
    place = lax.axis_index("dp")
    turn = lax.axis_index("mp")
    core, side, level = place % 2, (place // 2) % 2, place // 4
    levels = lax.axis_size("dp") // 4
    sibling = {"dp": place + 1 - 2 * core}
    across = {"mp": 1 - turn}
    beside = {"dp": place + 2 - 4 * side}
    floors = [{"dp": (level + step) % levels * 4 + place % 4} for step in range(1, levels)]
    half, piece = CHUNK // 2, CHUNK // 2 // levels
    length, width = total.shape
    pairs = width // (2 * HD)
    units = d_up_ref.shape[1] // 2
    ffs = up_sums.shape[2] // units
    outs = width // 2 // (2 * CHUNK)
    s_mid, s_att = ffs, ffs + 2
    small_at = s_att + 2 * pairs
    first_head = 2 * ffs + outs
    chunk_count = first_head + 3 * outs
    rest = jnp.maximum(now - s_att + 1, 0)
    slot_now = now - rest // 4
    last_slot = small_at - (2 * pairs + 1) // 4
    parts = 5
    step = length // parts
    blocks = [pl.ds(start, step) for start in range(0, length, step)]

    def gain(index):
        return gain_ref[index : index + 1, :]

    takes = [
        pltpu.make_async_copy(source, target, take_sem.at[index])
        for index, (source, target) in enumerate(
            (
                (third_in, third_ref),
                (d_down_in, d_down_ref),
                (cot_in, cot_ref),
                (mixed_in, mixed_ref),
                (residual_in, residual_ref),
                (w_out_in, out_buf),
                (first_in, cot_ref),
                (tokens_in, d_down_ref),
            )
        )
    ]

    def take_att(index):
        return pltpu.make_async_copy(att_in.at[blocks[index], :], att_ref.at[index % 2], att_sem.at[index % 2])

    def save_down(chunk):
        return pltpu.make_async_copy(stage_down, grads.at[2 * chunk], stage_sem.at[0])

    def save_up(chunk):
        return pltpu.make_async_copy(stage_up, grads.at[2 * chunk + 1], stage_sem.at[1])

    out_saves = [
        pltpu.make_async_copy(
            out_buf.at[pl.ds(group * width // 2 + (index * 2 + which) * CHUNK, CHUNK), :],
            grads.at[2 * ffs + index, pl.ds((2 * which + group) * CHUNK, CHUNK), :],
            out_sem.at[group, index, which],
        )
        for group in range(2)
        for index in range(outs)
        for which in range(2)
    ]

    def head_saves(turn_of):
        return [
            pltpu.make_async_copy(
                stage_down.at[pl.ds(kind * CHUNK, CHUNK), :],
                grads.at[first_head + turn_of // 4 * 3 + kind, aligned(turn_of % 4 * CHUNK, CHUNK), :],
                head_sem.at[kind],
            )
            for kind in range(3)
        ]

    def pair_at(turn_of):
        return turn_of % 2 * (pairs // 2) + turn_of // 4 * 2 + turn_of % 4 // 2

    def save_pair(turn_of):
        return pltpu.make_async_copy(pair_buf.at[turn_of % 2], kept_pairs.at[turn_of], pair_sem.at[turn_of % 2])


    def tail_turn(index):
        return (index + pairs - 2) % pairs

    def load_back(index):
        return pltpu.make_async_copy(kept_pairs.at[tail_turn(index)], pair_buf.at[index % 2], back_sem.at[index % 2])

    def load_weights(index):
        columns = aligned(pair_at(tail_turn(index)) * 2 * HD, 2 * HD, 128)
        return pltpu.make_async_copy(w_qkv_in.at[:, :, columns], w_buf.at[index % 2], w_sem.at[index % 2])

    save_input = pltpu.make_async_copy(residual_ref, input_out, end_sem)

    @pl.when(now == 0)
    def _():
        for copy in takes[:2]:
            copy.start()
        barrier = pltpu.get_barrier_semaphore()
        partners = [sibling, across, beside, *floors]
        for partner in partners:
            pl.semaphore_signal(barrier, inc=1, device_id=partner, device_id_type=MESH)
        pl.semaphore_wait(barrier, len(partners))
        takes[0].wait()
        takes[1].wait()
        for copy in takes[2:6]:
            copy.start()
        take_att(0).start()
        take_att(1).start()

    @pl.when((now >= 1) & (now <= ffs))
    def _():
        save_down(now - 1).wait()

    @pl.when((now >= s_att + 2) & (now <= small_at) & ((now - s_att) % 2 == 0))
    def _():
        for copy in head_saves((now - s_att) // 2 - 1):
            copy.wait()


    def loads(chunk, slot):
        kept = grads.at[chunk, aligned(core * 2 * CHUNK, 2 * CHUNK), :]
        sent = grads.at[chunk, aligned((1 - core) * 2 * CHUNK, 2 * CHUNK), :]
        return [
            pltpu.make_async_copy(kept, mine, load_sem),
            remote(sent, core_in.at[slot], core_sem, (slot,), sibling),
        ]

    def x_copy(slot):
        return remote(x_out.at[slot % 2], x_in.at[slot], x_sem, (slot,), across)

    def y_copy(slot):
        return remote(
            y_out.at[slot % 2, aligned((1 - side) * half, half)], y_in.at[slot], y_sem, (slot,), beside
        )

    def z_copies(slot):
        return [
            remote(
                z_out.at[slot % 2, aligned((level + move) % levels * piece, piece)],
                z_in.at[slot, move - 1],
                z_sem,
                (slot, move - 1),
                floors[move - 1],
            )
            for move in range(1, levels)
        ]

    def target(chunk, first, size):
        return whole.at[aligned((2 * chunk + core) * CHUNK + first, size), :]

    def keep_copies(chunk, slot):
        part = target(chunk, side * half + level * piece, piece)
        copies = [pltpu.make_async_copy(last.at[slot % 2], part, keep_sem.at[slot % 2])]
        for move in range(1, levels):
            copies.append(remote(last.at[slot % 2], part, zz_sem, (slot, move - 1), floors[move - 1]))
        return copies

    def yy_copy(chunk, slot):
        part = target(chunk, side * half, half)
        return remote(part, part, yy_sem, (slot,), beside)

    def cc_copy(chunk, slot):
        part = target(chunk, 0, CHUNK)
        return remote(part, part, cc_sem, (slot,), sibling)

    def stage_7(chunk, slot):
        cc_copy(chunk, slot).wait()

    def stage_6(chunk, slot):
        yy_copy(chunk, slot).wait()
        cc_copy(chunk, slot).start()

    def stage_5(chunk, slot):
        for copy in keep_copies(chunk, slot):
            copy.wait()
        yy_copy(chunk, slot).start()

    def stage_4(chunk, slot):
        for copy in z_copies(slot):
            copy.wait()
        summed = wide(z_out[slot % 2, aligned(level * piece, piece), :])
        for move in range(1, levels):
            summed = summed + wide(z_in[slot, move - 1])
        last[slot % 2] = low(summed)
        for copy in keep_copies(chunk, slot):
            copy.start()

    def stage_3(chunk, slot):
        y_copy(slot).wait()
        z_out[slot % 2] = low(wide(y_out[slot % 2, aligned(side * half, half), :]) + wide(y_in[slot]))
        for copy in z_copies(slot):
            copy.start()

    def stage_2(chunk, slot):
        x_copy(slot).wait()
        y_out[slot % 2] = low(held[slot % 2] + wide(x_in[slot]))
        y_copy(slot).start()

    def stage_1(chunk, slot):
        for copy in loads(chunk, slot):
            copy.wait()
        x_out[slot % 2] = low(wide(mine[CHUNK:]) + wide(core_in[slot, CHUNK:]))
        x_copy(slot).start()
        held[slot % 2] = wide(mine[:CHUNK]) + wide(core_in[slot, :CHUNK])

    def stage_0(chunk, slot):
        for copy in loads(chunk, slot):
            copy.start()

    stages = [stage_0, stage_1, stage_2, stage_3, stage_4, stage_5, stage_6, stage_7]

    def advance(moment):
        for stage in reversed(range(len(stages))):
            chunk = moment - 1 - STAGE_STEPS[stage]

            @pl.when((chunk >= 0) & (chunk < chunk_count))
            def _(stage=stage, chunk=chunk):
                stages[stage](chunk, chunk % 4)

    @pl.when((rest == 0) | (rest % 4 > 0))
    def _():
        advance(slot_now)


    @pl.when(now < ffs)
    def _():
        act = braid(act_own[...], act_other[...], 1)
        stage_down[...] = low(dot_tn(act, d_down_ref[...]))
        save_down(now).start()
        w_down = braid(down_own[...], down_other[...], 0)
        w_up = braid(up_own[...], up_other[...], 1)
        for part in (pl.ds(0, length // 2), pl.ds(length // 2, length // 2)):
            d_act = dot_nt(d_down_ref[part, :], w_down)
            slope = braid(slope_own[part, :], slope_other[part, :], 1)
            d_up = low(d_act * wide(slope))
            d_up_ref[part, :] = d_up
            update = dot_nt(d_up, w_up)
            total[part, :] = jnp.where(now == 0, update, update + total[part, :])
        sums = column_sum(wide(d_up_ref[...]))
        for group in range(2):
            for which in range(2):
                first = (2 * which + group) * CHUNK
                spot = aligned(now * units + which * CHUNK, CHUNK, 128)
                up_sums[group, 0:1, spot] = sums[:, first : first + CHUNK]

    @pl.when((now >= 1) & (now <= ffs))
    def _():
        save_up(now - 1).wait()

    @pl.when(now < ffs)
    def _():
        stage_up[...] = low(dot_tn(d_up_ref[...], third_ref[...]))
        save_up(now).start()


    @pl.when(now == s_mid)
    def _():
        for copy in takes[2:6]:
            copy.wait()
        sums = [0.0] * 5
        for index, part in enumerate(blocks):
            take_att(index).wait()
            normed_three, scale_three = standardize(residual_ref[part, :])
            normed_two, scale_two = standardize(att_ref[index % 2])
            d_third = total[part, :]
            d_residual = wide(cot_ref[part, :]) + norm_back(d_third, normed_three, scale_three, gain(2))
            residual_ref[part, :] = d_residual
            d_attended = norm_back(d_residual, normed_two, scale_two, gain(1))
            d_down_ref[part, :] = low(d_attended)
            if index + 2 < parts:
                take_att(index + 2).start()
            terms = [d_residual * normed_two, d_third * normed_three, d_residual, d_third, d_attended]
            sums = [old + column_sum(term) for old, term in zip(sums, terms)]
        small_out[...] = front_sums[...]
        for index, row in enumerate((1, 2, 5, 6, 8)):
            small_out[row : row + 1, :] = sums[index]
        takes[6].start()


    @pl.when(now == s_mid + 1)
    def _():
        for part in blocks:
            third_ref[part, :] = low(dot_nt(d_down_ref[part, :], out_buf[...]))
        out_buf[...] = low(dot_tn(mixed_ref[...], d_down_ref[...]))
        for copy in out_saves:
            copy.start()

    @pl.when(now == s_att)
    def _():
        for copy in out_saves:
            copy.wait()
        takes[7].start()
        load_weights(0).start()
        load_weights(1).start()
        takes[6].wait()


    @pl.when((now >= s_att) & (now < small_at))
    def _():
        head = (now - s_att) % 2
        turn_of = (now - s_att) // 2
        pair = pair_at(turn_of)
        spot = aligned(pair * 2 * HD, 2 * HD, 128)
        lane = lax.broadcasted_iota(jnp.int32, (1, 2 * HD), 1)
        own = (lane // HD) == head
        scaled = wide(third_ref[:, spot]) * inv_ref[...]
        grad = jnp.where(own, scaled * relax_factor, 0.0).astype(jnp.bfloat16)
        inner = jnp.sum(wide(grad) * wide(mixed_ref[:, spot]), axis=1, keepdims=True)
        d_probs = dot_nt(grad, v_ref[...])
        ds_ref[...] = low(wide(weight_ref[0]) * (d_probs - inner))
        dq = low(dot_nn(ds_ref[...], k_ref[...]) * query_scale)
        dk = low(dot_tn(ds_ref[...], q_ref[...]))
        dv = low(dot_tn(weight_ref[0], low(scaled)))
        for index, value in enumerate((dq, dk, dv)):
            part = pl.ds(index * 2 * HD, 2 * HD)
            dqkv_ref[:, part] = jnp.where(own | (head == 0), value, dqkv_ref[:, part])

        @pl.when(head == 1)
        def _():
            d_qkv = dqkv_ref[...]
            stage_down[pl.ds(0, 6 * HD), :] = low(dot_tn(d_qkv, cot_ref[...]))
            for copy in head_saves(turn_of):
                copy.start()
            group, start = pair // (pairs // 2), pair % (pairs // 2) * 2 * HD
            sums = column_sum(wide(d_qkv))
            columns_of[group, 0:1, aligned(start, 2 * HD, 128)] = sums[:, : 2 * HD]
            columns_of[group, 0:1, aligned(width // 2 + start, 2 * HD, 128)] = sums[:, 4 * HD :]

            @pl.when(turn_of >= 2)
            def _():
                save_pair(turn_of - 2).wait()

            pair_buf[turn_of % 2] = d_qkv

            @pl.when(turn_of < pairs - 2)
            def _():
                save_pair(turn_of).start()


    def project_back(index):
        slot = index % 2
        load_weights(index).wait()

        @pl.when(index >= 2)
        def _():
            load_back(index).wait()

        weights = jnp.concatenate([w_buf[slot, 0], w_buf[slot, 1], w_buf[slot, 2]], axis=1)
        update = dot_nt(pair_buf[slot], weights)
        total[...] = jnp.where(index == 0, update, update + total[...])

        @pl.when(index + 2 < pairs)
        def _():
            load_weights(index + 2).start()
            load_back(index + 2).start()

    def first_norm_back():
        takes[7].wait()
        sums = [0.0, 0.0]
        for part in blocks:
            normed, scale = standardize(wide(d_down_ref[part, :]))
            errors = total[part, :]
            residual_ref[part, :] += norm_back(errors, normed, scale, gain(0))
            sums = [sums[0] + column_sum(errors * normed), sums[1] + column_sum(errors)]
        save_input.start()
        small_out[0:1, :] = sums[0]
        small_out[4:5, :] = sums[1]
        for group in range(2):
            small_out[10 + 3 * group : 11 + 3 * group, :] = columns_of[group, 0:1, :]
            for index in range(2):
                row = 11 + 3 * group + index
                small_out[row : row + 1, :] = up_sums[group, 0:1, index * width : (index + 1) * width]
        small_copies(0)[0].start()


    def small_copies(stage):
        if stage < 3:
            return [remote(small_out, small_in.at[stage], small_sem, (stage,), (sibling, across, beside)[stage])]
        return [
            remote(small_out, small_in.at[3 + level], small_sem, (2 + move,), floors[move - 1])
            for move in range(1, levels)
        ]

    def small_step_1():
        small_copies(0)[0].wait()
        small_out[...] += small_in[0]
        small_copies(1)[0].start()

    def small_step_2():
        small_copies(1)[0].wait()
        small_out[0:10, :] += small_in[1, 0:10, :]
        small_out[10:13, :] += small_in[1, 13:16, :]
        small_copies(2)[0].start()

    def small_step_3():
        small_copies(2)[0].wait()
        small_out[...] += small_in[2]
        small_in[3 + level] = small_out[...]
        for copy in small_copies(3):
            copy.start()

    def small_step_4():
        for copy in small_copies(3):
            copy.wait()
        summed = small_in[3]
        for index in range(1, levels):
            summed = summed + small_in[3 + index]
        sums_ref[...] = summed


    @pl.when(now == small_at)
    def _():
        first = last_slot + 1

        @pl.loop(first, chunk_count + 1 + STAGE_STEPS[-1])
        def _(moment):
            advance(moment)

            @pl.when(moment < first + pairs)
            def _():
                project_back(moment - first)

            steps = (first_norm_back, small_step_1, small_step_2, small_step_3, small_step_4)
            for index, small_step in enumerate(steps):
                pl.when(moment == first + pairs + index)(small_step)

        save_input.wait()


def rear(
    acts, slopes, w_up, w_down, queries, keys, values, inv, weights, w_qkv, gains, sums, third, d_down, cotangent, mixed,
    first, tokens, attended, residual, w_out, query_scale,
):
    length, width = queries.shape
    pairs = width // (2 * HD)
    ff = w_up.shape[1]
    units = 2 * CHUNK
    ffs = ff // 2 // units
    outs = width // 2 // units
    levels = lax.axis_size("dp") // 4
    half, piece = CHUNK // 2, CHUNK // 2 // levels
    s_att = ffs + 2
    small_at = s_att + 2 * pairs
    chunks = 2 * ffs + outs + 3 * outs
    kind, sem = jnp.bfloat16, pltpu.SemaphoreType.DMA

    def pair_of(i):
        turn_of = jnp.clip(i - s_att, 0, 2 * pairs - 1) // 2
        return turn_of % 2 * (pairs // 2) + turn_of // 4 * 2 + turn_of % 4 // 2

    def head_of(i):
        return pair_of(i) * 2 + jnp.clip(i - s_att, 0, 2 * pairs - 1) % 2

    def fixed(shape):
        return pl.BlockSpec(shape, lambda i: (0,) * len(shape), pipeline_mode=pl.Buffered(1))

    def unit_of(i):
        return jnp.minimum(i, ffs - 1)

    def lanes(rows):
        return [
            pl.BlockSpec((rows, units), lambda i: (0, unit_of(i))),
            pl.BlockSpec((rows, units), lambda i: (0, ffs + unit_of(i))),
        ]

    column = pl.BlockSpec((length, 2 * HD), lambda i: (0, pair_of(i)))
    hbm = pl.BlockSpec(memory_space=pl.ANY)
    return pl.pallas_call(
        partial(rear_kernel, query_scale),
        grid=(small_at + 1,),
        in_specs=[
            *lanes(length),
            *lanes(length),
            *lanes(width),
            pl.BlockSpec((units, width), lambda i: (unit_of(i), 0)),
            pl.BlockSpec((units, width), lambda i: (ffs + unit_of(i), 0)),
            *[column] * 4,
            pl.BlockSpec((1, length, length), lambda i: (head_of(i), 0, 0)),
            fixed((4, width)),
            fixed((16, width)),
            *[hbm] * 10,
        ],
        out_specs=[fixed((16, width)), hbm, hbm, hbm, hbm],
        out_shape=[
            jax.ShapeDtypeStruct((16, width), jnp.float32),
            jax.ShapeDtypeStruct((length, width), jnp.float32),
            jax.ShapeDtypeStruct((chunks * 2 * CHUNK, width), kind),
            jax.ShapeDtypeStruct((chunks, 4 * CHUNK, width), kind),
            jax.ShapeDtypeStruct((pairs - 2, length, 6 * HD), kind),
        ],
        scratch_shapes=[
            *[pltpu.VMEM((length, width), kind)] * 4,
            pltpu.VMEM((2, length // 5, width), jnp.float32),
            pltpu.VMEM((length, width), jnp.float32),
            pltpu.VMEM((length, width), jnp.float32),
            pltpu.VMEM((width, width), kind),
            pltpu.VMEM((length, 2 * units), kind),
            pltpu.VMEM((4 * CHUNK, width), kind),
            pltpu.VMEM((4 * CHUNK, width), kind),
            pltpu.VMEM((length, length), kind),
            pltpu.VMEM((length, 6 * HD), kind),
            pltpu.VMEM((2, length, 6 * HD), kind),
            pltpu.VMEM((2, 3, width, 2 * HD), kind),
            pltpu.VMEM((2, 8, ff // 2), jnp.float32),
            pltpu.VMEM((2, 8, width), jnp.float32),
            pltpu.VMEM((16, width), jnp.float32),
            pltpu.VMEM((3 + levels, 16, width), jnp.float32),
            pltpu.VMEM((2 * CHUNK, width), kind),
            pltpu.VMEM((4, 2 * CHUNK, width), kind),
            pltpu.VMEM((2, CHUNK, width), jnp.float32),
            pltpu.VMEM((2, CHUNK, width), kind),
            pltpu.VMEM((4, CHUNK, width), kind),
            pltpu.VMEM((2, CHUNK, width), kind),
            pltpu.VMEM((4, half, width), kind),
            pltpu.VMEM((2, half, width), kind),
            pltpu.VMEM((4, levels - 1, piece, width), kind),
            pltpu.VMEM((2, piece, width), kind),
            sem((8,)),
            sem((2,)),
            sem((2,)),
            sem((2, outs, 2)),
            sem((3,)),
            sem,
            sem((2,)),
            sem((2,)),
            sem((2,)),
            sem,
            sem((2, 4)),
            sem((2, 4)),
            sem((2, 4)),
            sem((2, 4, levels - 1)),
            sem((2, 4, levels - 1)),
            sem((2, 4)),
            sem((2, 4)),
            sem((2,)),
            sem((2, 2 + levels)),
        ],
        compiler_params=pltpu.CompilerParams(
            collective_id=0, has_side_effects=True, vmem_limit_bytes=63 * 2**20
        ),
    )(
        acts, acts, slopes, slopes, w_up, w_up, w_down, w_down, queries, keys, values, inv, weights, gains, sums,
        third, d_down, cotangent, mixed, first, tokens, attended, residual, w_out, w_qkv,
    )[:3]


def unpack_kernel(
    ffs,
    outs,
    whole_ref,
    grad_ref,
    result_ref,
    sums_ref,
    down_ref,
    up_ref,
    out_ref,
    qkv_ref,
    input_ref,
    output_ref,
    gains_ref,
    shifts_ref,
    outer_ref,
    qv_ref,
    bias_ref,
):
    now = pl.program_id(0)
    value = wide(whole_ref[...])

    @pl.when(now < 5)
    def _():
        input_ref[...] = grad_ref[...]
        output_ref[...] = result_ref[...]

    @pl.when(now == 0)
    def _():
        width = sums_ref.shape[1]
        gains_ref[...] = sums_ref[0:4, :]
        shifts_ref[...] = sums_ref[4:8, :]
        outer_ref[...] = sums_ref[8:10, :]
        for index in range(2):
            qv_ref[index : index + 1, :] = sums_ref[10:11, index * width // 2 : (index + 1) * width // 2]
            bias_ref[:, index * width : (index + 1) * width] = sums_ref[11 + index : 12 + index, :]

    @pl.when((now < 2 * ffs) & (now % 2 == 0))
    def _():
        down_ref[...] = value

    @pl.when((now < 2 * ffs) & (now % 2 == 1))
    def _():
        up_ref[...] = value.T

    @pl.when((now >= 2 * ffs) & (now < 2 * ffs + outs))
    def _():
        out_ref[...] = value

    @pl.when(now >= 2 * ffs + outs)
    def _():
        qkv_ref[0] = value.T


def unpack(whole, grad_input, result, sums, ff):
    length, width = result.shape
    units = 2 * CHUNK
    ffs = ff // 2 // units
    outs = width // 2 // units
    first_head = 2 * ffs + outs

    def head_turn(i):
        return jnp.maximum(i - first_head, 0)

    def fixed(*shape):
        return pl.BlockSpec(shape, lambda i: (0,) * len(shape), pipeline_mode=pl.Buffered(1))

    rows = pl.BlockSpec((length // 5, width), lambda i: (jnp.minimum(i, 4), 0))

    def wide_like(*shape):
        return jax.ShapeDtypeStruct(shape, jnp.float32)

    return pl.pallas_call(
        partial(unpack_kernel, ffs, outs),
        grid=(first_head + 3 * outs,),
        in_specs=[pl.BlockSpec((units, width), lambda i: (i, 0)), rows, rows, fixed(16, width)],
        out_specs=[
            pl.BlockSpec((units, width), lambda i: (jnp.minimum(i // 2, ffs - 1), 0)),
            pl.BlockSpec((width, units), lambda i: (0, jnp.minimum(i // 2, ffs - 1))),
            pl.BlockSpec((units, width), lambda i: (jnp.clip(i - 2 * ffs, 0, outs - 1), 0)),
            pl.BlockSpec((1, width, units), lambda i: (head_turn(i) % 3, 0, head_turn(i) // 3)),
            rows,
            rows,
            fixed(4, width),
            fixed(4, width),
            fixed(2, width),
            fixed(2, width // 2),
            fixed(1, ff // 2),
        ],
        out_shape=[
            wide_like(ff // 2, width),
            wide_like(width, ff // 2),
            wide_like(width // 2, width),
            wide_like(3, width, width // 2),
            wide_like(length, width),
            jax.ShapeDtypeStruct((length, width), jnp.bfloat16),
            wide_like(4, width),
            wide_like(4, width),
            wide_like(2, width),
            wide_like(2, width // 2),
            wide_like(1, ff // 2),
        ],
        compiler_params=pltpu.CompilerParams(vmem_limit_bytes=48 * 2**20),
    )(whole, grad_input, result, sums)


def sequence_shards(
    tokens,
    cond_flags,
    seg_lengths,
    norm_gains,
    norm_biases,
    w_qkv,
    qv_bias,
    w_out,
    out_biases,
    w_up,
    up_bias,
    w_down,
    cotangent,
):
    width = tokens.shape[1]
    query_scale = 1.0 / (relax_factor * math.sqrt(HD))
    (
        queries, keys, values, inv, kept, acts, slopes, small, first_in, mixed, attended, residual, third_in, result,
        d_down, all_qkv, all_out, all_up, all_down,
    ) = front(
        cond_flags, seg_lengths, tokens, cotangent, norm_gains, norm_biases, out_biases, qv_bias, up_bias,
        w_qkv, w_out, w_up, w_down, query_scale,
    )
    sums, grad_input, whole = rear(
        acts, slopes, all_up, all_down, queries, keys, values, inv, kept, all_qkv, norm_gains, small, third_in, d_down,
        cotangent, mixed, first_in, tokens, attended, residual, all_out, query_scale,
    )
    (
        grad_w_down, grad_w_up, grad_w_out, grad_w_qkv, grad_input, result, grad_gains, grad_shifts, grad_outer, grad_qv,
        grad_up_bias,
    ) = unpack(whole, grad_input, result, sums, all_up.shape[1])
    return (
        result,
        grad_input,
        grad_gains,
        grad_shifts,
        grad_w_qkv,
        grad_qv,
        grad_w_out,
        grad_outer,
        grad_w_up,
        grad_up_bias.reshape(-1),
        grad_w_down,
    )


def solution(mesh):
    in_specs = (
        P(("dp", "mp"), None),
        P("dp", None),
        P("dp", None),
        P(),
        P(),
        P(None, None, "mp"),
        P(None, "mp"),
        P("mp", None),
        P(),
        P(None, "mp"),
        P("mp"),
        P("mp", None),
        P(("dp", "mp"), None),
    )
    out_specs = (
        P(("dp", "mp"), None),
        P(("dp", "mp"), None),
        P(),
        P(),
        P(None, None, "mp"),
        P(None, "mp"),
        P("mp", None),
        P(),
        P(None, "mp"),
        P("mp"),
        P("mp", None),
    )
    per_device = mesh.shape["dp"] * mesh.shape["mp"]

    def step(*args):
        whole_sequences = args[1].shape[0] == per_device
        local = sequence_shards if whole_sequences and mesh.shape["mp"] == 2 and mesh.shape["dp"] == 16 else shards
        return jax.shard_map(
            local, mesh=mesh, in_specs=in_specs, out_specs=out_specs, check_vma=False
        )(*args)

    return step
```

```python
from functools import partial
import math

import jax
import jax.numpy as jnp
from jax import lax
from jax.experimental import pallas as pl
from jax.experimental.pallas import tpu as pltpu
from jax.sharding import PartitionSpec as P

HD = 64


epsilon = 1e-05
relax_factor = 32.0


def standardize(entries):
    average = jnp.mean(entries, axis=-1, keepdims=True)
    centred = entries - average
    spread = jnp.mean(centred * centred, axis=-1, keepdims=True)
    inv_std = lax.rsqrt(spread + epsilon)
    return (centred * inv_std, inv_std)


def norm_back(grad_in, normed, inv_std, gain_row):
    weighted = grad_in * gain_row
    return inv_std * (
        weighted
        - jnp.mean(weighted, axis=-1, keepdims=True)
        - normed * jnp.mean(weighted * normed, axis=-1, keepdims=True)
    )


def token_marks(seg_flags, lengths, length):
    position = jnp.arange(length, dtype=jnp.int32)
    segment = (position >= lengths[0]).astype(jnp.int32) + (
        position >= lengths[0] + lengths[1]
    ).astype(jnp.int32)
    segment_hits = (segment[:, None] == jnp.arange(3, dtype=jnp.int32)[None, :]).astype(jnp.int32)
    return jnp.sum(segment_hits * seg_flags[None, :], axis=1)


def block_mask(marks_seq, first_row, block_rows, length):
    query_places = first_row + jnp.arange(block_rows, dtype=jnp.int32)
    key_places = jnp.arange(length, dtype=jnp.int32)
    return (key_places[None, :] <= query_places[:, None]) | (marks_seq[None, :] == 1)


def shards(
    tokens,
    cond_flags,
    seg_lengths,
    norm_gains,
    norm_biases,
    w_qkv,
    qv_bias,
    w_out,
    out_biases,
    w_up,
    up_bias,
    w_down,
    cotangent,
):
    shard_rows = tokens.shape[0]
    group_rows = shard_rows * lax.axis_size("mp")
    seq_count = cond_flags.shape[0]
    length = group_rows // seq_count
    block_rows = length // 2
    head_count = w_qkv.shape[2] // HD
    local_width = head_count * HD
    query_scale = 1.0 / (relax_factor * math.sqrt(HD))
    all_marks = jax.vmap(lambda seg_flags, lengths: token_marks(seg_flags, lengths, length))(
        cond_flags, seg_lengths
    )
    numbers = jnp.arange(seq_count * 2, dtype=jnp.int32)
    source = tokens.astype(jnp.float32)
    normed_one, scale_one = standardize(source)
    first_in = (normed_one * norm_gains[0] + norm_biases[0]).astype(jnp.bfloat16)
    first_all = lax.all_gather(first_in, "mp", axis=0, tiled=True)
    bias_rows = jnp.stack([qv_bias[0], jnp.zeros_like(qv_bias[0]), qv_bias[1]])
    projected = (
        jnp.einsum("td,cde->cte", first_all, w_qkv, preferred_element_type=jnp.float32)
        + bias_rows[:, None, :]
    )
    queries = (
        (projected[0] * query_scale)
        .astype(jnp.bfloat16)
        .reshape(seq_count * 2, block_rows, head_count, HD)
    )
    key_all = projected[1].astype(jnp.bfloat16).reshape(seq_count, length, head_count, HD)
    value_all = projected[2].astype(jnp.bfloat16).reshape(seq_count, length, head_count, HD)

    def block_probs(query_block, number, row_top, row_total):
        sequence = number // 2
        first_row = number % 2 * block_rows
        key_seq = lax.dynamic_index_in_dim(key_all, sequence, 0, keepdims=False)
        allowed = block_mask(
            lax.dynamic_index_in_dim(all_marks, sequence, 0, keepdims=False),
            first_row,
            block_rows,
            length,
        )
        scores = jnp.einsum(
            "qhd,khd->hqk", query_block, key_seq, preferred_element_type=jnp.float32
        )
        if row_top is None:
            row_top = jnp.max(jnp.where(allowed[None], scores, -1e30), axis=-1, keepdims=True)
        weights = jnp.exp(jnp.where(allowed[None], (scores - row_top) * relax_factor, -30000.0))
        if row_total is None:
            row_total = jnp.sum(weights, axis=-1, keepdims=True)
        return (weights / row_total, row_top, row_total, key_seq)

    def forward_block(block_item):
        query_block, number = block_item
        probs, row_top, row_total, key_seq = block_probs(query_block, number, None, None)
        value_seq = lax.dynamic_index_in_dim(value_all, number // 2, 0, keepdims=False)
        mixed_block = jnp.einsum(
            "hqk,khd->qhd",
            probs.astype(jnp.bfloat16),
            value_seq,
            preferred_element_type=jnp.float32,
        )
        return (mixed_block.astype(jnp.bfloat16), row_top, row_total)

    mixed_heads, row_tops, row_totals = lax.map(forward_block, (queries, numbers))
    mixed_heads = mixed_heads.reshape(group_rows, local_width)
    attended = (
        lax.psum_scatter(
            jnp.dot(mixed_heads, w_out, preferred_element_type=jnp.float32),
            "mp",
            scatter_dimension=0,
            tiled=True,
        )
        + out_biases[0]
    )
    normed_two, scale_two = standardize(attended)
    residual = source + normed_two * norm_gains[1] + norm_biases[1]
    normed_three, scale_three = standardize(residual)
    third_in = (normed_three * norm_gains[2] + norm_biases[2]).astype(jnp.bfloat16)
    third_all = lax.all_gather(third_in, "mp", axis=0, tiled=True)
    up_value = jnp.dot(third_all, w_up, preferred_element_type=jnp.float32) + up_bias
    activated = jax.nn.gelu(up_value, approximate=True).astype(jnp.bfloat16)
    down = (
        lax.psum_scatter(
            jnp.dot(activated, w_down, preferred_element_type=jnp.float32),
            "mp",
            scatter_dimension=0,
            tiled=True,
        )
        + out_biases[1]
    )
    normed_four, scale_four = standardize(down)
    result = (residual + normed_four * norm_gains[3] + norm_biases[3]).astype(jnp.bfloat16)
    grad_out = cotangent.astype(jnp.float32)
    d_down = norm_back(grad_out, normed_four, scale_four, norm_gains[3])
    d_down_low = d_down.astype(jnp.bfloat16)
    d_down_all = lax.all_gather(d_down_low, "mp", axis=0, tiled=True)
    d_act = jnp.einsum("td,fd->tf", d_down_all, w_down, preferred_element_type=jnp.float32)
    grad_w_down = jnp.einsum("tf,td->fd", activated, d_down_all, preferred_element_type=jnp.float32)
    gelu_value, gelu_pull = jax.vjp(partial(jax.nn.gelu, approximate=True), up_value)
    d_up = gelu_pull(d_act)[0].astype(jnp.bfloat16)
    grad_w_up = jnp.einsum("td,tf->df", third_all, d_up, preferred_element_type=jnp.float32)
    grad_up_bias = jnp.sum(d_up, axis=0, dtype=jnp.float32)
    d_third = lax.psum_scatter(
        jnp.einsum("tf,df->td", d_up, w_up, preferred_element_type=jnp.float32),
        "mp",
        scatter_dimension=0,
        tiled=True,
    )
    d_residual = grad_out + norm_back(d_third, normed_three, scale_three, norm_gains[2])
    d_attended = norm_back(d_residual, normed_two, scale_two, norm_gains[1])
    d_att_low = d_attended.astype(jnp.bfloat16)
    d_att_all = lax.all_gather(d_att_low, "mp", axis=0, tiled=True)
    d_mixed = jnp.einsum("td,hd->th", d_att_all, w_out, preferred_element_type=jnp.float32).astype(
        jnp.bfloat16
    )
    grad_w_out = jnp.einsum("th,td->hd", mixed_heads, d_att_all, preferred_element_type=jnp.float32)
    d_mixed_blocks = d_mixed.reshape(seq_count * 2, block_rows, head_count, HD)

    def backward_block(block_item):
        query_block, d_block, row_top, row_total, number = block_item
        probs, kept_top, kept_total, key_seq = block_probs(query_block, number, row_top, row_total)
        value_seq = lax.dynamic_index_in_dim(value_all, number // 2, 0, keepdims=False)
        d_probs = jnp.einsum("qhd,khd->hqk", d_block, value_seq, preferred_element_type=jnp.float32)
        inner = jnp.sum(probs * d_probs, axis=-1, keepdims=True)
        d_scores = (relax_factor * probs * (d_probs - inner)).astype(jnp.bfloat16)
        d_query = (
            jnp.einsum("hqk,khd->qhd", d_scores, key_seq, preferred_element_type=jnp.float32)
            * query_scale
        )
        d_key = jnp.einsum(
            "hqk,qhd->khd", d_scores, query_block, preferred_element_type=jnp.float32
        )
        d_value = jnp.einsum(
            "hqk,qhd->khd", probs.astype(jnp.bfloat16), d_block, preferred_element_type=jnp.float32
        )
        return (d_query.astype(jnp.bfloat16), d_key, d_value)

    d_queries, d_keys, d_values = lax.map(
        backward_block, (queries, d_mixed_blocks, row_tops, row_totals, numbers)
    )
    d_keys = jnp.sum(d_keys.reshape(seq_count, 2, length, local_width), axis=1).reshape(
        group_rows, local_width
    )
    d_values = jnp.sum(d_values.reshape(seq_count, 2, length, local_width), axis=1).reshape(
        group_rows, local_width
    )
    d_qkv = jnp.stack(
        [
            d_queries.reshape(group_rows, local_width),
            d_keys.astype(jnp.bfloat16),
            d_values.astype(jnp.bfloat16),
        ]
    )
    grad_w_qkv = jnp.einsum("td,cte->cde", first_all, d_qkv, preferred_element_type=jnp.float32)
    grad_qv_bias = jnp.stack(
        [jnp.sum(d_qkv[0], axis=0, dtype=jnp.float32), jnp.sum(d_qkv[2], axis=0, dtype=jnp.float32)]
    )
    d_first = lax.psum_scatter(
        jnp.einsum("cte,cde->td", d_qkv, w_qkv, preferred_element_type=jnp.float32).astype(
            jnp.bfloat16
        ),
        "mp",
        scatter_dimension=0,
        tiled=True,
    ).astype(jnp.float32)
    grad_input = d_residual + norm_back(d_first, normed_one, scale_one, norm_gains[0])
    error_terms = (d_first, d_residual, d_third, grad_out)
    normed_terms = (normed_one, normed_two, normed_three, normed_four)
    gain_sums = jnp.stack(
        [
            jnp.sum(error_term * normed_term, axis=0)
            for error_term, normed_term in zip(error_terms, normed_terms)
        ]
    )
    bias_sums = jnp.stack([jnp.sum(error_term, axis=0) for error_term in error_terms])
    outer_sums = jnp.stack([jnp.sum(d_attended, axis=0), jnp.sum(d_down, axis=0)])
    gain_sums, bias_sums, outer_sums = lax.psum((gain_sums, bias_sums, outer_sums), ("dp", "mp"))
    grad_w_qkv, grad_qv_bias, grad_w_out, grad_w_up, grad_up_bias, grad_w_down = (
        lax.psum(grad_w_qkv.astype(jnp.bfloat16), "dp").astype(jnp.float32),
        lax.psum(grad_qv_bias.astype(jnp.bfloat16), "dp").astype(jnp.float32),
        lax.psum(grad_w_out.astype(jnp.bfloat16), "dp").astype(jnp.float32),
        lax.psum(grad_w_up.astype(jnp.bfloat16), "dp").astype(jnp.float32),
        lax.psum(grad_up_bias.astype(jnp.bfloat16), "dp").astype(jnp.float32),
        lax.psum(grad_w_down.astype(jnp.bfloat16), "dp").astype(jnp.float32),
    )
    return (
        result,
        grad_input,
        gain_sums,
        bias_sums,
        grad_w_qkv,
        grad_qv_bias,
        grad_w_out,
        outer_sums,
        grad_w_up,
        grad_up_bias,
        grad_w_down,
    )


LOG2E = 1.4426950408889634
HIDDEN = -1e30


def dot_nt(a, b):
    return lax.dot_general(a, b, (((1,), (1,)), ((), ())), preferred_element_type=jnp.float32)


def dot_nn(a, b):
    return lax.dot_general(a, b, (((1,), (0,)), ((), ())), preferred_element_type=jnp.float32)


def dot_tn(a, b):
    return lax.dot_general(a, b, (((0,), (0,)), ((), ())), preferred_element_type=jnp.float32)


def low(value):
    return value.astype(jnp.bfloat16)


MESH = pl.DeviceIdType.MESH
CHUNK = 128


def remote(source, target, sems, index, device):
    return pltpu.make_async_remote_copy(
        src_ref=source,
        dst_ref=target,
        send_sem=sems.at[(0, *index)],
        recv_sem=sems.at[(1, *index)],
        device_id=device,
        device_id_type=MESH,
    )


def aligned(start, size, unit=16):
    return pl.ds(pl.multiple_of(start, unit), size)


def wide(value):
    return value.astype(jnp.float32)


GELU_SCALE = math.sqrt(2.0 / math.pi)
GELU_CUBE = 0.044715


def gelu_both(up):
    square = up * up
    half = 0.5 * jnp.tanh(up * (GELU_SCALE + GELU_SCALE * GELU_CUBE * square)) + 0.5
    value = up * half
    slope = half + value * (1.0 - half) * (2.0 * GELU_SCALE + 6.0 * GELU_SCALE * GELU_CUBE * square)
    return value, slope


def column_sum(value):
    return jnp.sum(value, axis=0, keepdims=True)


def front_kernel(
    query_scale,
    events,
    flags_ref,
    lengths_ref,
    gain_ref,
    shift_ref,
    out_bias_ref,
    qv_bias_ref,
    up_bias_ref,
    tokens_in,
    cot_in,
    own_qkv,
    own_out,
    own_up,
    own_down,
    q_ref,
    k_ref,
    v_ref,
    inv_ref,
    weight_ref,
    act_ref,
    slope_ref,
    small_ref,
    first_out,
    mixed_out,
    att_out,
    residual_out,
    third_out,
    result_out,
    d_down_out,
    all_qkv,
    all_out,
    all_up,
    all_down,
    first_ref,
    mixed_ref,
    tokens_ref,
    third_ref,
    att_ref,
    residual_ref,
    total,
    qkv_buf,
    out_buf,
    up_buf,
    down_buf,
    hide_ref,
    qv_all,
    up_bias_all,
    qkv_load,
    out_load,
    up_load,
    down_load,
    qkv_keep,
    out_keep,
    up_keep,
    down_keep,
    bias_sem,
    x_sem,
    y_sem,
    z_sem,
    c_sem,
    in_sem,
    save_sem,
    end_sem,
):
    now = pl.program_id(0)
    place = lax.axis_index("dp")
    turn = lax.axis_index("mp")
    core, side, odd = place % 2, (place // 2) % 2, place // 4 % 2
    above = {"dp": place + 4 - 8 * odd}
    sibling = {"dp": place + 1 - 2 * core}
    across = {"mp": 1 - turn}
    beside = {"dp": place + 2 - 4 * side}
    length, width = tokens_ref.shape
    pairs = width // (2 * HD)
    size = act_ref.shape[1]
    ff = all_up.shape[1]
    chunks = ff // size
    mid = pairs
    end = mid + chunks + 1
    parts = 5
    step = length // parts
    blocks = [pl.ds(start, step) for start in range(0, length, step)]

    def gain(index):
        return gain_ref[index : index + 1, :]

    def shift(index):
        return shift_ref[index : index + 1, :]


    q_qkv, q_out, q_up, q_down = width // 8, width // 8, ff // 8, ff // 8
    row_up = width // 4

    def places(index, quarter, count, narrow):
        if index < 3:
            cols = aligned(quarter * q_qkv, count * q_qkv, 128)
            far = aligned(width // 2 + quarter * q_qkv, count * q_qkv, 128)
            return own_qkv.at[index, :, cols], all_qkv.at[index, :, far]
        if index < 4:
            rows = aligned(quarter * q_out, count * q_out)
            return own_out.at[rows, :], all_out.at[aligned(width // 2 + quarter * q_out, count * q_out), :]
        first, span = (index - 4) % 4 * row_up, row_up
        if narrow:
            first, span = first + odd * (row_up // 2), row_up // 2
        if index < 8:
            rows = aligned(first, span)
            cols = aligned(quarter * q_up, count * q_up, 128)
            return own_up.at[rows, cols], all_up.at[rows, aligned(ff // 2 + quarter * q_up, count * q_up, 128)]
        cols = aligned(first, span, 128)
        rows = aligned(quarter * q_down, count * q_down)
        return own_down.at[rows, cols], all_down.at[aligned(ff // 2 + quarter * q_down, count * q_down), cols]

    def hop(index, stage):
        narrow = FLOORED[0] <= index < FLOORED[1]
        if stage == 0:
            source, target = places(index, 2 * core + side, 1, narrow)
            return remote(source, target, x_sem, (index,), across)
        if stage == 1:
            part = places(index, 2 * core + side, 1, narrow)[1]
            return remote(part, part, y_sem, (index,), beside)
        part = places(index, 2 * core, 2, narrow and stage == 2)[1]
        if narrow and stage == 2:
            return remote(part, part, z_sem, (index,), above)
        return remote(part, part, c_sem, (index,), sibling)

    bias_copies = [
        remote(qv_bias_ref, qv_all.at[1], bias_sem, (0,), across),
        remote(up_bias_ref, up_bias_all.at[1], bias_sem, (1,), across),
    ]
    def load_pair(pair, ref):
        start = pair % (pairs // 2) * 2 * HD if ref is own_qkv else pair * 2 * HD
        return pltpu.make_async_copy(
            ref.at[:, :, aligned(start, 2 * HD, 128)], qkv_buf.at[pair % 2], qkv_load.at[pair % 2]
        )

    def load_chunk(chunk, up, down):
        slot = chunk % 2
        return [
            pltpu.make_async_copy(up.at[:, aligned(chunk * size, size, 128)], up_buf.at[slot], up_load.at[slot]),
            pltpu.make_async_copy(down.at[aligned(chunk * size, size), :], down_buf.at[slot], down_load.at[slot]),
        ]

    out_loads = [
        pltpu.make_async_copy(
            own_out, out_buf.at[pl.ds(0, width // 2), :], out_load.at[0]
        ),
        pltpu.make_async_copy(
            all_out.at[pl.ds(width // 2, width // 2), :], out_buf.at[pl.ds(width // 2, width // 2), :], out_load.at[1]
        ),
    ]

    def keep_pair(pair):
        return pltpu.make_async_copy(
            qkv_buf.at[pair % 2], all_qkv.at[:, :, aligned(pair * 2 * HD, 2 * HD, 128)], qkv_keep.at[pair % 2]
        )

    def keep_chunk(chunk):
        slot = chunk % 2
        return [
            pltpu.make_async_copy(up_buf.at[slot], all_up.at[:, aligned(chunk * size, size, 128)], up_keep.at[slot]),
            pltpu.make_async_copy(down_buf.at[slot], all_down.at[aligned(chunk * size, size), :], down_keep.at[slot]),
        ]

    keep_out = pltpu.make_async_copy(
        out_buf.at[pl.ds(0, width // 2), :], all_out.at[pl.ds(0, width // 2), :], out_keep
    )
    take_tokens = pltpu.make_async_copy(tokens_in, tokens_ref, in_sem.at[0])
    take_cot = pltpu.make_async_copy(cot_in, first_ref, in_sem.at[1])
    save_first = pltpu.make_async_copy(first_ref, first_out, save_sem.at[0])
    saves = [
        pltpu.make_async_copy(mixed_ref, mixed_out, save_sem.at[1]),
        pltpu.make_async_copy(att_ref, att_out, save_sem.at[2]),
        pltpu.make_async_copy(residual_ref, residual_out, save_sem.at[3]),
        pltpu.make_async_copy(third_ref, third_out, save_sem.at[4]),
    ]

    def end_copies(index):
        part = blocks[index]
        return [
            pltpu.make_async_copy(tokens_ref.at[part, :], result_out.at[part, :], end_sem.at[0, index]),
            pltpu.make_async_copy(mixed_ref.at[part, :], d_down_out.at[part, :], end_sem.at[1, index]),
        ]

    def run_events(slot):
        for index, stage in events.get(slot, []):
            hops = 4 if FLOORED[0] <= index < FLOORED[1] else 3
            if stage > 0:
                hop(index, stage - 1).wait()
            if stage < hops:
                hop(index, stage).start()

    @pl.when(now == 0)
    def _():
        take_tokens.start()
        load_pair(0, own_qkv).start()
        barrier = pltpu.get_barrier_semaphore()
        partners = [sibling, across, beside, above]
        for partner in partners:
            pl.semaphore_signal(barrier, inc=1, device_id=partner, device_id_type=MESH)
        pl.semaphore_wait(barrier, len(partners))
        for copy in bias_copies:
            copy.start()

    for moment in range(end):

        @pl.when(now == moment)
        def _(moment=moment):
            run_events(2 * moment if moment < mid else moment + mid)

    @pl.when(now == 0)
    def _():
        qv_all[0] = qv_bias_ref[...]
        up_bias_all[0] = up_bias_ref[...]
        spots = lax.broadcasted_iota(jnp.int32, (1, length), 1)
        one = lengths_ref[turn, 0]
        two = one + lengths_ref[turn, 1]
        marks = jnp.where(
            spots < one, flags_ref[turn, 0], jnp.where(spots < two, flags_ref[turn, 1], flags_ref[turn, 2])
        )
        hide_ref[...] = jnp.where(marks == 1, 0.0, HIDDEN)
        take_tokens.wait()
        for part in blocks:
            normed, _ = standardize(wide(tokens_ref[part, :]))
            first_ref[part, :] = low(normed * gain(0) + shift(0))
        save_first.start()

    @pl.when(now == pairs // 2)
    def _():
        bias_copies[0].wait()

    @pl.when(now == mid)
    def _():
        bias_copies[1].wait()


    def attend_head(head):
        lane = lax.broadcasted_iota(jnp.int32, (1, 2 * HD), 1)
        own = (lane // HD) == head
        keys = k_ref[...]
        values = jnp.where(own, v_ref[...], jnp.ones((1, 2 * HD), jnp.bfloat16))
        rows = length // 2
        spot = aligned(now * 2 * HD, 2 * HD, 128)
        for start in (0, rows):
            part = pl.ds(start, rows)
            mine = jnp.where(own, q_ref[part, :], jnp.zeros((1, 2 * HD), jnp.bfloat16))
            scores = dot_nt(mine, keys)
            query_places = lax.broadcasted_iota(jnp.int32, (rows, length), 0) + start
            key_places = lax.broadcasted_iota(jnp.int32, (rows, length), 1)
            scores = scores + jnp.where(key_places <= query_places, 0.0, hide_ref[...])
            top = jnp.max(scores, axis=1, keepdims=True)
            kept = low(jnp.exp2((scores - top) * (relax_factor * LOG2E)))
            weight_ref[head, part, :] = kept
            mixed = dot_nn(kept, values)
            inv = 1.0 / pltpu.roll(mixed, HD, 1)
            out = low(mixed * inv)
            mixed_ref[part, spot] = out if head == 0 else jnp.where(own, out, mixed_ref[part, spot])
            inv_ref[part, :] = inv if head == 0 else jnp.where(own, inv, inv_ref[part, :])

    @pl.when(now < mid)
    def _():
        pair = now
        load_pair(pair, all_qkv).wait()
        group, start = pair // (pairs // 2), pair % (pairs // 2) * 2 * HD
        parts_of = qkv_buf[pair % 2]
        projected = dot_nn(first_ref[...], jnp.concatenate([parts_of[0], parts_of[1], parts_of[2]], axis=1))
        bias_q = qv_all[group, 0:1, aligned(start, 2 * HD, 128)]
        bias_v = qv_all[group, 1:2, aligned(start, 2 * HD, 128)]
        q_ref[...] = low((projected[:, : 2 * HD] + bias_q) * query_scale)
        k_ref[...] = low(projected[:, 2 * HD : 4 * HD])
        v_ref[...] = low(projected[:, 4 * HD :] + bias_v)

    @pl.when(now < pairs // 2)
    def _():
        keep_pair(now).start()

    @pl.when(now < mid)
    def _():
        attend_head(0)

    for moment in range(mid):

        @pl.when(now == moment)
        def _(moment=moment):
            run_events(2 * moment + 1)

    @pl.when((now >= 1) & (now <= pairs // 2))
    def _():
        keep_pair(now - 1).wait()

    @pl.when(now < pairs // 2 - 1)
    def _():
        load_pair(now + 1, own_qkv).start()

    @pl.when((now >= pairs // 2 - 1) & (now < mid - 1))
    def _():
        load_pair(now + 1, all_qkv).start()

    @pl.when(now == mid - 1)
    def _():
        for copy in out_loads:
            copy.start()

    @pl.when(now < mid)
    def _():
        attend_head(1)

    @pl.when(now == mid)
    def _():
        for copy in load_chunk(0, own_up, own_down):
            copy.start()
        save_first.wait()
        take_cot.start()
        for copy in out_loads:
            copy.wait()
        keep_out.start()
        for part in (pl.ds(0, length // 2), pl.ds(length // 2, length // 2)):
            att_ref[part, :] = dot_nn(mixed_ref[part, :], out_buf[...]) + out_bias_ref[0:1, :]
        for part in blocks:
            attended = att_ref[part, :]
            normed_two, _ = standardize(attended)
            residual = wide(tokens_ref[part, :]) + normed_two * gain(1) + shift(1)
            residual_ref[part, :] = residual
            normed_three, _ = standardize(residual)
            third_ref[part, :] = low(normed_three * gain(2) + shift(2))
            total[part, :] = jnp.broadcast_to(out_bias_ref[1:2, :], (step, width))
        for copy in saves:
            copy.start()

    @pl.when((now > mid) & (now < end))
    def _():
        for copy in load_chunk(now - mid - 1, all_up, all_down):
            copy.wait()

    @pl.when((now > mid + 1) & (now <= mid + 1 + chunks // 2))
    def _():
        for copy in keep_chunk(now - mid - 2):
            copy.wait()

    @pl.when((now > mid) & (now < mid + chunks // 2))
    def _():
        for copy in load_chunk(now - mid, own_up, own_down):
            copy.start()

    @pl.when((now >= mid + chunks // 2) & (now < end - 1))
    def _():
        for copy in load_chunk(now - mid, all_up, all_down):
            copy.start()

    @pl.when((now > mid) & (now <= mid + chunks // 2))
    def _():
        for copy in keep_chunk(now - mid - 1):
            copy.start()

    @pl.when((now > mid) & (now < end))
    def _():
        chunk = now - mid - 1
        slot = chunk % 2
        group, start = chunk // (chunks // 2), chunk % (chunks // 2) * size
        bias = up_bias_all[group, 0:1, aligned(start, size, 128)]
        for part in (pl.ds(0, length // 2), pl.ds(length // 2, length // 2)):
            up = dot_nn(third_ref[part, :], up_buf[slot]) + bias
            value, slope = gelu_both(up)
            act = low(value)
            act_ref[part, :] = act
            slope_ref[part, :] = low(slope)
            total[part, :] += dot_nn(act, down_buf[slot])

    @pl.when(now == end)
    def _():
        take_cot.wait()
        keep_out.wait()
        for copy in saves:
            copy.wait()
        sums = [0.0, 0.0, 0.0]
        for index, part in enumerate(blocks):
            normed_four, scale_four = standardize(total[part, :])
            tokens_ref[part, :] = low(residual_ref[part, :] + normed_four * gain(3) + shift(3))
            grad_out = wide(first_ref[part, :])
            d_down = norm_back(grad_out, normed_four, scale_four, gain(3))
            mixed_ref[part, :] = low(d_down)
            for copy in end_copies(index):
                copy.start()
            terms = [grad_out * normed_four, grad_out, d_down]
            sums = [old + column_sum(term) for old, term in zip(sums, terms)]
        small_ref[...] = jnp.zeros_like(small_ref)
        small_ref[3:4, :] = sums[0]
        small_ref[7:8, :] = sums[1]
        small_ref[9:10, :] = sums[2]
        for index in range(parts):
            for copy in end_copies(index):
                copy.wait()


FLOORED = (4, 10)


def front_events():
    times = (
        (0, 1, 3, 4), (0, 3, 5, 6), (0, 4, 6, 7), (6, 10, 12, 13),
        (2, 6, 7, 9, 10), (3, 7, 8, 11, 12), (4, 8, 9, 13, 14), (5, 9, 10, 14, 15),
        (8, 12, 13, 16, 17), (9, 13, 14, 17, 18), (11, 14, 16, 17), (12, 16, 18, 19),
    )
    plan = {}
    for index, moments in enumerate(times):
        for stage, moment in enumerate(moments):
            plan.setdefault(moment, []).append((index, stage))
    return {moment: sorted(items, key=lambda item: -item[1]) for moment, items in plan.items()}


def front(flags, lengths, tokens, cotangent, gains, shifts, out_biases, qv_bias, up_bias, w_qkv, w_out, w_up, w_down, query_scale):
    length, width = tokens.shape
    pairs = width // (2 * HD)
    ff = 2 * w_up.shape[1]
    size = 512
    chunks = ff // size
    kind, sem = jnp.bfloat16, pltpu.SemaphoreType.DMA

    def whole(shape):
        return pl.BlockSpec(shape, lambda i: (0,) * len(shape), pipeline_mode=pl.Buffered(1))

    hbm = pl.BlockSpec(memory_space=pl.ANY)
    smem = pl.BlockSpec(memory_space=pltpu.SMEM)
    column = pl.BlockSpec((length, 2 * HD), lambda i: (0, jnp.minimum(i, pairs - 1)))
    piece = pl.BlockSpec((length, size), lambda i: (0, jnp.clip(i - pairs - 1, 0, chunks - 1)))

    def low_like(*shape):
        return jax.ShapeDtypeStruct(shape, kind)

    def wide_like(*shape):
        return jax.ShapeDtypeStruct(shape, jnp.float32)

    return pl.pallas_call(
        partial(front_kernel, query_scale, front_events()),
        grid=(pairs + chunks + 2,),
        in_specs=[
            smem,
            smem,
            whole((4, width)),
            whole((4, width)),
            whole((2, width)),
            whole(qv_bias.shape),
            whole((1, ff // 2)),
            *[hbm] * 6,
        ],
        out_specs=[
            column,
            column,
            column,
            column,
            pl.BlockSpec((2, length, length), lambda i: (jnp.minimum(i, pairs - 1), 0, 0)),
            piece,
            piece,
            whole((16, width)),
            *[hbm] * 11,
        ],
        out_shape=[
            low_like(length, width),
            low_like(length, width),
            low_like(length, width),
            wide_like(length, width),
            low_like(2 * pairs, length, length),
            low_like(length, ff),
            low_like(length, ff),
            wide_like(16, width),
            low_like(length, width),
            low_like(length, width),
            wide_like(length, width),
            wide_like(length, width),
            low_like(length, width),
            low_like(length, width),
            low_like(length, width),
            low_like(3, width, width),
            low_like(width, width),
            low_like(width, ff),
            low_like(ff, width),
        ],
        scratch_shapes=[
            *[pltpu.VMEM((length, width), kind)] * 4,
            *[pltpu.VMEM((length, width), jnp.float32)] * 3,
            pltpu.VMEM((2, 3, width, 2 * HD), kind),
            pltpu.VMEM((width, width), kind),
            pltpu.VMEM((2, width, size), kind),
            pltpu.VMEM((2, size, width), kind),
            pltpu.VMEM((1, length), jnp.float32),
            pltpu.VMEM((2, *qv_bias.shape), jnp.float32),
            pltpu.VMEM((2, 1, ff // 2), jnp.float32),
            sem((2,)),
            sem((2,)),
            sem((2,)),
            sem((2,)),
            sem((2,)),
            sem,
            sem((2,)),
            sem((2,)),
            sem((2, 2)),
            sem((2, 12)),
            sem((2, 12)),
            sem((2, 12)),
            sem((2, 12)),
            sem((2,)),
            sem((5,)),
            sem((2, 5)),
        ],
        compiler_params=pltpu.CompilerParams(
            collective_id=1, has_side_effects=True, vmem_limit_bytes=63 * 2**20
        ),
    )(
        flags, lengths, gains, shifts, out_biases, qv_bias, up_bias.reshape(1, -1), tokens, cotangent,
        w_qkv, w_out, w_up, w_down,
    )


STAGE_STEPS = (0, 1, 3, 5, 7, 9, 11, 12)


def braid(own, other, axis):
    cut = partial(lax.slice_in_dim, axis=axis)
    return jnp.concatenate(
        [cut(own, 0, CHUNK), cut(other, 0, CHUNK), cut(own, CHUNK, 2 * CHUNK), cut(other, CHUNK, 2 * CHUNK)], axis=axis
    )


def rear_kernel(
    query_scale,
    act_own,
    act_other,
    slope_own,
    slope_other,
    up_own,
    up_other,
    down_own,
    down_other,
    q_ref,
    k_ref,
    v_ref,
    inv_ref,
    weight_ref,
    gain_ref,
    front_sums,
    third_in,
    d_down_in,
    cot_in,
    mixed_in,
    first_in,
    tokens_in,
    att_in,
    residual_in,
    w_out_in,
    w_qkv_in,
    sums_ref,
    input_out,
    whole,
    grads,
    kept_pairs,
    third_ref,
    d_down_ref,
    cot_ref,
    mixed_ref,
    att_ref,
    residual_ref,
    total,
    out_buf,
    d_up_ref,
    stage_down,
    stage_up,
    ds_ref,
    dqkv_ref,
    pair_buf,
    w_buf,
    up_sums,
    columns_of,
    small_out,
    small_in,
    mine,
    core_in,
    held,
    x_out,
    x_in,
    y_out,
    y_in,
    z_out,
    z_in,
    last,
    take_sem,
    att_sem,
    stage_sem,
    out_sem,
    head_sem,
    end_sem,
    pair_sem,
    back_sem,
    w_sem,
    load_sem,
    core_sem,
    x_sem,
    y_sem,
    z_sem,
    zz_sem,
    yy_sem,
    cc_sem,
    keep_sem,
    small_sem,
):
    now = pl.program_id(0)
    place = lax.axis_index("dp")
    turn = lax.axis_index("mp")
    core, side, level = place % 2, (place // 2) % 2, place // 4
    levels = lax.axis_size("dp") // 4
    sibling = {"dp": place + 1 - 2 * core}
    across = {"mp": 1 - turn}
    beside = {"dp": place + 2 - 4 * side}
    floors = [{"dp": (level + step) % levels * 4 + place % 4} for step in range(1, levels)]
    half, piece = CHUNK // 2, CHUNK // 2 // levels
    length, width = total.shape
    pairs = width // (2 * HD)
    units = d_up_ref.shape[1] // 2
    ffs = up_sums.shape[2] // units
    outs = width // 2 // (2 * CHUNK)
    s_mid, s_att = ffs, ffs + 2
    small_at = s_att + 2 * pairs
    first_head = 2 * ffs + outs
    chunk_count = first_head + 3 * outs
    rest = jnp.maximum(now - s_att + 1, 0)
    slot_now = now - rest // 4
    last_slot = small_at - (2 * pairs + 1) // 4
    parts = 5
    step = length // parts
    blocks = [pl.ds(start, step) for start in range(0, length, step)]

    def gain(index):
        return gain_ref[index : index + 1, :]

    takes = [
        pltpu.make_async_copy(source, target, take_sem.at[index])
        for index, (source, target) in enumerate(
            (
                (third_in, third_ref),
                (d_down_in, d_down_ref),
                (cot_in, cot_ref),
                (mixed_in, mixed_ref),
                (residual_in, residual_ref),
                (w_out_in, out_buf),
                (first_in, cot_ref),
                (tokens_in, d_down_ref),
            )
        )
    ]

    def take_att(index):
        return pltpu.make_async_copy(att_in.at[blocks[index], :], att_ref.at[index % 2], att_sem.at[index % 2])

    def save_down(chunk):
        return pltpu.make_async_copy(stage_down, grads.at[2 * chunk], stage_sem.at[0])

    def save_up(chunk):
        return pltpu.make_async_copy(stage_up, grads.at[2 * chunk + 1], stage_sem.at[1])

    out_saves = [
        pltpu.make_async_copy(
            out_buf.at[pl.ds(group * width // 2 + (index * 2 + which) * CHUNK, CHUNK), :],
            grads.at[2 * ffs + index, pl.ds((2 * which + group) * CHUNK, CHUNK), :],
            out_sem.at[group, index, which],
        )
        for group in range(2)
        for index in range(outs)
        for which in range(2)
    ]

    def head_saves(turn_of):
        return [
            pltpu.make_async_copy(
                stage_down.at[pl.ds(kind * CHUNK, CHUNK), :],
                grads.at[first_head + turn_of // 4 * 3 + kind, aligned(turn_of % 4 * CHUNK, CHUNK), :],
                head_sem.at[kind],
            )
            for kind in range(3)
        ]

    def pair_at(turn_of):
        return turn_of % 2 * (pairs // 2) + turn_of // 4 * 2 + turn_of % 4 // 2

    def save_pair(turn_of):
        return pltpu.make_async_copy(pair_buf.at[turn_of % 2], kept_pairs.at[turn_of], pair_sem.at[turn_of % 2])


    def tail_turn(index):
        return (index + pairs - 2) % pairs

    def load_back(index):
        return pltpu.make_async_copy(kept_pairs.at[tail_turn(index)], pair_buf.at[index % 2], back_sem.at[index % 2])

    def load_weights(index):
        columns = aligned(pair_at(tail_turn(index)) * 2 * HD, 2 * HD, 128)
        return pltpu.make_async_copy(w_qkv_in.at[:, :, columns], w_buf.at[index % 2], w_sem.at[index % 2])

    save_input = pltpu.make_async_copy(residual_ref, input_out, end_sem)

    @pl.when(now == 0)
    def _():
        for copy in takes[:2]:
            copy.start()
        barrier = pltpu.get_barrier_semaphore()
        partners = [sibling, across, beside, *floors]
        for partner in partners:
            pl.semaphore_signal(barrier, inc=1, device_id=partner, device_id_type=MESH)
        pl.semaphore_wait(barrier, len(partners))
        takes[0].wait()
        takes[1].wait()
        for copy in takes[2:6]:
            copy.start()
        take_att(0).start()
        take_att(1).start()

    @pl.when((now >= 1) & (now <= ffs))
    def _():
        save_down(now - 1).wait()

    @pl.when((now >= s_att + 2) & (now <= small_at) & ((now - s_att) % 2 == 0))
    def _():
        for copy in head_saves((now - s_att) // 2 - 1):
            copy.wait()


    def loads(chunk, slot):
        kept = grads.at[chunk, aligned(core * 2 * CHUNK, 2 * CHUNK), :]
        sent = grads.at[chunk, aligned((1 - core) * 2 * CHUNK, 2 * CHUNK), :]
        return [
            pltpu.make_async_copy(kept, mine, load_sem),
            remote(sent, core_in.at[slot], core_sem, (slot,), sibling),
        ]

    def x_copy(slot):
        return remote(x_out.at[slot % 2], x_in.at[slot], x_sem, (slot,), across)

    def y_copy(slot):
        return remote(
            y_out.at[slot % 2, aligned((1 - side) * half, half)], y_in.at[slot], y_sem, (slot,), beside
        )

    def z_copies(slot):
        return [
            remote(
                z_out.at[slot % 2, aligned((level + move) % levels * piece, piece)],
                z_in.at[slot, move - 1],
                z_sem,
                (slot, move - 1),
                floors[move - 1],
            )
            for move in range(1, levels)
        ]

    def target(chunk, first, size):
        return whole.at[aligned((2 * chunk + core) * CHUNK + first, size), :]

    def keep_copies(chunk, slot):
        part = target(chunk, side * half + level * piece, piece)
        copies = [pltpu.make_async_copy(last.at[slot % 2], part, keep_sem.at[slot % 2])]
        for move in range(1, levels):
            copies.append(remote(last.at[slot % 2], part, zz_sem, (slot, move - 1), floors[move - 1]))
        return copies

    def yy_copy(chunk, slot):
        part = target(chunk, side * half, half)
        return remote(part, part, yy_sem, (slot,), beside)

    def cc_copy(chunk, slot):
        part = target(chunk, 0, CHUNK)
        return remote(part, part, cc_sem, (slot,), sibling)

    def stage_7(chunk, slot):
        cc_copy(chunk, slot).wait()

    def stage_6(chunk, slot):
        yy_copy(chunk, slot).wait()
        cc_copy(chunk, slot).start()

    def stage_5(chunk, slot):
        for copy in keep_copies(chunk, slot):
            copy.wait()
        yy_copy(chunk, slot).start()

    def stage_4(chunk, slot):
        for copy in z_copies(slot):
            copy.wait()
        summed = wide(z_out[slot % 2, aligned(level * piece, piece), :])
        for move in range(1, levels):
            summed = summed + wide(z_in[slot, move - 1])
        last[slot % 2] = low(summed)
        for copy in keep_copies(chunk, slot):
            copy.start()

    def stage_3(chunk, slot):
        y_copy(slot).wait()
        z_out[slot % 2] = low(wide(y_out[slot % 2, aligned(side * half, half), :]) + wide(y_in[slot]))
        for copy in z_copies(slot):
            copy.start()

    def stage_2(chunk, slot):
        x_copy(slot).wait()
        y_out[slot % 2] = low(held[slot % 2] + wide(x_in[slot]))
        y_copy(slot).start()

    def stage_1(chunk, slot):
        for copy in loads(chunk, slot):
            copy.wait()
        x_out[slot % 2] = low(wide(mine[CHUNK:]) + wide(core_in[slot, CHUNK:]))
        x_copy(slot).start()
        held[slot % 2] = wide(mine[:CHUNK]) + wide(core_in[slot, :CHUNK])

    def stage_0(chunk, slot):
        for copy in loads(chunk, slot):
            copy.start()

    stages = [stage_0, stage_1, stage_2, stage_3, stage_4, stage_5, stage_6, stage_7]

    def advance(moment):
        for stage in reversed(range(len(stages))):
            chunk = moment - 1 - STAGE_STEPS[stage]

            @pl.when((chunk >= 0) & (chunk < chunk_count))
            def _(stage=stage, chunk=chunk):
                stages[stage](chunk, chunk % 4)

    @pl.when((rest == 0) | (rest % 4 > 0))
    def _():
        advance(slot_now)


    @pl.when(now < ffs)
    def _():
        act = braid(act_own[...], act_other[...], 1)
        stage_down[...] = low(dot_tn(act, d_down_ref[...]))
        save_down(now).start()
        w_down = braid(down_own[...], down_other[...], 0)
        w_up = braid(up_own[...], up_other[...], 1)
        for part in (pl.ds(0, length // 2), pl.ds(length // 2, length // 2)):
            d_act = dot_nt(d_down_ref[part, :], w_down)
            slope = braid(slope_own[part, :], slope_other[part, :], 1)
            d_up = low(d_act * wide(slope))
            d_up_ref[part, :] = d_up
            update = dot_nt(d_up, w_up)
            total[part, :] = jnp.where(now == 0, update, update + total[part, :])
        sums = column_sum(wide(d_up_ref[...]))
        for group in range(2):
            for which in range(2):
                first = (2 * which + group) * CHUNK
                spot = aligned(now * units + which * CHUNK, CHUNK, 128)
                up_sums[group, 0:1, spot] = sums[:, first : first + CHUNK]

    @pl.when((now >= 1) & (now <= ffs))
    def _():
        save_up(now - 1).wait()

    @pl.when(now < ffs)
    def _():
        stage_up[...] = low(dot_tn(d_up_ref[...], third_ref[...]))
        save_up(now).start()


    @pl.when(now == s_mid)
    def _():
        for copy in takes[2:6]:
            copy.wait()
        sums = [0.0] * 5
        for index, part in enumerate(blocks):
            take_att(index).wait()
            normed_three, scale_three = standardize(residual_ref[part, :])
            normed_two, scale_two = standardize(att_ref[index % 2])
            d_third = total[part, :]
            d_residual = wide(cot_ref[part, :]) + norm_back(d_third, normed_three, scale_three, gain(2))
            residual_ref[part, :] = d_residual
            d_attended = norm_back(d_residual, normed_two, scale_two, gain(1))
            d_down_ref[part, :] = low(d_attended)
            if index + 2 < parts:
                take_att(index + 2).start()
            terms = [d_residual * normed_two, d_third * normed_three, d_residual, d_third, d_attended]
            sums = [old + column_sum(term) for old, term in zip(sums, terms)]
        small_out[...] = front_sums[...]
        for index, row in enumerate((1, 2, 5, 6, 8)):
            small_out[row : row + 1, :] = sums[index]
        takes[6].start()


    @pl.when(now == s_mid + 1)
    def _():
        for part in (pl.ds(0, length // 2), pl.ds(length // 2, length // 2)):
            third_ref[part, :] = low(dot_nt(d_down_ref[part, :], out_buf[...]))
        out_buf[...] = low(dot_tn(mixed_ref[...], d_down_ref[...]))
        for copy in out_saves:
            copy.start()

    @pl.when(now == s_att)
    def _():
        for copy in out_saves:
            copy.wait()
        takes[7].start()
        load_weights(0).start()
        load_weights(1).start()
        takes[6].wait()


    @pl.when((now >= s_att) & (now < small_at))
    def _():
        head = (now - s_att) % 2
        turn_of = (now - s_att) // 2
        pair = pair_at(turn_of)
        spot = aligned(pair * 2 * HD, 2 * HD, 128)
        lane = lax.broadcasted_iota(jnp.int32, (1, 2 * HD), 1)
        own = (lane // HD) == head
        scaled = wide(third_ref[:, spot]) * inv_ref[...]
        grad = jnp.where(own, scaled * relax_factor, 0.0).astype(jnp.bfloat16)
        inner = jnp.sum(wide(grad) * wide(mixed_ref[:, spot]), axis=1, keepdims=True)
        d_probs = dot_nt(grad, v_ref[...])
        ds_ref[...] = low(wide(weight_ref[0]) * (d_probs - inner))
        dq = low(dot_nn(ds_ref[...], k_ref[...]) * query_scale)
        dk = low(dot_tn(ds_ref[...], q_ref[...]))
        dv = low(dot_tn(weight_ref[0], low(scaled)))
        for index, value in enumerate((dq, dk, dv)):
            part = pl.ds(index * 2 * HD, 2 * HD)
            dqkv_ref[:, part] = jnp.where(own | (head == 0), value, dqkv_ref[:, part])

        @pl.when(head == 1)
        def _():
            d_qkv = dqkv_ref[...]
            stage_down[pl.ds(0, 6 * HD), :] = low(dot_tn(d_qkv, cot_ref[...]))
            for copy in head_saves(turn_of):
                copy.start()
            group, start = pair // (pairs // 2), pair % (pairs // 2) * 2 * HD
            sums = column_sum(wide(d_qkv))
            columns_of[group, 0:1, aligned(start, 2 * HD, 128)] = sums[:, : 2 * HD]
            columns_of[group, 0:1, aligned(width // 2 + start, 2 * HD, 128)] = sums[:, 4 * HD :]

            @pl.when(turn_of >= 2)
            def _():
                save_pair(turn_of - 2).wait()

            pair_buf[turn_of % 2] = d_qkv

            @pl.when(turn_of < pairs - 2)
            def _():
                save_pair(turn_of).start()


    def project_back(index):
        slot = index % 2
        load_weights(index).wait()

        @pl.when(index >= 2)
        def _():
            load_back(index).wait()

        weights = jnp.concatenate([w_buf[slot, 0], w_buf[slot, 1], w_buf[slot, 2]], axis=1)
        update = dot_nt(pair_buf[slot], weights)
        total[...] = jnp.where(index == 0, update, update + total[...])

        @pl.when(index + 2 < pairs)
        def _():
            load_weights(index + 2).start()
            load_back(index + 2).start()

    def first_norm_back():
        takes[7].wait()
        sums = [0.0, 0.0]
        for part in blocks:
            normed, scale = standardize(wide(d_down_ref[part, :]))
            errors = total[part, :]
            residual_ref[part, :] += norm_back(errors, normed, scale, gain(0))
            sums = [sums[0] + column_sum(errors * normed), sums[1] + column_sum(errors)]
        save_input.start()
        small_out[0:1, :] = sums[0]
        small_out[4:5, :] = sums[1]
        for group in range(2):
            small_out[10 + 3 * group : 11 + 3 * group, :] = columns_of[group, 0:1, :]
            for index in range(2):
                row = 11 + 3 * group + index
                small_out[row : row + 1, :] = up_sums[group, 0:1, index * width : (index + 1) * width]
        small_copies(0)[0].start()


    def small_copies(stage):
        if stage < 3:
            return [remote(small_out, small_in.at[stage], small_sem, (stage,), (sibling, across, beside)[stage])]
        return [
            remote(small_out, small_in.at[3 + level], small_sem, (2 + move,), floors[move - 1])
            for move in range(1, levels)
        ]

    def small_step_1():
        small_copies(0)[0].wait()
        small_out[...] += small_in[0]
        small_copies(1)[0].start()

    def small_step_2():
        small_copies(1)[0].wait()
        small_out[0:10, :] += small_in[1, 0:10, :]
        small_out[10:13, :] += small_in[1, 13:16, :]
        small_copies(2)[0].start()

    def small_step_3():
        small_copies(2)[0].wait()
        small_out[...] += small_in[2]
        small_in[3 + level] = small_out[...]
        for copy in small_copies(3):
            copy.start()

    def small_step_4():
        for copy in small_copies(3):
            copy.wait()
        summed = small_in[3]
        for index in range(1, levels):
            summed = summed + small_in[3 + index]
        sums_ref[...] = summed


    @pl.when(now == small_at)
    def _():
        first = last_slot + 1

        @pl.loop(first, chunk_count + 1 + STAGE_STEPS[-1])
        def _(moment):
            advance(moment)

            @pl.when(moment < first + pairs)
            def _():
                project_back(moment - first)

            steps = (first_norm_back, small_step_1, small_step_2, small_step_3, small_step_4)
            for index, small_step in enumerate(steps):
                pl.when(moment == first + pairs + index)(small_step)

        save_input.wait()


def rear(
    acts, slopes, w_up, w_down, queries, keys, values, inv, weights, w_qkv, gains, sums, third, d_down, cotangent, mixed,
    first, tokens, attended, residual, w_out, query_scale,
):
    length, width = queries.shape
    pairs = width // (2 * HD)
    ff = w_up.shape[1]
    units = 2 * CHUNK
    ffs = ff // 2 // units
    outs = width // 2 // units
    levels = lax.axis_size("dp") // 4
    half, piece = CHUNK // 2, CHUNK // 2 // levels
    s_att = ffs + 2
    small_at = s_att + 2 * pairs
    chunks = 2 * ffs + outs + 3 * outs
    kind, sem = jnp.bfloat16, pltpu.SemaphoreType.DMA

    def pair_of(i):
        turn_of = jnp.clip(i - s_att, 0, 2 * pairs - 1) // 2
        return turn_of % 2 * (pairs // 2) + turn_of // 4 * 2 + turn_of % 4 // 2

    def head_of(i):
        return pair_of(i) * 2 + jnp.clip(i - s_att, 0, 2 * pairs - 1) % 2

    def fixed(shape):
        return pl.BlockSpec(shape, lambda i: (0,) * len(shape), pipeline_mode=pl.Buffered(1))

    def unit_of(i):
        return jnp.minimum(i, ffs - 1)

    def lanes(rows):
        return [
            pl.BlockSpec((rows, units), lambda i: (0, unit_of(i))),
            pl.BlockSpec((rows, units), lambda i: (0, ffs + unit_of(i))),
        ]

    column = pl.BlockSpec((length, 2 * HD), lambda i: (0, pair_of(i)))
    hbm = pl.BlockSpec(memory_space=pl.ANY)
    return pl.pallas_call(
        partial(rear_kernel, query_scale),
        grid=(small_at + 1,),
        in_specs=[
            *lanes(length),
            *lanes(length),
            *lanes(width),
            pl.BlockSpec((units, width), lambda i: (unit_of(i), 0)),
            pl.BlockSpec((units, width), lambda i: (ffs + unit_of(i), 0)),
            *[column] * 4,
            pl.BlockSpec((1, length, length), lambda i: (head_of(i), 0, 0)),
            fixed((4, width)),
            fixed((16, width)),
            *[hbm] * 10,
        ],
        out_specs=[fixed((16, width)), hbm, hbm, hbm, hbm],
        out_shape=[
            jax.ShapeDtypeStruct((16, width), jnp.float32),
            jax.ShapeDtypeStruct((length, width), jnp.float32),
            jax.ShapeDtypeStruct((chunks * 2 * CHUNK, width), kind),
            jax.ShapeDtypeStruct((chunks, 4 * CHUNK, width), kind),
            jax.ShapeDtypeStruct((pairs - 2, length, 6 * HD), kind),
        ],
        scratch_shapes=[
            *[pltpu.VMEM((length, width), kind)] * 4,
            pltpu.VMEM((2, length // 5, width), jnp.float32),
            pltpu.VMEM((length, width), jnp.float32),
            pltpu.VMEM((length, width), jnp.float32),
            pltpu.VMEM((width, width), kind),
            pltpu.VMEM((length, 2 * units), kind),
            pltpu.VMEM((4 * CHUNK, width), kind),
            pltpu.VMEM((4 * CHUNK, width), kind),
            pltpu.VMEM((length, length), kind),
            pltpu.VMEM((length, 6 * HD), kind),
            pltpu.VMEM((2, length, 6 * HD), kind),
            pltpu.VMEM((2, 3, width, 2 * HD), kind),
            pltpu.VMEM((2, 8, ff // 2), jnp.float32),
            pltpu.VMEM((2, 8, width), jnp.float32),
            pltpu.VMEM((16, width), jnp.float32),
            pltpu.VMEM((3 + levels, 16, width), jnp.float32),
            pltpu.VMEM((2 * CHUNK, width), kind),
            pltpu.VMEM((4, 2 * CHUNK, width), kind),
            pltpu.VMEM((2, CHUNK, width), jnp.float32),
            pltpu.VMEM((2, CHUNK, width), kind),
            pltpu.VMEM((4, CHUNK, width), kind),
            pltpu.VMEM((2, CHUNK, width), kind),
            pltpu.VMEM((4, half, width), kind),
            pltpu.VMEM((2, half, width), kind),
            pltpu.VMEM((4, levels - 1, piece, width), kind),
            pltpu.VMEM((2, piece, width), kind),
            sem((8,)),
            sem((2,)),
            sem((2,)),
            sem((2, outs, 2)),
            sem((3,)),
            sem,
            sem((2,)),
            sem((2,)),
            sem((2,)),
            sem,
            sem((2, 4)),
            sem((2, 4)),
            sem((2, 4)),
            sem((2, 4, levels - 1)),
            sem((2, 4, levels - 1)),
            sem((2, 4)),
            sem((2, 4)),
            sem((2,)),
            sem((2, 2 + levels)),
        ],
        compiler_params=pltpu.CompilerParams(
            collective_id=0, has_side_effects=True, vmem_limit_bytes=63 * 2**20
        ),
    )(
        acts, acts, slopes, slopes, w_up, w_up, w_down, w_down, queries, keys, values, inv, weights, gains, sums,
        third, d_down, cotangent, mixed, first, tokens, attended, residual, w_out, w_qkv,
    )[:3]


def unpack_kernel(
    ffs,
    outs,
    whole_ref,
    grad_ref,
    result_ref,
    sums_ref,
    down_ref,
    up_ref,
    out_ref,
    qkv_ref,
    input_ref,
    output_ref,
    gains_ref,
    shifts_ref,
    outer_ref,
    qv_ref,
    bias_ref,
):
    now = pl.program_id(0)
    value = wide(whole_ref[...])

    @pl.when(now < 5)
    def _():
        input_ref[...] = grad_ref[...]
        output_ref[...] = result_ref[...]

    @pl.when(now == 0)
    def _():
        width = sums_ref.shape[1]
        gains_ref[...] = sums_ref[0:4, :]
        shifts_ref[...] = sums_ref[4:8, :]
        outer_ref[...] = sums_ref[8:10, :]
        for index in range(2):
            qv_ref[index : index + 1, :] = sums_ref[10:11, index * width // 2 : (index + 1) * width // 2]
            bias_ref[:, index * width : (index + 1) * width] = sums_ref[11 + index : 12 + index, :]

    @pl.when((now < 2 * ffs) & (now % 2 == 0))
    def _():
        down_ref[...] = value

    @pl.when((now < 2 * ffs) & (now % 2 == 1))
    def _():
        up_ref[...] = value.T

    @pl.when((now >= 2 * ffs) & (now < 2 * ffs + outs))
    def _():
        out_ref[...] = value

    @pl.when(now >= 2 * ffs + outs)
    def _():
        qkv_ref[0] = value.T


def unpack(whole, grad_input, result, sums, ff):
    length, width = result.shape
    units = 2 * CHUNK
    ffs = ff // 2 // units
    outs = width // 2 // units
    first_head = 2 * ffs + outs

    def head_turn(i):
        return jnp.maximum(i - first_head, 0)

    def fixed(*shape):
        return pl.BlockSpec(shape, lambda i: (0,) * len(shape), pipeline_mode=pl.Buffered(1))

    rows = pl.BlockSpec((length // 5, width), lambda i: (jnp.minimum(i, 4), 0))

    def wide_like(*shape):
        return jax.ShapeDtypeStruct(shape, jnp.float32)

    return pl.pallas_call(
        partial(unpack_kernel, ffs, outs),
        grid=(first_head + 3 * outs,),
        in_specs=[pl.BlockSpec((units, width), lambda i: (i, 0)), rows, rows, fixed(16, width)],
        out_specs=[
            pl.BlockSpec((units, width), lambda i: (jnp.minimum(i // 2, ffs - 1), 0)),
            pl.BlockSpec((width, units), lambda i: (0, jnp.minimum(i // 2, ffs - 1))),
            pl.BlockSpec((units, width), lambda i: (jnp.clip(i - 2 * ffs, 0, outs - 1), 0)),
            pl.BlockSpec((1, width, units), lambda i: (head_turn(i) % 3, 0, head_turn(i) // 3)),
            rows,
            rows,
            fixed(4, width),
            fixed(4, width),
            fixed(2, width),
            fixed(2, width // 2),
            fixed(1, ff // 2),
        ],
        out_shape=[
            wide_like(ff // 2, width),
            wide_like(width, ff // 2),
            wide_like(width // 2, width),
            wide_like(3, width, width // 2),
            wide_like(length, width),
            jax.ShapeDtypeStruct((length, width), jnp.bfloat16),
            wide_like(4, width),
            wide_like(4, width),
            wide_like(2, width),
            wide_like(2, width // 2),
            wide_like(1, ff // 2),
        ],
        compiler_params=pltpu.CompilerParams(vmem_limit_bytes=48 * 2**20),
    )(whole, grad_input, result, sums)


def sequence_shards(
    tokens,
    cond_flags,
    seg_lengths,
    norm_gains,
    norm_biases,
    w_qkv,
    qv_bias,
    w_out,
    out_biases,
    w_up,
    up_bias,
    w_down,
    cotangent,
):
    width = tokens.shape[1]
    query_scale = 1.0 / (relax_factor * math.sqrt(HD))
    (
        queries, keys, values, inv, kept, acts, slopes, small, first_in, mixed, attended, residual, third_in, result,
        d_down, all_qkv, all_out, all_up, all_down,
    ) = front(
        cond_flags, seg_lengths, tokens, cotangent, norm_gains, norm_biases, out_biases, qv_bias, up_bias,
        w_qkv, w_out, w_up, w_down, query_scale,
    )
    sums, grad_input, whole = rear(
        acts, slopes, all_up, all_down, queries, keys, values, inv, kept, all_qkv, norm_gains, small, third_in, d_down,
        cotangent, mixed, first_in, tokens, attended, residual, all_out, query_scale,
    )
    (
        grad_w_down, grad_w_up, grad_w_out, grad_w_qkv, grad_input, result, grad_gains, grad_shifts, grad_outer, grad_qv,
        grad_up_bias,
    ) = unpack(whole, grad_input, result, sums, all_up.shape[1])
    return (
        result,
        grad_input,
        grad_gains,
        grad_shifts,
        grad_w_qkv,
        grad_qv,
        grad_w_out,
        grad_outer,
        grad_w_up,
        grad_up_bias.reshape(-1),
        grad_w_down,
    )


def solution(mesh):
    in_specs = (
        P(("dp", "mp"), None),
        P("dp", None),
        P("dp", None),
        P(),
        P(),
        P(None, None, "mp"),
        P(None, "mp"),
        P("mp", None),
        P(),
        P(None, "mp"),
        P("mp"),
        P("mp", None),
        P(("dp", "mp"), None),
    )
    out_specs = (
        P(("dp", "mp"), None),
        P(("dp", "mp"), None),
        P(),
        P(),
        P(None, None, "mp"),
        P(None, "mp"),
        P("mp", None),
        P(),
        P(None, "mp"),
        P("mp"),
        P("mp", None),
    )
    per_device = mesh.shape["dp"] * mesh.shape["mp"]

    def step(*args):
        whole_sequences = args[1].shape[0] == per_device
        local = sequence_shards if whole_sequences and mesh.shape["mp"] == 2 and mesh.shape["dp"] == 16 else shards
        return jax.shard_map(
            local, mesh=mesh, in_specs=in_specs, out_specs=out_specs, check_vma=False
        )(*args)

    return step
```
